32 devices in a mesh: grp: 8 (over z, x), wide: 4 (over y, core).
Axes of the slice: x: 2, y: 2, z: 4, core: 2. Of those that a mesh axis runs over, the one named last changes fastest.
Arguments:
- hidden: bfloat16 [4096, 768], P(('grp', 'wide')), may hold values from -6 to 6
- char_codes: int32 [4096, 20], P(('grp', 'wide')), may hold values from 0 to 999
- word_length: int32 [4096], P(('grp', 'wide')), may hold values from 1 to 20, as said below
- sequence_length: int32 [32], P(('grp', 'wide')), may hold values from 64 to 128, as said below
- cotangent: bfloat16 [4096, 768], P(('grp', 'wide')), may hold values from -6 to 6
- attention_in: bfloat16 [768, 2304], P(None, ('grp', 'wide')), may hold values from -0.21875 to 0.21875
- attention_out: bfloat16 [768, 768], P(None, ('grp', 'wide')), may hold values from -1.5 to 1.5
- feed_in: bfloat16 [768, 3072], P(None, ('grp', 'wide')), may hold values from -0.21875 to 0.21875
- feed_bias: bfloat16 [3072], P(('grp', 'wide')), may hold values from -1 to 1
- feed_out: bfloat16 [3072, 768], P(None, ('grp', 'wide')), may hold values from -0.109375 to 0.109375
- char_table: bfloat16 [1000, 256], P(None, ('grp', 'wide')), may hold values from -6 to 6
- cell_input: bfloat16 [256, 2304], P(None, ('grp', 'wide')), may hold values from -0.375 to 0.375
- cell_recurrent: bfloat16 [384, 2304], P(None, ('grp', 'wide')), may hold values from -0.3125 to 0.3125
- cell_bias: bfloat16 [2, 2304], P(None, ('grp', 'wide')), may hold values from -1 to 1
- stream_weight: bfloat16 [2, 768, 768], P(None, None, ('grp', 'wide')), may hold values from -0.21875 to 0.21875
- merging_kernel: bfloat16 [3, 1536, 768], P(None, None, ('grp', 'wide')), may hold values from -0.09375 to 0.09375
- norm_gains: bfloat16 [3, 768], P(None, ('grp', 'wide')), may hold values from 0.5 to 1.5
- biases: bfloat16 [10, 768], P(None, ('grp', 'wide')), may hold values from -1 to 1
Outputs:
- output: bfloat16 [4096, 768], P(('grp', 'wide'))
- hidden_grad: bfloat16 [4096, 768], P(('grp', 'wide'))
- grad_attention_in: float32 [768, 2304], P(None, 'grp')
- grad_attention_out: float32 [768, 768], P(None, 'grp')
- grad_feed_in: float32 [768, 3072], P(None, 'grp')
- grad_feed_bias: float32 [3072], P('grp')
- grad_feed_out: float32 [3072, 768], P(None, 'grp')
- grad_char_table: float32 [1000, 256], P(None, 'grp')
- grad_cell_input: float32 [256, 2304], P(None, 'grp')
- grad_cell_recurrent: float32 [384, 2304], P(None, 'grp')
- grad_cell_bias: float32 [2, 2304], P(None, 'grp')
- grad_stream_weight: float32 [2, 768, 768], P(None, None, 'grp')
- grad_merging_kernel: float32 [3, 1536, 768], P(None, None, 'grp')
- grad_norm_gains: float32 [3, 768], P(None, 'grp')
- grad_biases: float32 [10, 768], P(None, 'grp')
The draws below stay inside these ranges and needn't reach their ends.
Inputs may be any that keep to these rules, and one draw needn't show every extreme that they name: `word_length`: every token has at least one character; one token of the draw fills all 20 slots and one has a single character. `sequence_length`: one sequence of the draw is full and one holds 64 valid tokens.
All inputs are finite; a program needn't handle non-finite values.
Results may differ from the reference program's by a relative error of at most 0.02.
Values may be sent and summed in bfloat16 or wider, within the bound.
A program may use at most 320 MiB of HBM per device.

```python
import math
import jax
import jax.numpy as jnp
import numpy as np
from jax import lax

D = 768
HEADS = 12
FF = 3072
HID = 384
CHAR_EMB = 256
VOCAB = 1000
CHARS = 20
SEQ = 128
SEQS = 32
TOKENS = 4096


def draw_word_length(key, part):
    key = jax.random.fold_in(key, 11)
    lengths = jax.random.randint(key, (TOKENS,), 1, CHARS + 1, dtype=jnp.int32)
    return lengths.at[0].set(CHARS).at[1].set(1)


def draw_sequence_length(key, part):
    key = jax.random.fold_in(key, 23)
    lengths = jax.random.randint(key, (SEQS,), SEQ // 2, SEQ + 1, dtype=jnp.int32)
    return lengths.at[0].set(SEQ).at[1].set(SEQ // 2)


def set_ends(entries, stream_key, least, largest):
    longest = entries.shape.index(max(entries.shape))
    spots = []
    for shift in (0, 1):
        where = [jax.random.randint(jax.random.fold_in(stream_key, axis), (), 0, length) for axis, length in enumerate(entries.shape)]
        where[longest] = (where[longest] + shift) % entries.shape[longest]
        spots.append(tuple(where))
    return entries.at[spots[0]].set(least).at[spots[1]].set(largest)


def with_spikes(drawn, rng, source, target, parts, factor):
    owner, partner = [(jnp.arange(drawn.shape[axis_at]) // (drawn.shape[axis_at] // parts)).reshape([-1 if axis == axis_at else 1 for axis in range(drawn.ndim)]) for axis_at in (source, target)]
    chosen = jax.random.permutation(rng, parts)[partner]
    strong = (owner == chosen) | (owner == (partner + parts // 2) % parts)
    return jnp.where(strong, factor * drawn, drawn)


def levels(key, dims, cuts, smallest, largest):
    gain = 1.0
    for dim, blocks in cuts:
        heights = jax.random.uniform(jax.random.fold_in(jax.random.fold_in(key, 6), dim), (blocks,), jnp.float32, smallest / len(cuts), largest / len(cuts))
        gain = gain * jnp.repeat(jnp.exp(heights), dims[dim] // blocks).reshape((-1,) + (1,) * (len(dims) - 1 - dim))
    return gain


def rank_bounds(amount, lean):
    loads = [(1 << 20) // math.isqrt(rank ** lean) + 1 for rank in range(1, amount + 1)]
    width = 1 + sum(loads) // (1 << 30)
    return np.cumsum(np.array([max(1, weight // width) for weight in loads]))


def skewed_ids(stream_key, dims, number_of, lean):
    grid = rank_bounds(number_of, lean)
    pick = jax.random.randint(jax.random.fold_in(stream_key, 1), dims, 0, int(grid[number_of - 1]))
    standing = jnp.searchsorted(jnp.asarray(grid, jnp.int32), pick, side="right")
    return jax.random.permutation(jax.random.fold_in(stream_key, 2), number_of)[standing].astype(jnp.int32)


def gaussian(key, shape, width, reach, cuts=(), kind=jnp.bfloat16):
    entries = jax.random.normal(key, shape, jnp.float32) * width
    if len(cuts) > 0:
        entries = levels(key, shape, cuts, -0.22, 0.18) * entries
    return jnp.clip(entries, min=-reach, max=reach).astype(kind)


def gaussian_with(key, extent, deviation, limit, cuts, heavy, held_as=jnp.bfloat16):
    drawn = deviation * jax.random.normal(key, extent, jnp.float32)
    if cuts:
        drawn = drawn * levels(key, extent, cuts, -0.22, 0.18)
    return jnp.clip(with_spikes(drawn, jax.random.fold_in(key, 3), *heavy), -limit, limit).astype(held_as)


def setup_inputs(seed: int = 0) -> dict:
    key_list = jax.random.split(jax.random.key(seed), 19)
    hidden = gaussian(key_list[0], (TOKENS, D), 1.0, 6.0, ((0, 32),))
    char_codes = set_ends(skewed_ids(key_list[1], (TOKENS, CHARS), VOCAB, 2), jax.random.fold_in(key_list[1], 3), 0, VOCAB - 1).astype(jnp.int32)
    word_length = draw_word_length(jax.random.fold_in(key_list[18], 71), 0)
    sequence_length = draw_sequence_length(jax.random.fold_in(key_list[18], 71), 0)
    cotangent = gaussian_with(key_list[4], (TOKENS, D), 1.0, 6.0, ((0, 32),), (0, 1, 32, 2.75))
    attention_in = gaussian(key_list[5], (D, 3 * D), D ** -0.5, 0.21875, ((1, 32),))
    attention_out = gaussian(key_list[6], (D, D), (D * 3 // SEQ) ** -0.5, 1.5, ((1, 32),))
    feed_in = gaussian(key_list[7], (D, FF), D ** -0.5, 0.21875, ((1, 32),))
    feed_bias = gaussian(key_list[8], (FF,), 0.2, 1.0, ((0, 32),))
    feed_out = gaussian(key_list[9], (FF, D), FF ** -0.5, 0.109375, ((1, 32),))
    char_table = gaussian(key_list[10], (VOCAB, CHAR_EMB), 1.0, 6.0, ((1, 32),))
    cell_input = gaussian(key_list[11], (CHAR_EMB, 6 * HID), CHAR_EMB ** -0.5, 0.375, ((1, 32),))
    cell_recurrent = gaussian(key_list[12], (HID, 6 * HID), HID ** -0.5, 0.3125, ((1, 32),))
    cell_bias = gaussian(key_list[13], (2, 6 * HID), 0.2, 1.0, ((1, 32),))
    stream_weight = gaussian(key_list[14], (2, D, D), D ** -0.5, 0.21875, ((2, 32),))
    merging_kernel = gaussian(key_list[15], (3, 2 * D, D), (6 * D) ** -0.5, 0.09375, ((2, 32),))
    norm_gains = jnp.clip(1.0 + 0.1 * jax.random.normal(key_list[16], (3, D), jnp.float32), 0.5, 1.5).astype(jnp.bfloat16)
    biases = gaussian(key_list[17], (10, D), 0.2, 1.0, ((1, 32),))
    return dict(hidden=hidden, char_codes=char_codes, word_length=word_length, sequence_length=sequence_length, cotangent=cotangent, attention_in=attention_in, attention_out=attention_out, feed_in=feed_in, feed_bias=feed_bias, feed_out=feed_out, char_table=char_table, cell_input=cell_input, cell_recurrent=cell_recurrent, cell_bias=cell_bias, stream_weight=stream_weight, merging_kernel=merging_kernel, norm_gains=norm_gains, biases=biases)


@jax.custom_vjp
def low(v):
    return lax.optimization_barrier(v.astype(jnp.bfloat16)).astype(jnp.float32)

@jax.custom_vjp
def low_back(v):
    return v

def low_keep(v):
    return (low(v), None)

def low_pass(kept, grad):
    return (grad,)

def back_keep(v):
    return (v, None)

def back_low(kept, grad):
    return (low(grad),)
low.defvjp(low_keep, low_pass)
low_back.defvjp(back_keep, back_low)
norm_eps = 1e-05
masked_score = -1e+30

def matmul(left_side, right_side):
    return jnp.dot(left_side, right_side, precision=lax.Precision.HIGHEST)

def layer_norm(inputs, gain_row, shift_row):
    centred = inputs - lax.optimization_barrier(jnp.mean(inputs, axis=-1, keepdims=True))
    spread = lax.optimization_barrier(jnp.mean(centred * centred, axis=-1, keepdims=True))
    return centred * lax.rsqrt(spread + norm_eps) * gain_row + shift_row

def gate_cell(previous, drive_in, recurrent, marker):
    hidden_units = previous.shape[-1]
    reset_gate = jax.nn.sigmoid(drive_in[:, :hidden_units] + recurrent[:, :hidden_units])
    update = jax.nn.sigmoid(drive_in[:, hidden_units:2 * hidden_units] + recurrent[:, hidden_units:2 * hidden_units])
    candidate = jnp.tanh(drive_in[:, 2 * hidden_units:] + reset_gate * recurrent[:, 2 * hidden_units:])
    fresh_state = (1.0 - update) * candidate + update * previous
    return marker * fresh_state + (1.0 - marker) * previous

def forward(params, hidden, char_codes, word_length, sequence_length):
    attention_in, attention_out, feed_in, feed_bias, feed_out, char_table, cell_input, cell_recurrent, cell_bias, stream_weight, merging_kernel, norm_gains, biases = params
    group_seqs, length, model_width = hidden.shape
    head_size = model_width // HEADS
    tokens_here = group_seqs * length
    token_rows = hidden.reshape(tokens_here, model_width)
    joint_bias = jnp.concatenate([biases[0], jnp.zeros_like(biases[0]), biases[1]])
    projected = low(low_back(matmul(token_rows, attention_in)) + joint_bias)
    projected = projected.reshape(group_seqs, length, 3, HEADS, head_size)
    queries = projected[:, :, 0]
    key_rows = projected[:, :, 1]
    value_rows = projected[:, :, 2]
    key_valid = jnp.arange(length)[None, :] < sequence_length[:, None]
    key_mask = jnp.where(key_valid, jnp.float32(0.0), jnp.float32(masked_score))[:, None, None, :]
    products = jnp.einsum('gqhd,gkhd->ghqk', queries, key_rows, precision=lax.Precision.HIGHEST)
    scores = low_back(products * head_size ** (-0.5) + key_mask)
    top_score = lax.optimization_barrier(jnp.max(scores, axis=-1, keepdims=True))
    exponent = jnp.exp(scores - top_score)
    probabilities = exponent / lax.optimization_barrier(jnp.sum(exponent, axis=-1, keepdims=True))
    context = low(low_back(jnp.einsum('ghqk,gkhd->gqhd', low(probabilities), value_rows, precision=lax.Precision.HIGHEST)))
    attended = low_back(matmul(context.reshape(tokens_here, model_width), attention_out)) + biases[2]
    first = layer_norm(token_rows + attended, norm_gains[0], biases[3])
    inner_sum = low_back(matmul(low(first), feed_in)) + feed_bias
    activation = low(jax.nn.gelu(inner_sum, approximate=False))
    second = layer_norm(first + low_back(matmul(activation, feed_out)) + biases[4], norm_gains[1], biases[5])
    hidden_units = cell_recurrent.shape[0]
    gate_width = 3 * hidden_units
    char_count = char_codes.shape[-1]
    embedded = char_table[char_codes.reshape(tokens_here * char_count)]
    drives = (low_back(matmul(embedded, cell_input)) + cell_bias[0]).reshape(tokens_here, char_count, 2 * gate_width)
    char_marks = (jnp.arange(char_count)[None, :] < word_length.reshape(tokens_here)[:, None]).astype(jnp.float32)
    drives_time = jnp.transpose(drives, (1, 0, 2))
    marks_time = jnp.transpose(char_marks)[:, :, None]
    sequence_in = (drives_time[:, :, :gate_width], marks_time, drives_time[::-1, :, gate_width:], marks_time[::-1])

    def advance(carried, pieces):
        onward, behind, total_onward, total_behind = carried
        drive_onward, mark_onward, drive_behind, mark_behind = pieces
        recur_onward = low_back(matmul(low(onward), cell_recurrent[:, :gate_width])) + cell_bias[1, :gate_width]
        recur_behind = low_back(matmul(low(behind), cell_recurrent[:, gate_width:])) + cell_bias[1, gate_width:]
        onward = gate_cell(onward, drive_onward, recur_onward, mark_onward)
        behind = gate_cell(behind, drive_behind, recur_behind, mark_behind)
        return ((onward, behind, total_onward + mark_onward * onward, total_behind + mark_behind * behind), None)
    zero_state = jnp.zeros((tokens_here, hidden_units), jnp.float32)
    final_carry, _ = lax.scan(jax.checkpoint(advance), (zero_state, zero_state, zero_state, zero_state), sequence_in)
    counts = word_length.reshape(tokens_here).astype(jnp.float32)[:, None]
    pooled = jnp.concatenate([final_carry[2], final_carry[3]], axis=-1) / counts
    token_side = low_back(matmul(low(second), stream_weight[0])) + biases[6]
    char_side = low_back(matmul(low(pooled), stream_weight[1])) + biases[7]
    joined = low(jnp.concatenate([token_side, char_side], axis=-1)).reshape(group_seqs, length, 2 * model_width)
    padded = jnp.pad(joined, ((0, 0), (1, 1), (0, 0)))
    windows = jnp.concatenate([padded[:, :-2], padded[:, 1:-1], padded[:, 2:]], axis=-1)
    merged_out = low_back(matmul(windows.reshape(tokens_here, 6 * model_width), merging_kernel.reshape(6 * model_width, model_width))) + biases[8]
    result = layer_norm(second + merged_out, norm_gains[2], biases[9])
    return result.reshape(group_seqs, length, model_width)

def group_size(seq_total):
    chosen = 1
    while chosen * 2 <= max(1, 1024 // SEQ) and seq_total % (chosen * 2) == 0:
        chosen = chosen * 2
    return chosen

def reference(hidden, char_codes, word_length, sequence_length, cotangent, attention_in, attention_out, feed_in, feed_bias, feed_out, char_table, cell_input, cell_recurrent, cell_bias, stream_weight, merging_kernel, norm_gains, biases):
    params = tuple((weight.astype(jnp.float32) for weight in (attention_in, attention_out, feed_in, feed_bias, feed_out, char_table, cell_input, cell_recurrent, cell_bias, stream_weight, merging_kernel, norm_gains, biases)))
    group_seqs = group_size(SEQS)
    rounds = SEQS // group_seqs

    def by_group(array):
        return array.reshape((rounds, group_seqs, SEQ) + array.shape[1:])
    inputs = (by_group(hidden.astype(jnp.float32)), by_group(char_codes), by_group(word_length), sequence_length.reshape(rounds, group_seqs), by_group(cotangent.astype(jnp.float32)))

    def one_group(totals, pieces):
        block_hidden, block_codes, block_length, block_seqs, block_cotangent = pieces

        def local_forward(weights, states):
            return forward(weights, states, block_codes, block_length, block_seqs)
        result, pull_back = jax.vjp(local_forward, params, block_hidden)
        param_grads, grad_states = pull_back(block_cotangent)
        totals = jax.tree.map(lambda left_side, right_side: left_side + right_side, totals, param_grads)
        return (totals, (result, grad_states))
    totals, (results, grad_states) = lax.scan(one_group, jax.tree.map(jnp.zeros_like, params), inputs)
    output = results.reshape(TOKENS, D).astype(jnp.bfloat16)
    hidden_grad = grad_states.reshape(TOKENS, D).astype(jnp.bfloat16)
    return (output, hidden_grad, totals[0], totals[1], totals[2], totals[3], totals[4], totals[5], totals[6], totals[7], totals[8], totals[9], totals[10], totals[11], totals[12])
```

```python
from functools import partial

import jax
import jax.numpy as jnp
from jax import lax
from jax.experimental import pallas as pl
from jax.experimental.pallas import tpu as pltpu
from jax.sharding import PartitionSpec as P

HEADS = 12
HID = 384
EMB = 256
CHARS = 20
TOKENS = 128
norm_eps = 1e-05
masked_score = -1e30
MESH = pl.DeviceIdType.MESH
EVERY = slice(None)
LOW = jnp.bfloat16
WIDE = jnp.float32

BLOCKS = {
    "CELL": (144, 768),
    "TABLE": (16, 1024),
    "ATT": (144, 768),
    "OUT": (48, 1024),
    "IN": (192, 768),
    "FEED": (48, 3072),
    "STREAM": (48, 1536),
    "MERGE": (48, 4608),
}
KINDS = tuple(BLOCKS)
PIECES = (
    ("CELL", 0, 384, 384),
    ("TABLE", 0, 512, 512),
    ("ATT", 0, 384, 384),
    ("OUT", 0, 512, 512),
    ("IN", 0, 128, 128),
    ("IN", 256, 512, 256),
    ("FEED", 0, 768, 768),
    ("FEED", 1536, 2304, 768),
    ("STREAM", 0, 768, 768),
    ("MERGE", 0, 768, 768),
    ("MERGE", 1536, 2304, 768),
    ("MERGE", 3072, 3840, 768),
)

X_WIDTH = 768
RECORD = X_WIDTH + 4 * HID
GATE_R, GATE_Z, GATE_N, GATE_Q = (X_WIDTH + i * HID for i in range(4))


def dot_plain(left_side, right_side):
    return jnp.dot(left_side, right_side, preferred_element_type=WIDE)


def dot_first(left_side, right_side):
    return lax.dot_general(left_side, right_side, (((0,), (0,)), ((), ())), preferred_element_type=WIDE)


def dot_second(left_side, right_side):
    return lax.dot_general(left_side, right_side, (((1,), (1,)), ((), ())), preferred_element_type=WIDE)


def sigmoid(inputs):
    return 0.5 * jnp.tanh(0.5 * inputs) + 0.5


class Spot:
    def __init__(self, per_place):
        self.grp, self.wide = lax.axis_index("grp"), lax.axis_index("wide")
        self.z, self.x = self.grp // 2, self.grp % 2
        self.y, self.core = self.wide // per_place, self.wide % 2
        self.to_x = (self.grp + 1 - 2 * self.x, self.wide)
        self.to_y = (self.grp, self.wide + per_place - 2 * per_place * self.y)
        self.sibling = (self.grp, self.wide + 1 - 2 * self.core)

    def hop(self, k):
        return (2 * ((self.z + k) % 4) + self.x, self.wide)

    def greet(self):
        barrier = pltpu.get_barrier_semaphore()
        for other in [self.to_x, self.to_y, self.sibling] + [self.hop(k) for k in (1, 2, 3)]:
            pl.semaphore_signal(barrier, 1, device_id=other, device_id_type=MESH)
        pl.semaphore_wait(barrier, 6)

    def near(self, core):
        if core == 0:
            return self.x, self.y, self.to_x, self.to_y
        return self.y, self.x, self.to_y, self.to_x


def remote(source, target, sent, received, device):
    return pltpu.make_async_remote_copy(
        src_ref=source, dst_ref=target, send_sem=sent, recv_sem=received, device_id=device, device_id_type=MESH
    )


class Gather:
    def __init__(self, spot, own, whole, sems):
        self.spot, self.own, self.whole = spot, own, whole
        self.sent, self.got = sems

    def region(self, core, p, z, f, l):
        kind, first, second, width = PIECES[p]
        lanes = pl.ds((first, second)[core], width)
        return self.whole[kind].at[z, f, l, :, lanes] if core == 0 else self.whole[kind].at[z, l, f, :, lanes]

    def move(self, part, p, j, device, source=None):
        return remote(part if source is None else source, part, self.sent.at[p, j], self.got.at[p, j], device)

    def along(self, core, p, k):
        f, l, _, _ = self.spot.near(core)
        kind, first, second, width = PIECES[p]
        source = self.own[kind].at[:, pl.ds((first, second)[core], width)]
        return self.move(self.region(core, p, self.spot.z, f, l), p, k - 1, self.spot.hop(k), source)

    def along_in(self, core, p, k):
        f, l, _, _ = self.spot.near(core)
        return self.move(self.region(core, p, (self.spot.z + 4 - k) % 4, f, l), p, k - 1, self.spot.hop(k))

    def line(self, core, p, mine):
        f, l, to_f, _ = self.spot.near(core)
        return self.move(self.region(core, p, EVERY, f if mine else 1 - f, l), p, 3, to_f)

    def plane(self, core, p, mine):
        f, l, _, to_l = self.spot.near(core)
        return self.move(self.region(core, p, EVERY, EVERY, l if mine else 1 - l), p, 4, to_l)

    def aside(self, core, p, j):
        f, l, _, _ = self.spot.near(core)
        if j < 3:
            part = self.region(core, p, (self.spot.z + 3 - j) % 4, f, l)
        elif j == 3:
            part = self.region(core, p, EVERY, 1 - f, l)
        else:
            part = self.region(core, p, EVERY, EVERY, 1 - l)
        return self.move(part, p, 5 + j, self.spot.sibling)

    def start(self, core, p):
        for k in (1, 3, 2):
            self.along(core, p, k).start()

    def second(self, core, p):
        for k in (1, 3, 2):
            self.along_in(core, p, k).wait_recv()
        self.line(core, p, True).start()
        for k in (1, 3, 2):
            self.aside(core, p, k - 1).start()

    def third(self, core, p):
        self.line(core, p, False).wait_recv()
        self.plane(core, p, True).start()
        self.aside(core, p, 3).start()

    def fourth(self, core, p):
        self.plane(core, p, False).wait_recv()
        self.aside(core, p, 4).start()

    def fifth(self, core, p):
        for j in range(5):
            self.aside(1 - core, p, j).wait_recv()

    def drain(self, core, p):
        for k in (1, 2, 3):
            self.along(core, p, k).wait_send()
        self.line(core, p, True).wait_send()
        self.plane(core, p, True).wait_send()
        for j in range(5):
            self.aside(core, p, j).wait_send()

    def program(self):
        steps = []
        count = len(PIECES)
        ahead = 3
        for p in range(ahead):
            steps.append(("start", p))
        for s in range(count + 3):
            if s + ahead < count:
                steps.append(("start", s + ahead))
            for lag, stage in enumerate(("second", "third", "fourth", "fifth")):
                if 0 <= s - lag < count:
                    steps.append((stage, s - lag))
        return steps

    def run(self, steps):
        for core in (0, 1):

            @pl.when(self.spot.core == core)
            def _():
                for stage, p in steps:
                    getattr(self, stage)(core, p)


def gru_forward_step(t, cell, record, state, total, shifts, lengths):
    for way in (0, 1):
        base = way * RECORD
        place = t if way == 0 else CHARS - 1 - t
        live = lengths[...] > place
        lanes = pl.ds(way * HID, HID)
        h = state[:, lanes]
        record[t, :, pl.ds(base + EMB, HID)] = h.astype(LOW)
        x = record[t, :, pl.ds(base, X_WIDTH)]
        weights = cell[pl.ds(2 * way, 2)].reshape(3 * HID, X_WIDTH)
        both = dot_second(x, weights[: 2 * HID])
        drive_n = dot_second(x[:, :EMB], weights[2 * HID :, :EMB]) + shifts[way, 0:1]
        recur_n = dot_second(x[:, EMB : EMB + HID], weights[2 * HID :, EMB : EMB + HID]) + shifts[way, 1:2]
        r = sigmoid(both[:, :HID])
        u = sigmoid(both[:, HID:])
        n = jnp.tanh(drive_n + r * recur_n)
        fresh = jnp.where(live, n + u * (h - n), h)
        state[:, lanes] = fresh
        total[:, lanes] += jnp.where(live, fresh, 0.0)
        record[t, :, pl.ds(base + GATE_R, HID)] = r.astype(LOW)
        record[t, :, pl.ds(base + GATE_Z, HID)] = u.astype(LOW)
        record[t, :, pl.ds(base + GATE_N, HID)] = n.astype(LOW)
        record[t, :, pl.ds(base + GATE_Q, HID)] = recur_n.astype(LOW)


def one_hot(codes, t, vocabulary):
    return (lax.broadcasted_iota(jnp.int32, (TOKENS, vocabulary), 1) == codes[t]).astype(LOW)


def forward_kernel(per_place, *refs):
    count = len(KINDS)
    own = dict(zip(KINDS, refs[:count]))
    codes, lengths = refs[count : count + 2]
    outs = refs[count + 2 :]
    whole = dict(zip(KINDS, outs[:count]))
    record_out, pooled = outs[count : count + 2]
    record, state, shifts, sent, got, own_sem, record_sem = outs[count + 2 :]
    spot = Spot(per_place)
    own_copies = [
        pltpu.make_async_copy(own[kind], whole[kind].at[spot.z, spot.x, spot.y], own_sem.at[i])
        for i, kind in enumerate(KINDS)
    ]
    for copy in own_copies:
        copy.start()
    spot.greet()
    for copy in own_copies:
        copy.wait()
    gather = Gather(spot, own, whole, (sent, got))
    steps = gather.program()
    lead = steps.index(("fifth", 1)) + 1
    gather.run(steps[:lead])

    table = whole["TABLE"][...].reshape(EMB, 1024)
    cell = whole["CELL"]
    ones = (lax.broadcasted_iota(jnp.int32, (TOKENS, 128), 1) < 2).astype(LOW)

    def embed(c, carry):
        rows = dot_second(one_hot(codes, c, 1024), table).astype(LOW)
        record[c, :, pl.ds(0, EMB)] = rows
        record[CHARS - 1 - c, :, pl.ds(RECORD, EMB)] = rows
        record[c, :, pl.ds(EMB + HID, 128)] = ones
        record[c, :, pl.ds(RECORD + EMB + HID, 128)] = ones
        return carry

    lax.fori_loop(0, CHARS, embed, 0)
    pick = (
        lax.broadcasted_iota(jnp.int32, (8, 128), 0) == lax.broadcasted_iota(jnp.int32, (8, 128), 1)
    ).astype(LOW)
    for way in (0, 1):
        late = cell[pl.ds(2 * way, 2)].reshape(3 * HID, X_WIDTH)[2 * HID :, EMB + HID :]
        shifts[way] = dot_second(pick, late)
    state[...] = jnp.zeros_like(state)
    pooled[...] = jnp.zeros_like(pooled)
    rest = steps[lead:]
    share = -(-len(rest) // CHARS)

    def advance(t, carry):
        gru_forward_step(t, cell, record, state, pooled, shifts, lengths)
        pltpu.make_async_copy(record.at[t], record_out.at[t], record_sem.at[t]).start()
        for k in range(CHARS):

            @pl.when(t == k)
            def _():
                gather.run(rest[k * share : (k + 1) * share])

        return carry

    lax.fori_loop(0, CHARS, advance, 0)
    pooled[...] = pooled[...] / lengths[...].astype(WIDE)

    def landed(t, carry):
        pltpu.make_async_copy(record.at[t], record_out.at[t], record_sem.at[t]).wait()
        return carry

    lax.fori_loop(0, CHARS, landed, 0)
    gather.run([("drain", p) for p in range(len(PIECES))])


def gather_and_read(own, codes, lengths, per_place):
    count = len(KINDS)
    in_vmem = pl.BlockSpec(memory_space=pltpu.VMEM)
    anywhere = pl.BlockSpec(memory_space=pl.ANY)
    results = pl.pallas_call(
        partial(forward_kernel, per_place),
        out_shape=[jax.ShapeDtypeStruct((4, 2, 2) + BLOCKS[kind], LOW) for kind in KINDS]
        + [
            jax.ShapeDtypeStruct((CHARS, TOKENS, 2 * RECORD), LOW),
            jax.ShapeDtypeStruct((TOKENS, 2 * HID), WIDE),
        ],
        in_specs=[in_vmem] * (count + 2),
        out_specs=[in_vmem if kind in ("CELL", "TABLE") else anywhere for kind in KINDS] + [anywhere, in_vmem],
        scratch_shapes=[
            pltpu.VMEM((CHARS, TOKENS, 2 * RECORD), LOW),
            pltpu.VMEM((TOKENS, 2 * HID), WIDE),
            pltpu.VMEM((2, 8, HID), WIDE),
            pltpu.SemaphoreType.DMA((len(PIECES), 10)),
            pltpu.SemaphoreType.DMA((len(PIECES), 10)),
            pltpu.SemaphoreType.DMA((count,)),
            pltpu.SemaphoreType.DMA((CHARS,)),
        ],
        compiler_params=pltpu.CompilerParams(collective_id=0, has_side_effects=True, vmem_limit_bytes=56 << 20),
    )(*[own[kind] for kind in KINDS], codes, lengths)
    return dict(zip(KINDS, results[:count])), results[count], results[count + 1]


def pack(shards, per_place):
    (attention_in, attention_out, feed_in, feed_bias, feed_out, char_table, cell_input, cell_recurrent, cell_bias,
     stream_weight, merging_kernel, norm_gains, biases) = shards

    def lanes(parts, width):
        together = jnp.concatenate(parts, axis=1)
        return jnp.pad(together, ((0, 0), (0, width - together.shape[1])))

    def flat(stacked):
        return [jnp.transpose(part) for part in stacked]

    rows = attention_out.shape[1]
    thin = lanes(
        [
            lanes([attention_out.T, biases.T, norm_gains.T, feed_bias.reshape(rows, 4)], 1024),
            feed_out.T,
            *flat(stream_weight),
            *flat(merging_kernel),
        ],
        10240,
    )
    middle = lanes([cell_input.T, cell_recurrent.T, cell_bias.T], 768)
    middle = jnp.concatenate([middle, attention_in.T], axis=1)
    parts = [thin, middle, feed_in.T, lanes([char_table.T], 1024)]
    if per_place == 2:
        size = lax.axis_size("wide")
        swap = [(i, i + 1 - 2 * (i % 2)) for i in range(size)]
        first = lax.axis_index("wide") % 2 == 0
        whole = []
        for part in parts:
            other = lax.ppermute(part, "wide", swap)
            whole.append(jnp.concatenate([jnp.where(first, part, other), jnp.where(first, other, part)], axis=0))
    else:
        size = lax.axis_size("wide")
        groups = [list(range(i, i + per_place)) for i in range(0, size, per_place)]
        whole = [lax.all_gather(part, "wide", axis=0, tiled=True, axis_index_groups=groups) for part in parts]
    thin, middle, feed, table = whole
    return {
        "CELL": middle[:, :768],
        "TABLE": table,
        "ATT": middle[:, 768:],
        "OUT": thin[:, :1024],
        "IN": feed,
        "FEED": thin[:, 1024:4096],
        "STREAM": thin[:, 4096:5632],
        "MERGE": thin[:, 5632:],
    }


def gru_backward_step(t, cell, record, state_grad, pool_grad, lengths):
    for way in (0, 1):
        base = way * RECORD
        place = t if way == 0 else CHARS - 1 - t
        live = lengths[...] > place
        lanes = pl.ds(way * HID, HID)

        def saved(at):
            return record[t, :, pl.ds(base + at, HID)].astype(WIDE)

        r, u, n, recur_n, h = saved(GATE_R), saved(GATE_Z), saved(GATE_N), saved(GATE_Q), saved(EMB)
        grad = state_grad[:, lanes]
        fresh = jnp.where(live, grad + pool_grad[:, lanes], 0.0)
        kept = jnp.where(live, 0.0, grad)
        grad_n = fresh * (1.0 - u) * (1.0 - n * n)
        grad_z = fresh * (h - n) * u * (1.0 - u)
        grad_r = grad_n * recur_n * r * (1.0 - r)
        low_r, low_z, low_n, low_q = (v.astype(LOW) for v in (grad_r, grad_z, grad_n, grad_n * r))
        record[t, :, pl.ds(base + GATE_R, HID)] = low_r
        record[t, :, pl.ds(base + GATE_Z, HID)] = low_z
        record[t, :, pl.ds(base + GATE_N, HID)] = low_n
        record[t, :, pl.ds(base + GATE_Q, HID)] = low_q
        weights = cell[pl.ds(2 * way, 2)].reshape(3 * HID, X_WIDTH)[:, EMB : EMB + HID]
        gates = jnp.concatenate([low_r, low_z, low_q], axis=1)
        state_grad[:, lanes] = kept + fresh * u + dot_plain(gates, weights)


def cell_gradient(way, record, result):
    base = way * RECORD
    rows = CHARS * TOKENS

    def every(at, width):
        return record[:, :, pl.ds(base + at, width)].reshape(rows, width)

    x = every(0, X_WIDTH)
    for gate, at in ((0, GATE_R), (1, GATE_Z)):
        result[pl.ds((3 * way + gate) * HID, HID)] = dot_first(every(at, HID), x).astype(LOW)
    drive, recur = dot_first(every(GATE_N, HID), x), dot_first(every(GATE_Q, HID), x)
    lane = lax.broadcasted_iota(jnp.int32, (HID, X_WIDTH), 1)
    result[pl.ds((3 * way + 2) * HID, HID)] = jnp.where(
        (lane < EMB) | (lane == EMB + HID), drive, recur
    ).astype(LOW)


def table_gradient(c, cell, record, codes, result):
    drive = jnp.zeros((TOKENS, EMB), WIDE)
    for way, t in ((0, c), (1, CHARS - 1 - c)):
        gates = record[t, :, pl.ds(way * RECORD + GATE_R, 3 * HID)]
        drive += dot_plain(gates, cell[pl.ds(2 * way, 2)].reshape(3 * HID, X_WIDTH)[:, :EMB])
    result[...] += dot_first(drive.astype(LOW), one_hot(codes, c, 1024))


def layer_norm(inputs, gain_row, shift_row):
    centred = inputs - jnp.mean(inputs, axis=-1, keepdims=True)
    spread = jnp.mean(centred * centred, axis=-1, keepdims=True)
    return centred * lax.rsqrt(spread + norm_eps) * gain_row + shift_row


def gelu_exact(inputs):
    return jax.nn.gelu(inputs, approximate=False)


def dense(whole, hidden, sequence_length, cotangent, pooled):
    w = {kind: part.reshape(-1, part.shape[-1]) for kind, part in whole.items()}
    small = w["OUT"][:, 768:785]
    small_rows = jnp.transpose(small[:, :13]).astype(WIDE)
    biases, gains = small_rows[:10], small_rows[10:]
    feed_bias = small[:, 13:].reshape(-1).astype(WIDE)
    length, width = hidden.shape
    head = width // HEADS
    scale = head ** (-0.5)
    joint_bias = jnp.concatenate([biases[0], jnp.zeros_like(biases[0]), biases[1]])
    projected = (dot_second(hidden, w["ATT"]) + joint_bias).astype(LOW)
    projected = projected.reshape(length, 3, HEADS, head)
    queries, keys, values = projected[:, 0], projected[:, 1], projected[:, 2]
    mask = jnp.where(jnp.arange(length) < sequence_length[0], 0.0, masked_score).astype(WIDE)
    scores = jnp.einsum("qhd,khd->hqk", queries, keys, preferred_element_type=WIDE) * scale + mask
    weight = jnp.exp(scores - jnp.max(scores, axis=-1, keepdims=True))
    soft = weight / jnp.sum(weight, axis=-1, keepdims=True)
    soft_low = soft.astype(LOW)
    context = jnp.einsum("hqk,khd->qhd", soft_low, values, preferred_element_type=WIDE)
    context = context.astype(LOW).reshape(length, width)
    one_sum = hidden.astype(WIDE) + dot_second(context, w["OUT"][:, :768]) + biases[2]
    first = layer_norm(one_sum, gains[0], biases[3])
    first_low = first.astype(LOW)
    inner = dot_second(first_low, w["IN"]) + feed_bias
    active = gelu_exact(inner).astype(LOW)
    two_sum = first + dot_second(active, w["FEED"]) + biases[4]
    second = layer_norm(two_sum, gains[1], biases[5])
    second_low = second.astype(LOW)
    pooled_low = pooled.astype(LOW)
    token_side = dot_second(second_low, w["STREAM"][:, :768]) + biases[6]
    char_side = dot_second(pooled_low, w["STREAM"][:, 768:]) + biases[7]
    joined = jnp.concatenate([token_side, char_side], axis=-1).astype(LOW)
    padded = jnp.pad(joined, ((1, 1), (0, 0)))
    windows = jnp.concatenate([padded[:-2], padded[1:-1], padded[2:]], axis=-1)
    third_sum = second + dot_second(windows, w["MERGE"]) + biases[8]
    output = layer_norm(third_sum, gains[2], biases[9]).astype(LOW)

    _, pull_three = jax.vjp(layer_norm, third_sum, gains[2], biases[9])
    merged_grad, gain_three, shift_three = pull_three(cotangent.astype(WIDE))
    merged_low = merged_grad.astype(LOW)
    grads = {"MERGE": dot_first(merged_low, windows)}
    window_grad = dot_plain(merged_low, w["MERGE"]).reshape(length, 3, 2 * width)
    joined_grad = (
        window_grad[:, 1]
        + jnp.pad(window_grad[1:, 0], ((0, 1), (0, 0)))
        + jnp.pad(window_grad[:-1, 2], ((1, 0), (0, 0)))
    )
    token_grad, char_grad = joined_grad[:, :width], joined_grad[:, width:]
    token_low, char_low = token_grad.astype(LOW), char_grad.astype(LOW)
    grads["STREAM"] = jnp.concatenate([dot_first(token_low, second_low), dot_first(char_low, pooled_low)], axis=1)
    pooled_grad = dot_plain(char_low, w["STREAM"][:, 768:])
    second_grad = merged_grad + dot_plain(token_low, w["STREAM"][:, :768])
    _, pull_two = jax.vjp(layer_norm, two_sum, gains[1], biases[5])
    two_grad, gain_two, shift_two = pull_two(second_grad)
    two_low = two_grad.astype(LOW)
    grads["FEED"] = dot_first(two_low, active)
    _, pull_gelu = jax.vjp(gelu_exact, inner)
    (inner_grad,) = pull_gelu(dot_plain(two_low, w["FEED"]))
    inner_low = inner_grad.astype(LOW)
    grads["IN"] = dot_first(inner_low, first_low)
    first_grad = two_grad + dot_plain(inner_low, w["IN"])
    _, pull_one = jax.vjp(layer_norm, one_sum, gains[0], biases[3])
    one_grad, gain_one, shift_one = pull_one(first_grad)
    one_low = one_grad.astype(LOW)
    grad_out = dot_first(one_low, context)
    context_grad = dot_plain(one_low, w["OUT"][:, :768]).astype(LOW).reshape(length, HEADS, head)
    soft_grad = jnp.einsum("qhd,khd->hqk", context_grad, values, preferred_element_type=WIDE)
    value_grad = jnp.einsum("hqk,qhd->khd", soft_low, context_grad, preferred_element_type=WIDE)
    score_grad = soft * (soft_grad - jnp.sum(soft * soft_grad, axis=-1, keepdims=True))
    score_low = score_grad.astype(LOW)
    query_grad = jnp.einsum("hqk,khd->qhd", score_low, keys, preferred_element_type=WIDE) * scale
    key_grad = jnp.einsum("hqk,qhd->khd", score_low, queries, preferred_element_type=WIDE) * scale
    projected_low = jnp.stack([query_grad, key_grad, value_grad], axis=1).reshape(length, 3 * width).astype(LOW)
    grads["ATT"] = dot_first(projected_low, hidden)
    hidden_grad = (one_grad + dot_plain(projected_low, w["ATT"])).astype(LOW)
    small_grads = jnp.stack(
        [
            jnp.sum(query_grad, axis=0).reshape(width),
            jnp.sum(value_grad, axis=0).reshape(width),
            jnp.sum(one_grad, axis=0),
            shift_one,
            jnp.sum(two_grad, axis=0),
            shift_two,
            jnp.sum(token_grad, axis=0),
            jnp.sum(char_grad, axis=0),
            jnp.sum(merged_grad, axis=0),
            shift_three,
            gain_one,
            gain_two,
            gain_three,
        ]
    )
    feed_bias_grad = jnp.sum(inner_grad, axis=0).reshape(width, 4)
    grads["OUT"] = jnp.pad(
        jnp.concatenate([grad_out, jnp.transpose(small_grads), feed_bias_grad], axis=1), ((0, 0), (0, 256 - 17))
    )
    grads = {
        kind: part.astype(LOW).reshape((4, 2, 2) + BLOCKS[kind]) for kind, part in grads.items()
    }
    return output, hidden_grad, pooled_grad, grads


def backward_kernel(record_in, cell, table, codes, lengths, pool_grad, cell_grad, table_grad, record, state_grad, total, record_sem):
    copy = pltpu.make_async_copy(record_in, record, record_sem)
    copy.start()
    copy.wait()
    state_grad[...] = jnp.zeros_like(state_grad)

    def retreat(i, carry):
        gru_backward_step(CHARS - 1 - i, cell, record, state_grad, pool_grad, lengths)
        return carry

    lax.fori_loop(0, CHARS, retreat, 0)
    for way in (0, 1):
        cell_gradient(way, record, cell_grad)
    total[...] = jnp.zeros_like(total)

    def look_up(c, carry):
        table_gradient(c, cell, record, codes, total)
        return carry

    lax.fori_loop(0, CHARS, look_up, 0)
    table_grad[...] = total[...].astype(LOW)


def gru_backward(record, cell, table, codes, lengths, pool_grad):
    in_vmem = pl.BlockSpec(memory_space=pltpu.VMEM)
    return pl.pallas_call(
        backward_kernel,
        out_shape=[jax.ShapeDtypeStruct((6 * HID, X_WIDTH), LOW), jax.ShapeDtypeStruct((EMB, 1024), LOW)],
        in_specs=[pl.BlockSpec(memory_space=pl.ANY)] + [in_vmem] * 5,
        out_specs=[in_vmem] * 2,
        scratch_shapes=[
            pltpu.VMEM((CHARS, TOKENS, 2 * RECORD), LOW),
            pltpu.VMEM((TOKENS, 2 * HID), WIDE),
            pltpu.VMEM((EMB, 1024), WIDE),
            pltpu.SemaphoreType.DMA,
        ],
        compiler_params=pltpu.CompilerParams(vmem_limit_bytes=56 << 20),
    )(record, cell, table, codes, lengths, pool_grad)


def unpack(final):
    part = {kind: value.reshape(-1, value.shape[-1]).astype(WIDE) for kind, value in final.items()}
    cell, table, out, stream, merge = (part[kind] for kind in ("CELL", "TABLE", "OUT", "STREAM", "MERGE"))
    small = out[:, 768:785]
    return (
        part["ATT"].T,
        out[:, :768].T,
        part["IN"].T,
        small[:, 13:].reshape(-1),
        part["FEED"].T,
        table[:, :1000].T,
        cell[:, :EMB].T,
        cell[:, EMB : EMB + HID].T,
        cell[:, EMB + HID : EMB + HID + 2].T,
        jnp.stack([stream[:, :768].T, stream[:, 768:].T]),
        jnp.stack([merge[:, k * 1536 : (k + 1) * 1536].T for k in range(3)]),
        small[:, 10:13].T,
        small[:, :10].T,
    )


def shards(hidden, char_codes, word_length, sequence_length, cotangent, *parameters):
    wide = lax.axis_size("wide")
    per_place = wide // 2
    own = pack(parameters, per_place)
    codes = jnp.transpose(char_codes)[:, :, None]
    lengths = word_length[:, None]
    whole, record, pooled = gather_and_read(own, codes, lengths, per_place)
    output, hidden_grad, pooled_grad, grads = dense(whole, hidden, sequence_length, cotangent, pooled)
    pool_grad = pooled_grad / lengths.astype(WIDE)
    cell_grad, table_grad = gru_backward(record, whole["CELL"], whole["TABLE"], codes, lengths, pool_grad)
    grads["CELL"] = cell_grad.reshape((4, 2, 2) + BLOCKS["CELL"])
    grads["TABLE"] = table_grad.reshape((4, 2, 2) + BLOCKS["TABLE"])
    final = {}
    for kind, part in grads.items():
        part = part.reshape((8, 2) + part.shape[3:])
        part = lax.psum_scatter(part, "grp", scatter_dimension=0, tiled=True)
        final[kind] = lax.psum(part, "wide")
    return (output, hidden_grad, *unpack(final))


def solution(mesh):
    rows = P(("grp", "wide"), None)
    flat = P(("grp", "wide"))
    last = P(None, ("grp", "wide"))
    deep = P(None, None, ("grp", "wide"))
    in_specs = (rows, rows, flat, flat, rows, last, last, last, flat, last, last, last, last, last, deep, deep, last, last)
    out_specs = (rows, rows) + (P(None, "grp"),) * 3 + (P("grp"),) + (P(None, "grp"),) * 5 + (P(None, None, "grp"),) * 2 + (P(None, "grp"),) * 2
    return jax.shard_map(shards, mesh=mesh, in_specs=in_specs, out_specs=out_specs, check_vma=False)
```

```python
from functools import partial

import jax
import jax.numpy as jnp
from jax import lax
from jax.experimental import pallas as pl
from jax.experimental.pallas import tpu as pltpu
from jax.sharding import PartitionSpec as P

HEADS = 12
HID = 384
EMB = 256
CHARS = 20
TOKENS = 128
norm_eps = 1e-05
masked_score = -1e30
MESH = pl.DeviceIdType.MESH
EVERY = slice(None)
LOW = jnp.bfloat16
WIDE = jnp.float32

BLOCKS = {
    "CELL": (144, 768),
    "TABLE": (16, 1024),
    "ATT": (144, 768),
    "OUT": (48, 1024),
    "IN": (192, 768),
    "FEED": (48, 3072),
    "STREAM": (48, 1536),
    "MERGE": (48, 4608),
}
KINDS = tuple(BLOCKS)
PIECES = (
    ("CELL", 0, 384, 384),
    ("TABLE", 0, 512, 512),
    ("ATT", 0, 384, 384),
    ("OUT", 0, 512, 512),
    ("IN", 0, 128, 128),
    ("IN", 256, 512, 256),
    ("FEED", 0, 768, 768),
    ("FEED", 1536, 2304, 768),
    ("STREAM", 0, 768, 768),
    ("MERGE", 0, 768, 768),
    ("MERGE", 1536, 2304, 768),
    ("MERGE", 3072, 3840, 768),
)

X_WIDTH = 768
RECORD = X_WIDTH + 4 * HID
GATE_R, GATE_Z, GATE_N, GATE_Q = (X_WIDTH + i * HID for i in range(4))


def dot_plain(left_side, right_side):
    return jnp.dot(left_side, right_side, preferred_element_type=WIDE)


def dot_first(left_side, right_side):
    return lax.dot_general(left_side, right_side, (((0,), (0,)), ((), ())), preferred_element_type=WIDE)


def dot_second(left_side, right_side):
    return lax.dot_general(left_side, right_side, (((1,), (1,)), ((), ())), preferred_element_type=WIDE)


def sigmoid(inputs):
    return 0.5 * jnp.tanh(0.5 * inputs) + 0.5


class Spot:
    def __init__(self, per_place):
        self.grp, self.wide = lax.axis_index("grp"), lax.axis_index("wide")
        self.z, self.x = self.grp // 2, self.grp % 2
        self.y, self.core = self.wide // per_place, self.wide % 2
        self.to_x = (self.grp + 1 - 2 * self.x, self.wide)
        self.to_y = (self.grp, self.wide + per_place - 2 * per_place * self.y)
        self.sibling = (self.grp, self.wide + 1 - 2 * self.core)

    def hop(self, k):
        return (2 * ((self.z + k) % 4) + self.x, self.wide)

    def greet(self):
        barrier = pltpu.get_barrier_semaphore()
        for other in [self.to_x, self.to_y, self.sibling] + [self.hop(k) for k in (1, 2, 3)]:
            pl.semaphore_signal(barrier, 1, device_id=other, device_id_type=MESH)
        pl.semaphore_wait(barrier, 6)

    def near(self, core):
        if core == 0:
            return self.x, self.y, self.to_x, self.to_y
        return self.y, self.x, self.to_y, self.to_x


def remote(source, target, sent, received, device):
    return pltpu.make_async_remote_copy(
        src_ref=source, dst_ref=target, send_sem=sent, recv_sem=received, device_id=device, device_id_type=MESH
    )


class Gather:
    def __init__(self, spot, own, whole, sems):
        self.spot, self.own, self.whole = spot, own, whole
        self.sent, self.got = sems

    def region(self, core, p, z, f, l):
        kind, first, second, width = PIECES[p]
        lanes = pl.ds((first, second)[core], width)
        return self.whole[kind].at[z, f, l, :, lanes] if core == 0 else self.whole[kind].at[z, l, f, :, lanes]

    def move(self, part, p, j, device, source=None):
        return remote(part if source is None else source, part, self.sent.at[p, j], self.got.at[p, j], device)

    def along(self, core, p, k):
        f, l, _, _ = self.spot.near(core)
        kind, first, second, width = PIECES[p]
        source = self.own[kind].at[:, pl.ds((first, second)[core], width)]
        return self.move(self.region(core, p, self.spot.z, f, l), p, k - 1, self.spot.hop(k), source)

    def along_in(self, core, p, k):
        f, l, _, _ = self.spot.near(core)
        return self.move(self.region(core, p, (self.spot.z + 4 - k) % 4, f, l), p, k - 1, self.spot.hop(k))

    def line(self, core, p, mine):
        f, l, to_f, _ = self.spot.near(core)
        return self.move(self.region(core, p, EVERY, f if mine else 1 - f, l), p, 3, to_f)

    def plane(self, core, p, mine):
        f, l, _, to_l = self.spot.near(core)
        return self.move(self.region(core, p, EVERY, EVERY, l if mine else 1 - l), p, 4, to_l)

    def aside(self, core, p, j):
        f, l, _, _ = self.spot.near(core)
        if j < 3:
            part = self.region(core, p, (self.spot.z + 3 - j) % 4, f, l)
        elif j == 3:
            part = self.region(core, p, EVERY, 1 - f, l)
        else:
            part = self.region(core, p, EVERY, EVERY, 1 - l)
        return self.move(part, p, 5 + j, self.spot.sibling)

    def start(self, core, p):
        for k in (1, 3, 2):
            self.along(core, p, k).start()

    def second(self, core, p):
        for k in (1, 3, 2):
            self.along_in(core, p, k).wait_recv()
        self.line(core, p, True).start()
        for k in (1, 3, 2):
            self.aside(core, p, k - 1).start()

    def third(self, core, p):
        self.line(core, p, False).wait_recv()
        self.plane(core, p, True).start()
        self.aside(core, p, 3).start()

    def fourth(self, core, p):
        self.plane(core, p, False).wait_recv()
        self.aside(core, p, 4).start()

    def fifth(self, core, p):
        for j in range(5):
            self.aside(1 - core, p, j).wait_recv()

    def drain(self, core, p):
        for k in (1, 2, 3):
            self.along(core, p, k).wait_send()
        self.line(core, p, True).wait_send()
        self.plane(core, p, True).wait_send()
        for j in range(5):
            self.aside(core, p, j).wait_send()

    def program(self):
        steps = []
        count = len(PIECES)
        ahead = 3
        for p in range(ahead):
            steps.append(("start", p))
        for s in range(count + 3):
            if s + ahead < count:
                steps.append(("start", s + ahead))
            for lag, stage in enumerate(("second", "third", "fourth", "fifth")):
                if 0 <= s - lag < count:
                    steps.append((stage, s - lag))
        return steps

    def run(self, steps):
        for core in (0, 1):

            @pl.when(self.spot.core == core)
            def _():
                for stage, p in steps:
                    getattr(self, stage)(core, p)


def gru_forward_step(t, cell, record, state, total, shifts, lengths):
    for way in (0, 1):
        base = way * RECORD
        place = t if way == 0 else CHARS - 1 - t
        live = lengths[...] > place
        lanes = pl.ds(way * HID, HID)
        h = state[:, lanes]
        record[t, :, pl.ds(base + EMB, HID)] = h.astype(LOW)
        x = record[t, :, pl.ds(base, X_WIDTH)]
        weights = cell[pl.ds(2 * way, 2)].reshape(3 * HID, X_WIDTH)
        both = dot_second(x, weights[: 2 * HID])
        drive_n = dot_second(x[:, :EMB], weights[2 * HID :, :EMB]) + shifts[way, 0:1]
        recur_n = dot_second(x[:, EMB : EMB + HID], weights[2 * HID :, EMB : EMB + HID]) + shifts[way, 1:2]
        r = sigmoid(both[:, :HID])
        u = sigmoid(both[:, HID:])
        n = jnp.tanh(drive_n + r * recur_n)
        fresh = jnp.where(live, n + u * (h - n), h)
        state[:, lanes] = fresh
        total[:, lanes] += jnp.where(live, fresh, 0.0)
        record[t, :, pl.ds(base + GATE_R, HID)] = r.astype(LOW)
        record[t, :, pl.ds(base + GATE_Z, HID)] = u.astype(LOW)
        record[t, :, pl.ds(base + GATE_N, HID)] = n.astype(LOW)
        record[t, :, pl.ds(base + GATE_Q, HID)] = recur_n.astype(LOW)


def one_hot(codes, t, vocabulary):
    return (lax.broadcasted_iota(jnp.int32, (TOKENS, vocabulary), 1) == codes[t]).astype(LOW)


def forward_kernel(per_place, *refs):
    count = len(KINDS)
    own = dict(zip(KINDS, refs[:count]))
    codes, lengths = refs[count : count + 2]
    outs = refs[count + 2 :]
    whole = dict(zip(KINDS, outs[:count]))
    record_out, pooled = outs[count : count + 2]
    record, state, shifts, sent, got, own_sem, record_sem = outs[count + 2 :]
    spot = Spot(per_place)
    own_copies = [
        pltpu.make_async_copy(own[kind], whole[kind].at[spot.z, spot.x, spot.y], own_sem.at[i])
        for i, kind in enumerate(KINDS)
    ]
    for copy in own_copies:
        copy.start()
    spot.greet()
    for copy in own_copies:
        copy.wait()
    gather = Gather(spot, own, whole, (sent, got))
    steps = gather.program()
    lead = steps.index(("fifth", 1)) + 1
    gather.run(steps[:lead])

    table = whole["TABLE"][...].reshape(EMB, 1024)
    cell = whole["CELL"]
    ones = (lax.broadcasted_iota(jnp.int32, (TOKENS, 128), 1) < 2).astype(LOW)

    def embed(c, carry):
        rows = dot_second(one_hot(codes, c, 1024), table).astype(LOW)
        record[c, :, pl.ds(0, EMB)] = rows
        record[CHARS - 1 - c, :, pl.ds(RECORD, EMB)] = rows
        record[c, :, pl.ds(EMB + HID, 128)] = ones
        record[c, :, pl.ds(RECORD + EMB + HID, 128)] = ones
        return carry

    lax.fori_loop(0, CHARS, embed, 0)
    pick = (
        lax.broadcasted_iota(jnp.int32, (8, 128), 0) == lax.broadcasted_iota(jnp.int32, (8, 128), 1)
    ).astype(LOW)
    for way in (0, 1):
        late = cell[pl.ds(2 * way, 2)].reshape(3 * HID, X_WIDTH)[2 * HID :, EMB + HID :]
        shifts[way] = dot_second(pick, late)
    state[...] = jnp.zeros_like(state)
    pooled[...] = jnp.zeros_like(pooled)
    rest = steps[lead:]
    share = -(-len(rest) // CHARS)

    def advance(t, carry):
        gru_forward_step(t, cell, record, state, pooled, shifts, lengths)
        pltpu.make_async_copy(record.at[t], record_out.at[t], record_sem.at[t]).start()
        for k in range(CHARS):

            @pl.when(t == k)
            def _():
                gather.run(rest[k * share : (k + 1) * share])

        return carry

    lax.fori_loop(0, CHARS, advance, 0)
    pooled[...] = pooled[...] / lengths[...].astype(WIDE)

    def landed(t, carry):
        pltpu.make_async_copy(record.at[t], record_out.at[t], record_sem.at[t]).wait()
        return carry

    lax.fori_loop(0, CHARS, landed, 0)
    gather.run([("drain", p) for p in range(len(PIECES))])


def gather_and_read(own, codes, lengths, per_place):
    count = len(KINDS)
    in_vmem = pl.BlockSpec(memory_space=pltpu.VMEM)
    anywhere = pl.BlockSpec(memory_space=pl.ANY)
    results = pl.pallas_call(
        partial(forward_kernel, per_place),
        out_shape=[jax.ShapeDtypeStruct((4, 2, 2) + BLOCKS[kind], LOW) for kind in KINDS]
        + [
            jax.ShapeDtypeStruct((CHARS, TOKENS, 2 * RECORD), LOW),
            jax.ShapeDtypeStruct((TOKENS, 2 * HID), WIDE),
        ],
        in_specs=[in_vmem] * (count + 2),
        out_specs=[in_vmem if kind in ("CELL", "TABLE") else anywhere for kind in KINDS] + [anywhere, in_vmem],
        scratch_shapes=[
            pltpu.VMEM((CHARS, TOKENS, 2 * RECORD), LOW),
            pltpu.VMEM((TOKENS, 2 * HID), WIDE),
            pltpu.VMEM((2, 8, HID), WIDE),
            pltpu.SemaphoreType.DMA((len(PIECES), 10)),
            pltpu.SemaphoreType.DMA((len(PIECES), 10)),
            pltpu.SemaphoreType.DMA((count,)),
            pltpu.SemaphoreType.DMA((CHARS,)),
        ],
        compiler_params=pltpu.CompilerParams(collective_id=0, has_side_effects=True, vmem_limit_bytes=56 << 20),
    )(*[own[kind] for kind in KINDS], codes, lengths)
    return dict(zip(KINDS, results[:count])), results[count], results[count + 1]


def pack(shards, per_place):
    (attention_in, attention_out, feed_in, feed_bias, feed_out, char_table, cell_input, cell_recurrent, cell_bias,
     stream_weight, merging_kernel, norm_gains, biases) = shards

    def lanes(parts, width):
        together = jnp.concatenate(parts, axis=1)
        return jnp.pad(together, ((0, 0), (0, width - together.shape[1])))

    def flat(stacked):
        return [jnp.transpose(part) for part in stacked]

    rows = attention_out.shape[1]
    thin = lanes(
        [
            lanes([attention_out.T, biases.T, norm_gains.T, feed_bias.reshape(rows, 4)], 1024),
            feed_out.T,
            *flat(stream_weight),
            *flat(merging_kernel),
        ],
        10240,
    )
    middle = lanes([cell_input.T, cell_recurrent.T, cell_bias.T], 768)
    middle = jnp.concatenate([middle, attention_in.T], axis=1)
    parts = [thin, middle, feed_in.T, lanes([char_table.T], 1024)]
    if per_place == 2:
        size = lax.axis_size("wide")
        swap = [(i, i + 1 - 2 * (i % 2)) for i in range(size)]
        first = lax.axis_index("wide") % 2 == 0
        whole = []
        for part in parts:
            other = lax.ppermute(part, "wide", swap)
            whole.append(jnp.concatenate([jnp.where(first, part, other), jnp.where(first, other, part)], axis=0))
    else:
        size = lax.axis_size("wide")
        groups = [list(range(i, i + per_place)) for i in range(0, size, per_place)]
        whole = [lax.all_gather(part, "wide", axis=0, tiled=True, axis_index_groups=groups) for part in parts]
    thin, middle, feed, table = whole
    return {
        "CELL": middle[:, :768],
        "TABLE": table,
        "ATT": middle[:, 768:],
        "OUT": thin[:, :1024],
        "IN": feed,
        "FEED": thin[:, 1024:4096],
        "STREAM": thin[:, 4096:5632],
        "MERGE": thin[:, 5632:],
    }


def gru_backward_step(t, cell, record, state_grad, pool_grad, lengths):
    for way in (0, 1):
        base = way * RECORD
        place = t if way == 0 else CHARS - 1 - t
        live = lengths[...] > place
        lanes = pl.ds(way * HID, HID)

        def saved(at):
            return record[t, :, pl.ds(base + at, HID)].astype(WIDE)

        r, u, n, recur_n, h = saved(GATE_R), saved(GATE_Z), saved(GATE_N), saved(GATE_Q), saved(EMB)
        grad = state_grad[:, lanes]
        fresh = jnp.where(live, grad + pool_grad[:, lanes], 0.0)
        kept = jnp.where(live, 0.0, grad)
        grad_n = fresh * (1.0 - u) * (1.0 - n * n)
        grad_z = fresh * (h - n) * u * (1.0 - u)
        grad_r = grad_n * recur_n * r * (1.0 - r)
        low_r, low_z, low_n, low_q = (v.astype(LOW) for v in (grad_r, grad_z, grad_n, grad_n * r))
        record[t, :, pl.ds(base + GATE_R, HID)] = low_r
        record[t, :, pl.ds(base + GATE_Z, HID)] = low_z
        record[t, :, pl.ds(base + GATE_N, HID)] = low_n
        record[t, :, pl.ds(base + GATE_Q, HID)] = low_q
        weights = cell[pl.ds(2 * way, 2)].reshape(3 * HID, X_WIDTH)[:, EMB : EMB + HID]
        gates = jnp.concatenate([low_r, low_z, low_q], axis=1)
        state_grad[:, lanes] = kept + fresh * u + dot_plain(gates, weights)


def cell_gradient(way, record, result):
    base = way * RECORD
    rows = CHARS * TOKENS

    def every(at, width):
        return record[:, :, pl.ds(base + at, width)].reshape(rows, width)

    x = every(0, X_WIDTH)
    parts = [dot_first(every(at, HID), x).astype(LOW) for at in (GATE_R, GATE_Z)]
    drive, recur = dot_first(every(GATE_N, HID), x), dot_first(every(GATE_Q, HID), x)
    lane = lax.broadcasted_iota(jnp.int32, (HID, X_WIDTH), 1)
    parts.append(jnp.where((lane < EMB) | (lane == EMB + HID), drive, recur).astype(LOW))
    result[...] = jnp.concatenate(parts, axis=0).reshape(result.shape)


def table_gradient(c, cell, record, codes, result):
    drive = jnp.zeros((TOKENS, EMB), WIDE)
    for way, t in ((0, c), (1, CHARS - 1 - c)):
        gates = record[t, :, pl.ds(way * RECORD + GATE_R, 3 * HID)]
        drive += dot_plain(gates, cell[pl.ds(2 * way, 2)].reshape(3 * HID, X_WIDTH)[:, :EMB])
    which = (lax.broadcasted_iota(jnp.int32, (1024, TOKENS), 0) == codes[pl.ds(c, 1)]).astype(LOW)
    result[...] += dot_plain(which, drive.astype(LOW))


ROWS, LANES = 48, 768
PARTS = (
    [("MERGE", 0, 48, 0, 768, 768, 0, 0, True)],
    [("MERGE", 0, 48, 1536, 2304, 768, 0, 0, True)],
    [("MERGE", 0, 48, 3072, 3840, 768, 0, 0, True)],
    [("STREAM", 0, 48, 0, 768, 768, 0, 0, True)],
    [("FEED", 0, 48, 0, 768, 768, 0, 0, True)],
    [("FEED", 0, 48, 1536, 2304, 768, 0, 0, True)],
    [("IN", 0, 48, 0, 384, 384, 0, 0, True), ("IN", 48, 48, 0, 384, 384, 0, 384, True)],
    [("IN", 96, 48, 0, 384, 384, 0, 0, True), ("IN", 144, 48, 0, 384, 384, 0, 384, True)],
    [("ATT", 0, 48, 0, 384, 384, 0, 0, True), ("ATT", 48, 48, 0, 384, 384, 0, 384, True)],
    [("ATT", 96, 48, 0, 384, 384, 0, 0, True), ("OUT", 0, 48, 0, 512, 384, 0, 384, True)],
    [("CELL", 0, 48, 0, 384, 384, 0, 0, True), ("CELL", 48, 48, 0, 384, 384, 0, 384, True)],
    [
        ("CELL", 96, 48, 0, 384, 384, 0, 0, True),
        ("OUT", 0, 48, 384, 896, 128, 0, 384, True),
        ("TABLE", 0, 16, 0, 512, 256, 0, 512, True),
        ("TABLE", 0, 16, 256, 768, 256, 16, 512, True),
        ("TABLE", 0, 16, 256, 768, 256, 32, 512, False),
    ],
)
SLOTS = 7
SUBS = 5
DENSE_PARTS = 10
AT_FIRST, AT_HOP, AT_NEXT, AT_LAST, AT_RESULT = SUBS, SUBS, SUBS + 4, SUBS + 5, SUBS + 6
MOVES = 2 * SUBS + 6


class Reduce:
    def __init__(self, spot, grads, landing, buffers, result, sems):
        self.spot, self.grads, self.landing, self.result = spot, grads, landing, result
        self.sums, self.other, self.one_in, self.next_in, self.final = buffers
        self.sent, self.got, self.load_sem, self.keep_sem, self.free = sems

    def move(self, source, target, p, j, device):
        return remote(source, target, self.sent.at[p, j], self.got.at[p, j], device)

    def outside(self, ref, sub, core):
        _, row, rows, first, second, width, _, _, _ = sub
        return ref.at[..., pl.ds(row, rows), pl.ds((first, second)[core], width)]

    def inside(self, ref, sub):
        _, _, rows, _, _, width, row, lane, _ = sub
        return ref.at[..., pl.ds(row, rows), pl.ds(lane, width)]

    def given(self, core, p):
        return [
            self.move(
                self.outside(self.grads[sub[0]], sub, 1 - core), self.inside(self.landing.at[p], sub), p, i, self.spot.sibling
            )
            for i, sub in enumerate(PARTS[p])
        ]

    def loads(self, core, p):
        own = [
            pltpu.make_async_copy(
                self.outside(self.grads[sub[0]], sub, core), self.inside(self.sums.at[p % SLOTS], sub), self.load_sem.at[p % 2, i]
            )
            for i, sub in enumerate(PARTS[p])
        ]
        return own + [pltpu.make_async_copy(self.landing.at[p], self.other.at[p % 2], self.load_sem.at[p % 2, SUBS])]

    def first(self, core, p):
        s, slot = self.spot, p % SLOTS
        if core == 0:
            return self.move(self.sums.at[slot, :, 1 - s.x], self.one_in.at[slot], p, AT_FIRST, s.to_x)
        return self.move(self.sums.at[slot, :, :, 1 - s.y], self.one_in.at[slot], p, AT_FIRST, s.to_y)

    def hop(self, core, p, k):
        s, slot = self.spot, p % SLOTS
        z = (s.z + k) % 4
        if core == 0:
            return self.move(self.sums.at[slot, z, s.x], self.next_in.at[slot, pl.ds(2 * k - 2, 2)], p, AT_HOP + k, s.hop(k))
        return self.move(self.sums.at[slot, z, s.x, s.y], self.next_in.at[slot, 3 + k], p, AT_HOP + k, s.hop(k))

    def next(self, core, p):
        s, slot = self.spot, p % SLOTS
        if core == 0:
            return self.move(self.sums.at[slot, s.z, s.x], self.next_in.at[slot, pl.ds(6, 2)], p, AT_NEXT, s.to_y)
        return self.move(self.sums.at[slot, :, 1 - s.x, s.y], self.next_in.at[slot, pl.ds(0, 4)], p, AT_NEXT, s.to_x)

    def last(self, p, mine):
        s, slot = self.spot, p % SLOTS
        part = self.final.at[slot, s.y if mine else 1 - s.y]
        return self.move(part, part, p, AT_LAST, s.to_y)

    def results(self, core, p):
        return [
            self.move(self.inside(self.final.at[p % SLOTS], sub), self.outside(self.result[sub[0]], sub, core), p, AT_RESULT + i, self.spot.sibling)
            for i, sub in enumerate(PARTS[p])
            if sub[-1]
        ]

    def kept(self, core, p):
        return [
            pltpu.make_async_copy(
                self.inside(self.final.at[p % SLOTS], sub), self.outside(self.result[sub[0]], sub, core), self.keep_sem.at[p, i]
            )
            for i, sub in enumerate(PARTS[p])
            if sub[-1]
        ]

    def give(self, core, p):
        for copy in self.given(core, p):
            copy.start()

    def fetch(self, core, p):
        for copy in self.given(core, p):
            copy.wait_recv()
        for copy in self.loads(core, p):
            copy.start()

    def stage_one(self, core, p):
        for copy in self.loads(core, p):
            copy.wait()
        slot = p % SLOTS

        def add(i, carry):
            at = (i // 4, i // 2 % 2, i % 2)
            self.sums[slot, at[0], at[1], at[2]] += self.other[p % 2, at[0], at[1], at[2]]
            return carry

        lax.fori_loop(0, 16, add, 0)
        if p >= SLOTS:
            for i in range(5):
                pl.semaphore_wait(self.free.at[i], 1)
        self.first(core, p).start()

    def stage_two(self, core, p):
        s, slot = self.spot, p % SLOTS
        self.first(core, p).wait_recv()

        def add(i, carry):
            if core == 0:
                self.sums[slot, i // 2, s.x, i % 2] += self.one_in[slot, i // 2, i % 2]
            else:
                self.sums[slot, i // 2, i % 2, s.y] += self.one_in[slot, i // 2, i % 2]
            return carry

        lax.fori_loop(0, 8, add, 0)
        if core == 0:
            for k in (1, 3, 2):
                self.hop(core, p, k).start()
        else:
            self.next(core, p).start()

    def stage_three(self, core, p):
        s, slot = self.spot, p % SLOTS
        if core == 0:
            for k in (1, 3, 2):
                self.hop(core, p, k).wait_recv()

            def add(i, carry):
                total = self.sums[slot, s.z, s.x, i].astype(WIDE)
                for k in range(3):
                    total += self.next_in[slot, 2 * k + i].astype(WIDE)
                self.sums[slot, s.z, s.x, i] = total.astype(LOW)
                return carry

            lax.fori_loop(0, 2, add, 0)
            self.next(core, p).start()
        else:
            self.next(core, p).wait_recv()

            def add(i, carry):
                self.sums[slot, i, s.x, s.y] += self.next_in[slot, i]
                return carry

            lax.fori_loop(0, 4, add, 0)
            for k in (1, 3, 2):
                self.hop(core, p, k).start()

    def stage_four(self, core, p):
        s, slot = self.spot, p % SLOTS
        if core == 0:
            self.next(core, p).wait_recv()

            def add(i, carry):
                self.final[slot, i] = self.sums[slot, s.z, s.x, i] + self.next_in[slot, 6 + i]
                return carry

            lax.fori_loop(0, 2, add, 0)
        else:
            for k in (1, 3, 2):
                self.hop(core, p, k).wait_recv()
            total = self.sums[slot, s.z, s.x, s.y].astype(WIDE)
            for k in range(3):
                total += self.next_in[slot, 4 + k].astype(WIDE)
            self.final[slot, s.y] = total.astype(LOW)
            self.last(p, True).start()

    def stage_five(self, core, p):
        if core == 1:
            self.last(p, False).wait_recv()
        for copy in self.results(core, p) + self.kept(core, p):
            copy.start()

    def release(self, core, p):
        self.first(core, p).wait_send()
        for k in (1, 2, 3):
            self.hop(core, p, k).wait_send()
        self.next(core, p).wait_send()
        if core == 1:
            self.last(p, True).wait_send()
        for copy in self.results(core, p):
            copy.wait_send()
        for copy in self.kept(core, p):
            copy.wait()
        if p + SLOTS < len(PARTS):
            s = self.spot
            for i, device in enumerate((s.to_x, s.to_y)):
                pl.semaphore_signal(self.free.at[i], 1, device_id=device, device_id_type=MESH)
            for k in (1, 2, 3):
                pl.semaphore_signal(self.free.at[1 + 4 - k], 1, device_id=s.hop(k), device_id_type=MESH)

    def finish(self, core, p):
        for copy in self.given(core, p):
            copy.wait_send()
        for copy in self.results(1 - core, p):
            copy.wait_recv()

    def program(self):
        count = len(PARTS)
        turns = [[("fetch", 0)]]
        for s in range(count + 6):
            turn = []
            for stage, p in (
                ("stage_one", s),
                ("fetch", s + 1),
                ("stage_two", s - 1),
                ("stage_three", s - 2),
                ("stage_four", s - 3),
                ("stage_five", s - 4),
                ("release", s - 5),
            ):
                if 0 <= p < count:
                    turn.append((stage, p))
            turns.append(turn)
        return turns

    def run(self, steps):
        for core in (0, 1):

            @pl.when(self.spot.core == core)
            def _():
                for stage, p in steps:
                    getattr(self, stage)(core, p)


def backward_kernel(per_place, *refs):
    dense_kinds = [kind for kind in KINDS if kind not in ("CELL", "TABLE")]
    grads = dict(zip(dense_kinds, refs[:6]))
    record_in, cell, codes, lengths, pool_grad = refs[6:11]
    result = dict(zip(KINDS, refs[11:19]))
    landing, grads["CELL"], grads["TABLE"] = refs[19:22]
    record, state_grad, total, cell_part, table_part = refs[22:27]
    buffers, (record_sem, out_sem), sems = refs[27:32], refs[32:34], refs[34:39]
    spot = Spot(per_place)

    def record_copy(t):
        return pltpu.make_async_copy(record_in.at[t], record.at[t], record_sem.at[t])

    def fill(i, carry):
        record_copy(CHARS - 1 - i).start()
        return carry

    lax.fori_loop(0, CHARS, fill, 0)
    spot.greet()
    reduce = Reduce(spot, grads, landing, buffers, result, sems)
    reduce.run([("give", p) for p in range(DENSE_PARTS)])
    turns = reduce.program()
    state_grad[...] = jnp.zeros_like(state_grad)
    total[...] = jnp.zeros_like(total)
    early = TURNS_IN_LOOP
    steps = [step for turn in turns[:early] for step in turn]
    share = -(-len(steps) // CHARS)

    def retreat(i, carry):
        t = CHARS - 1 - i
        record_copy(t).wait()
        gru_backward_step(t, cell, record, state_grad, pool_grad, lengths)
        for k in range(CHARS):

            @pl.when(i == k)
            def _():
                reduce.run(steps[k * share : (k + 1) * share])

        return carry

    lax.fori_loop(0, CHARS, retreat, 0)
    for way in (0, 1):
        cell_gradient(way, record, cell_part)
        copy = pltpu.make_async_copy(cell_part, grads["CELL"].at[pl.ds(2 * way, 2)], out_sem.at[0])
        copy.start()
        reduce.run(turns[early + way])
        copy.wait()

    def look_up(c, carry):
        table_gradient(c, cell, record, codes, total)
        return carry

    lax.fori_loop(0, CHARS, look_up, 0)
    table_part[...] = jnp.transpose(total[...]).astype(LOW).reshape((4, 2, 2) + BLOCKS["TABLE"])
    copy = pltpu.make_async_copy(table_part, grads["TABLE"], out_sem.at[0])
    copy.start()
    copy.wait()
    reduce.run([("give", p) for p in range(DENSE_PARTS, len(PARTS))])
    for turn in turns[early + 2 :]:
        reduce.run(turn)
    reduce.run([("finish", p) for p in range(len(PARTS))])


TURNS_IN_LOOP = 7


def reduce_and_return(grads, record, cell, codes, lengths, pool_grad, per_place):
    dense_kinds = [kind for kind in KINDS if kind not in ("CELL", "TABLE")]
    in_vmem = pl.BlockSpec(memory_space=pltpu.VMEM)
    anywhere = pl.BlockSpec(memory_space=pl.ANY)
    count = len(PARTS)
    shapes = [jax.ShapeDtypeStruct((2,) + BLOCKS[kind], LOW) for kind in KINDS]
    shapes += [jax.ShapeDtypeStruct((count, 4, 2, 2, ROWS, LANES), LOW)]
    shapes += [jax.ShapeDtypeStruct((4, 2, 2) + BLOCKS[kind], LOW) for kind in ("CELL", "TABLE")]
    results = pl.pallas_call(
        partial(backward_kernel, per_place),
        out_shape=shapes,
        in_specs=[anywhere] * 7 + [in_vmem] * 4,
        out_specs=[anywhere] * len(shapes),
        scratch_shapes=[
            pltpu.VMEM((CHARS, TOKENS, 2 * RECORD), LOW),
            pltpu.VMEM((TOKENS, 2 * HID), WIDE),
            pltpu.VMEM((1024, EMB), WIDE),
            pltpu.VMEM((2, 2, 2) + BLOCKS["CELL"], LOW),
            pltpu.VMEM((4, 2, 2) + BLOCKS["TABLE"], LOW),
            pltpu.VMEM((SLOTS, 4, 2, 2, ROWS, LANES), LOW),
            pltpu.VMEM((2, 4, 2, 2, ROWS, LANES), LOW),
            pltpu.VMEM((SLOTS, 4, 2, ROWS, LANES), LOW),
            pltpu.VMEM((SLOTS, 8, ROWS, LANES), LOW),
            pltpu.VMEM((SLOTS, 2, ROWS, LANES), LOW),
            pltpu.SemaphoreType.DMA((CHARS,)),
            pltpu.SemaphoreType.DMA((1,)),
            pltpu.SemaphoreType.DMA((count, MOVES)),
            pltpu.SemaphoreType.DMA((count, MOVES)),
            pltpu.SemaphoreType.DMA((2, SUBS + 1)),
            pltpu.SemaphoreType.DMA((count, SUBS)),
            pltpu.SemaphoreType.REGULAR((5,)),
        ],
        compiler_params=pltpu.CompilerParams(collective_id=1, has_side_effects=True, vmem_limit_bytes=60 << 20),
    )(*[grads[kind] for kind in dense_kinds], record, cell, codes, lengths, pool_grad)
    return dict(zip(KINDS, results[:8]))


def layer_norm(inputs, gain_row, shift_row):
    centred = inputs - jnp.mean(inputs, axis=-1, keepdims=True)
    spread = jnp.mean(centred * centred, axis=-1, keepdims=True)
    return centred * lax.rsqrt(spread + norm_eps) * gain_row + shift_row


def gelu_exact(inputs):
    return jax.nn.gelu(inputs, approximate=False)


def dense(whole, hidden, sequence_length, cotangent, pooled):
    w = {kind: part.reshape(-1, part.shape[-1]) for kind, part in whole.items()}
    small = w["OUT"][:, 768:785]
    small_rows = jnp.transpose(small[:, :13]).astype(WIDE)
    biases, gains = small_rows[:10], small_rows[10:]
    feed_bias = small[:, 13:].reshape(-1).astype(WIDE)
    length, width = hidden.shape
    head = width // HEADS
    scale = head ** (-0.5)
    joint_bias = jnp.concatenate([biases[0], jnp.zeros_like(biases[0]), biases[1]])
    projected = (dot_second(hidden, w["ATT"]) + joint_bias).astype(LOW)
    projected = projected.reshape(length, 3, HEADS, head)
    queries, keys, values = projected[:, 0], projected[:, 1], projected[:, 2]
    mask = jnp.where(jnp.arange(length) < sequence_length[0], 0.0, masked_score).astype(WIDE)
    scores = jnp.einsum("qhd,khd->hqk", queries, keys, preferred_element_type=WIDE) * scale + mask
    weight = jnp.exp(scores - jnp.max(scores, axis=-1, keepdims=True))
    soft = weight / jnp.sum(weight, axis=-1, keepdims=True)
    soft_low = soft.astype(LOW)
    context = jnp.einsum("hqk,khd->qhd", soft_low, values, preferred_element_type=WIDE)
    context = context.astype(LOW).reshape(length, width)
    one_sum = hidden.astype(WIDE) + dot_second(context, w["OUT"][:, :768]) + biases[2]
    first = layer_norm(one_sum, gains[0], biases[3])
    first_low = first.astype(LOW)
    inner = dot_second(first_low, w["IN"]) + feed_bias
    active = gelu_exact(inner).astype(LOW)
    two_sum = first + dot_second(active, w["FEED"]) + biases[4]
    second = layer_norm(two_sum, gains[1], biases[5])
    second_low = second.astype(LOW)
    pooled_low = pooled.astype(LOW)
    token_side = dot_second(second_low, w["STREAM"][:, :768]) + biases[6]
    char_side = dot_second(pooled_low, w["STREAM"][:, 768:]) + biases[7]
    joined = jnp.concatenate([token_side, char_side], axis=-1).astype(LOW)
    padded = jnp.pad(joined, ((1, 1), (0, 0)))
    windows = jnp.concatenate([padded[:-2], padded[1:-1], padded[2:]], axis=-1)
    third_sum = second + dot_second(windows, w["MERGE"]) + biases[8]
    output = layer_norm(third_sum, gains[2], biases[9]).astype(LOW)

    _, pull_three = jax.vjp(layer_norm, third_sum, gains[2], biases[9])
    merged_grad, gain_three, shift_three = pull_three(cotangent.astype(WIDE))
    merged_low = merged_grad.astype(LOW)
    grads = {"MERGE": dot_first(merged_low, windows)}
    window_grad = dot_plain(merged_low, w["MERGE"]).reshape(length, 3, 2 * width)
    joined_grad = (
        window_grad[:, 1]
        + jnp.pad(window_grad[1:, 0], ((0, 1), (0, 0)))
        + jnp.pad(window_grad[:-1, 2], ((1, 0), (0, 0)))
    )
    token_grad, char_grad = joined_grad[:, :width], joined_grad[:, width:]
    token_low, char_low = token_grad.astype(LOW), char_grad.astype(LOW)
    grads["STREAM"] = jnp.concatenate([dot_first(token_low, second_low), dot_first(char_low, pooled_low)], axis=1)
    pooled_grad = dot_plain(char_low, w["STREAM"][:, 768:])
    second_grad = merged_grad + dot_plain(token_low, w["STREAM"][:, :768])
    _, pull_two = jax.vjp(layer_norm, two_sum, gains[1], biases[5])
    two_grad, gain_two, shift_two = pull_two(second_grad)
    two_low = two_grad.astype(LOW)
    grads["FEED"] = dot_first(two_low, active)
    _, pull_gelu = jax.vjp(gelu_exact, inner)
    (inner_grad,) = pull_gelu(dot_plain(two_low, w["FEED"]))
    inner_low = inner_grad.astype(LOW)
    grads["IN"] = dot_first(inner_low, first_low)
    first_grad = two_grad + dot_plain(inner_low, w["IN"])
    _, pull_one = jax.vjp(layer_norm, one_sum, gains[0], biases[3])
    one_grad, gain_one, shift_one = pull_one(first_grad)
    one_low = one_grad.astype(LOW)
    grad_out = dot_first(one_low, context)
    context_grad = dot_plain(one_low, w["OUT"][:, :768]).astype(LOW).reshape(length, HEADS, head)
    soft_grad = jnp.einsum("qhd,khd->hqk", context_grad, values, preferred_element_type=WIDE)
    value_grad = jnp.einsum("hqk,qhd->khd", soft_low, context_grad, preferred_element_type=WIDE)
    score_grad = soft * (soft_grad - jnp.sum(soft * soft_grad, axis=-1, keepdims=True))
    score_low = score_grad.astype(LOW)
    query_grad = jnp.einsum("hqk,khd->qhd", score_low, keys, preferred_element_type=WIDE) * scale
    key_grad = jnp.einsum("hqk,qhd->khd", score_low, queries, preferred_element_type=WIDE) * scale
    projected_low = jnp.stack([query_grad, key_grad, value_grad], axis=1).reshape(length, 3 * width).astype(LOW)
    grads["ATT"] = dot_first(projected_low, hidden)
    hidden_grad = (one_grad + dot_plain(projected_low, w["ATT"])).astype(LOW)
    small_grads = jnp.stack(
        [
            jnp.sum(query_grad, axis=0).reshape(width),
            jnp.sum(value_grad, axis=0).reshape(width),
            jnp.sum(one_grad, axis=0),
            shift_one,
            jnp.sum(two_grad, axis=0),
            shift_two,
            jnp.sum(token_grad, axis=0),
            jnp.sum(char_grad, axis=0),
            jnp.sum(merged_grad, axis=0),
            shift_three,
            gain_one,
            gain_two,
            gain_three,
        ]
    )
    feed_bias_grad = jnp.sum(inner_grad, axis=0).reshape(width, 4)
    grads["OUT"] = jnp.pad(
        jnp.concatenate([grad_out, jnp.transpose(small_grads), feed_bias_grad], axis=1), ((0, 0), (0, 256 - 17))
    )
    grads = {
        kind: part.astype(LOW).reshape((4, 2, 2) + BLOCKS[kind]) for kind, part in grads.items()
    }
    return output, hidden_grad, pooled_grad, grads


def unpack(final):
    part = {kind: value.reshape(-1, value.shape[-1]).astype(WIDE) for kind, value in final.items()}
    cell, table, out, stream, merge = (part[kind] for kind in ("CELL", "TABLE", "OUT", "STREAM", "MERGE"))
    small = out[:, 768:785]
    return (
        part["ATT"].T,
        out[:, :768].T,
        part["IN"].T,
        small[:, 13:].reshape(-1),
        part["FEED"].T,
        table[:, :1000].T,
        cell[:, :EMB].T,
        cell[:, EMB : EMB + HID].T,
        cell[:, EMB + HID : EMB + HID + 2].T,
        jnp.stack([stream[:, :768].T, stream[:, 768:].T]),
        jnp.stack([merge[:, k * 1536 : (k + 1) * 1536].T for k in range(3)]),
        small[:, 10:13].T,
        small[:, :10].T,
    )


def shards(hidden, char_codes, word_length, sequence_length, cotangent, *parameters):
    wide = lax.axis_size("wide")
    per_place = wide // 2
    own = pack(parameters, per_place)
    codes = jnp.transpose(char_codes)[:, :, None]
    lengths = word_length[:, None]
    whole, record, pooled = gather_and_read(own, codes, lengths, per_place)
    output, hidden_grad, pooled_grad, grads = dense(whole, hidden, sequence_length, cotangent, pooled)
    pool_grad = pooled_grad / lengths.astype(WIDE)
    rows = jnp.transpose(char_codes)
    final = reduce_and_return(grads, record, whole["CELL"], rows, lengths, pool_grad, per_place)
    return (output, hidden_grad, *unpack(final))


def solution(mesh):
    rows = P(("grp", "wide"), None)
    flat = P(("grp", "wide"))
    last = P(None, ("grp", "wide"))
    deep = P(None, None, ("grp", "wide"))
    in_specs = (rows, rows, flat, flat, rows, last, last, last, flat, last, last, last, last, last, deep, deep, last, last)
    out_specs = (rows, rows) + (P(None, "grp"),) * 3 + (P("grp"),) + (P(None, "grp"),) * 5 + (P(None, None, "grp"),) * 2 + (P(None, "grp"),) * 2
    return jax.shard_map(shards, mesh=mesh, in_specs=in_specs, out_specs=out_specs, check_vma=False)
```

```python
from functools import partial

import jax
import jax.numpy as jnp
from jax import lax
from jax.experimental import pallas as pl
from jax.experimental.pallas import tpu as pltpu
from jax.sharding import PartitionSpec as P

HEADS = 12
HID = 384
EMB = 256
CHARS = 20
TOKENS = 128
norm_eps = 1e-05
masked_score = -1e30
MESH = pl.DeviceIdType.MESH
EVERY = slice(None)
LOW = jnp.bfloat16
WIDE = jnp.float32

BLOCKS = {
    "CELL": (144, 768),
    "TABLE": (16, 1024),
    "ATT": (144, 768),
    "OUT": (48, 1024),
    "IN": (192, 768),
    "FEED": (48, 3072),
    "STREAM": (48, 1536),
    "MERGE": (48, 4608),
}
KINDS = tuple(BLOCKS)
PIECES = (
    ("CELL", 0, 384, 384),
    ("TABLE", 0, 512, 512),
    ("ATT", 0, 384, 384),
    ("OUT", 0, 512, 512),
    ("IN", 0, 128, 128),
    ("IN", 256, 512, 256),
    ("FEED", 0, 768, 768),
    ("FEED", 1536, 2304, 768),
    ("STREAM", 0, 768, 768),
    ("MERGE", 0, 768, 768),
    ("MERGE", 1536, 2304, 768),
    ("MERGE", 3072, 3840, 768),
)

AHEAD = 3

X_WIDTH = 768
RECORD = X_WIDTH + 4 * HID
GATE_R, GATE_Z, GATE_N, GATE_Q = (X_WIDTH + i * HID for i in range(4))


def dot_plain(left_side, right_side):
    return jnp.dot(left_side, right_side, preferred_element_type=WIDE)


def dot_first(left_side, right_side):
    return lax.dot_general(left_side, right_side, (((0,), (0,)), ((), ())), preferred_element_type=WIDE)


def dot_second(left_side, right_side):
    return lax.dot_general(left_side, right_side, (((1,), (1,)), ((), ())), preferred_element_type=WIDE)


def lanes_of(ref, start, width):
    return ref[:, pl.ds(start, width)]


def sigmoid(inputs):
    return 0.5 * jnp.tanh(0.5 * inputs) + 0.5


class Spot:
    def __init__(self, per_place):
        self.grp, self.wide = lax.axis_index("grp"), lax.axis_index("wide")
        self.z, self.x = self.grp // 2, self.grp % 2
        self.y, self.core = self.wide // per_place, self.wide % 2
        self.to_x = (self.grp + 1 - 2 * self.x, self.wide)
        self.to_y = (self.grp, self.wide + per_place - 2 * per_place * self.y)
        self.sibling = (self.grp, self.wide + 1 - 2 * self.core)

    def hop(self, k):
        return (2 * ((self.z + k) % 4) + self.x, self.wide)

    def greet(self):
        barrier = pltpu.get_barrier_semaphore()
        for other in [self.to_x, self.to_y, self.sibling] + [self.hop(k) for k in (1, 2, 3)]:
            pl.semaphore_signal(barrier, 1, device_id=other, device_id_type=MESH)
        pl.semaphore_wait(barrier, 6)

    def near(self, core):
        if core == 0:
            return self.x, self.y, self.to_x, self.to_y
        return self.y, self.x, self.to_y, self.to_x


def remote(source, target, sent, received, device):
    return pltpu.make_async_remote_copy(
        src_ref=source, dst_ref=target, send_sem=sent, recv_sem=received, device_id=device, device_id_type=MESH
    )


class Gather:
    def __init__(self, spot, whole, sems):
        self.spot, self.whole = spot, whole
        self.sent, self.got = sems

    def region(self, core, p, z, f, l):
        kind, first, second, width = PIECES[p]
        lanes = pl.ds((first, second)[core], width)
        return self.whole[kind].at[z, f, l, :, lanes] if core == 0 else self.whole[kind].at[z, l, f, :, lanes]

    def move(self, part, p, j, device):
        return remote(part, part, self.sent.at[p, j], self.got.at[p, j], device)

    def along(self, core, p, k):
        f, l, _, _ = self.spot.near(core)
        return self.move(self.region(core, p, self.spot.z, f, l), p, k - 1, self.spot.hop(k))

    def along_in(self, core, p, k):
        f, l, _, _ = self.spot.near(core)
        return self.move(self.region(core, p, (self.spot.z + 4 - k) % 4, f, l), p, k - 1, self.spot.hop(k))

    def line(self, core, p, mine):
        f, l, to_f, _ = self.spot.near(core)
        return self.move(self.region(core, p, EVERY, f if mine else 1 - f, l), p, 3, to_f)

    def plane(self, core, p, mine):
        f, l, _, to_l = self.spot.near(core)
        return self.move(self.region(core, p, EVERY, EVERY, l if mine else 1 - l), p, 4, to_l)

    def aside(self, core, p, j):
        f, l, _, _ = self.spot.near(core)
        if j < 3:
            part = self.region(core, p, (self.spot.z + 3 - j) % 4, f, l)
        elif j == 3:
            part = self.region(core, p, EVERY, 1 - f, l)
        else:
            part = self.region(core, p, EVERY, EVERY, 1 - l)
        return self.move(part, p, 5 + j, self.spot.sibling)

    def start(self, core, p):
        for k in (1, 3, 2):
            self.along(core, p, k).start()

    def second(self, core, p):
        for k in (1, 3, 2):
            self.along_in(core, p, k).wait_recv()
        self.line(core, p, True).start()
        for k in (1, 3, 2):
            self.aside(core, p, k - 1).start()

    def third(self, core, p):
        self.line(core, p, False).wait_recv()
        self.plane(core, p, True).start()
        self.aside(core, p, 3).start()

    def fourth(self, core, p):
        self.plane(core, p, False).wait_recv()
        self.aside(core, p, 4).start()

    def fifth(self, core, p):
        for j in range(5):
            self.aside(1 - core, p, j).wait_recv()

    def drain(self, core, p):
        for k in (1, 2, 3):
            self.along(core, p, k).wait_send()
        self.line(core, p, True).wait_send()
        self.plane(core, p, True).wait_send()
        for j in range(5):
            self.aside(core, p, j).wait_send()

    def turns(self):
        count = len(PIECES)
        turns = []
        for s in range(count + 3):
            ahead = range(AHEAD + 1) if s == 0 else [s + AHEAD]
            turn = [("start", p) for p in ahead if p < count]
            for lag, stage in enumerate(("second", "third", "fourth", "fifth")):
                if 0 <= s - lag < count:
                    turn.append((stage, s - lag))
            turns.append(turn)
        return turns

    def run(self, steps):
        for core in (0, 1):

            @pl.when(self.spot.core == core)
            def _():
                for stage, p in steps:
                    getattr(self, stage)(core, p)


RING = 4


def gru_forward_step(t, cell, spelled, record, state, total, shifts, lengths):
    slot = t % RING
    for way in (0, 1):
        base = way * RECORD
        place = t if way == 0 else CHARS - 1 - t
        live = lengths[...] > place
        lanes = pl.ds(way * HID, HID)
        h = state[:, lanes]
        record[slot, :, pl.ds(base, EMB)] = spelled[place]
        record[slot, :, pl.ds(base + EMB, HID)] = h.astype(LOW)
        x = record[slot, :, pl.ds(base, X_WIDTH)]
        weights = cell[pl.ds(2 * way, 2)].reshape(3 * HID, X_WIDTH)
        both = dot_second(x, weights[: 2 * HID])
        drive_n = dot_second(x[:, :EMB], weights[2 * HID :, :EMB]) + shifts[way, 0:1]
        recur_n = dot_second(x[:, EMB : EMB + HID], weights[2 * HID :, EMB : EMB + HID]) + shifts[way, 1:2]
        r = sigmoid(both[:, :HID])
        u = sigmoid(both[:, HID:])
        n = jnp.tanh(drive_n + r * recur_n)
        fresh = jnp.where(live, n + u * (h - n), h)
        state[:, lanes] = fresh
        total[:, lanes] += jnp.where(live, fresh, 0.0)
        record[slot, :, pl.ds(base + GATE_R, HID)] = r.astype(LOW)
        record[slot, :, pl.ds(base + GATE_Z, HID)] = u.astype(LOW)
        record[slot, :, pl.ds(base + GATE_N, HID)] = n.astype(LOW)
        record[slot, :, pl.ds(base + GATE_Q, HID)] = recur_n.astype(LOW)


def spread_matrix():
    shape = (512, 512)
    row, lane = lax.broadcasted_iota(jnp.int32, shape, 0), lax.broadcasted_iota(jnp.int32, shape, 1)
    return (4 * (row % 128) + row // 128 == lane).astype(LOW)


def read_small(out, small, feed_row, shuffle):
    columns = out[:, :, :, :, pl.ds(768, 128)].reshape(768, 128).astype(WIDE)
    rows = jnp.transpose(columns)
    small[...] = rows[:32]
    shuffle[...] = jnp.zeros_like(shuffle)
    for c in range(6):
        for j in range(4):
            shuffle[c : c + 1, 128 * j : 128 * j + 128] = rows[13 + j : 14 + j, 128 * c : 128 * c + 128]
    flat = dot_plain(shuffle[...].astype(LOW), spread_matrix())
    for c in range(6):
        feed_row[:, 512 * c : 512 * c + 512] = flat[c : c + 1]


def norm_forward(inputs, i, small, gain, shift, norms, spreads):
    centred = inputs - jnp.mean(inputs, axis=-1, keepdims=True)
    inverse = lax.rsqrt(jnp.mean(centred * centred, axis=-1, keepdims=True) + norm_eps)
    unit = centred * inverse
    norms[i] = unit
    spreads[i] = jnp.broadcast_to(inverse, spreads.shape[1:])
    return unit * small[gain : gain + 1] + small[shift : shift + 1]


def head_mask(which):
    lane = lax.broadcasted_iota(jnp.int32, (TOKENS, 128), 1)
    return (lane < 64) if which == 0 else (lane >= 64)


def one_head(pair, which):
    return jnp.where(head_mask(which), pair, jnp.zeros_like(pair))


def soft_weights(queries, keys, which, valid):
    scores = dot_second(one_head(queries, which), keys) * 0.125 + valid
    weight = jnp.exp(scores - jnp.max(scores, axis=-1, keepdims=True))
    return weight / jnp.sum(weight, axis=-1, keepdims=True)


def key_mask(count):
    lane = lax.broadcasted_iota(jnp.int32, (TOKENS, TOKENS), 1)
    return jnp.where(lane < count, 0.0, masked_score).astype(WIDE)


def attention_forward(projected, context, valid):
    def pair(i, carry):
        def part(at):
            return projected[:, pl.ds(pl.multiple_of(at * 768 + 128 * i, 128), 128)]

        queries, keys, values = part(0), part(1), part(2)
        total = jnp.zeros((TOKENS, 128), WIDE)
        for which in (0, 1):
            soft = soft_weights(queries, keys, which, valid).astype(LOW)
            total += dot_plain(soft, one_head(values, which))
        context[:, pl.ds(pl.multiple_of(128 * i, 128), 128)] = total.astype(LOW)
        return carry

    lax.fori_loop(0, 6, pair, 0)


def shifted(rows, down):
    turned = pltpu.roll(rows, 1 if down else TOKENS - 1, 0)
    row = lax.broadcasted_iota(jnp.int32, rows.shape, 0)
    return jnp.where(row == (0 if down else TOKENS - 1), 0.0, turned)


def window(joined, k):
    if k == 1:
        return joined[...]
    return shifted(joined[...].astype(WIDE), k == 0).astype(LOW)


def forward_kernel(per_place, *refs):
    count = len(KINDS)
    own = dict(zip(KINDS, refs[:count]))
    codes, lengths, hidden, valid_keys = refs[count : count + 4]
    outs = refs[count + 4 :]
    kept = dict(zip(KINDS, outs[:count]))
    (record_out, output, projected, context, active, slope, joined, pooled_low, norms, spreads, small) = outs[count : count + 11]
    scratch = outs[count + 11 :]
    whole = dict(zip(KINDS, scratch[:count]))
    (record, spelled, state, pooled, shifts, feed_row, shuffle, first, second, merged, sent, got, own_sem, kept_sem, record_sem) = scratch[count:]
    spot = Spot(per_place)
    own_copies = [
        pltpu.make_async_copy(own[kind], whole[kind].at[spot.z, spot.x, spot.y], own_sem.at[i])
        for i, kind in enumerate(KINDS)
    ]
    for copy in own_copies:
        copy.start()
    spot.greet()
    for copy in own_copies:
        copy.wait()
    gather = Gather(spot, whole, (sent, got))
    turns = gather.turns()

    def keep(kind):
        return pltpu.make_async_copy(whole[kind], kept[kind], kept_sem.at[KINDS.index(kind)])

    def weights(kind):
        value = whole[kind][...]
        return value.reshape(-1, value.shape[-1])

    for turn in turns[:5]:
        gather.run(turn)
    for kind in ("CELL", "TABLE"):
        keep(kind).start()
    cell, table = whole["CELL"], weights("TABLE")

    def embed(c, carry):
        which = (lax.broadcasted_iota(jnp.int32, (1024, TOKENS), 0) == codes[pl.ds(c, 1)]).astype(LOW)
        spelled[c] = jnp.transpose(dot_plain(table, which)).astype(LOW)
        return carry

    lax.fori_loop(0, CHARS, embed, 0)
    pick = (
        lax.broadcasted_iota(jnp.int32, (8, 128), 0) == lax.broadcasted_iota(jnp.int32, (8, 128), 1)
    ).astype(LOW)
    ones = (lax.broadcasted_iota(jnp.int32, (TOKENS, 128), 1) < 2).astype(LOW)
    for way in (0, 1):
        late = cell[pl.ds(2 * way, 2)].reshape(3 * HID, X_WIDTH)[2 * HID :, EMB + HID :]
        shifts[way] = dot_second(pick, late)
        for slot in range(RING):
            record[slot, :, pl.ds(way * RECORD + EMB + HID, 128)] = ones
    state[...] = jnp.zeros_like(state)
    pooled[...] = jnp.zeros_like(pooled)
    steps = [step for turn in turns[5:GRU_TURNS] for step in turn]
    share = -(-len(steps) // CHARS)

    def record_copy(t):
        return pltpu.make_async_copy(record.at[t % RING], record_out.at[t], record_sem.at[t % RING])

    def advance(t, carry):
        @pl.when(t >= RING)
        def _():
            record_copy(t - RING).wait()

        gru_forward_step(t, cell, spelled, record, state, pooled, shifts, lengths)
        record_copy(t).start()
        for k in range(CHARS):
            if steps[k * share : (k + 1) * share]:

                @pl.when(t == k)
                def _():
                    gather.run(steps[k * share : (k + 1) * share])

        return carry

    lax.fori_loop(0, CHARS, advance, 0)
    pooled_low[...] = (pooled[...] / lengths[...].astype(WIDE)).astype(LOW)

    later = iter(turns[GRU_TURNS:])

    def go_on():
        gather.run(next(later))

    for kind in ("ATT", "OUT"):
        keep(kind).start()
    read_small(whole["OUT"], small, feed_row, shuffle)
    attention_in = weights("ATT")
    for i, bias in enumerate((0, None, 1)):
        block = dot_second(hidden[...], attention_in[768 * i : 768 * i + 768])
        if bias is not None:
            block = block + small[bias : bias + 1]
        projected[:, 768 * i : 768 * i + 768] = block.astype(LOW)
    attention_forward(projected, context, key_mask(valid_keys[0]))
    attended = dot_second(context[...], weights("OUT")[:, :768]) + small[2:3]
    first[...] = norm_forward(hidden[...].astype(WIDE) + attended, 0, small, 10, 3, norms, spreads)
    go_on()
    keep("IN").start()
    first_low = first[...].astype(LOW)
    for c in range(4):
        rows = whole["IN"][c].reshape(768, 768)
        inner = dot_second(first_low, rows) + feed_row[:, 768 * c : 768 * c + 768]
        share_below = 0.5 * (1.0 + lax.erf(inner * 0.7071067811865476))
        active[:, 768 * c : 768 * c + 768] = (inner * share_below).astype(LOW)
        slope[:, 768 * c : 768 * c + 768] = (
            share_below + inner * (0.3989422804014327 * jnp.exp(-0.5 * inner * inner))
        ).astype(LOW)
    go_on()
    go_on()
    keep("FEED").start()
    two = first[...] + dot_second(active[...], weights("FEED")) + small[4:5]
    second[...] = norm_forward(two, 1, small, 11, 5, norms, spreads)
    go_on()
    keep("STREAM").start()
    stream = weights("STREAM")
    joined[:, :768] = (dot_second(second[...].astype(LOW), stream[:, :768]) + small[6:7]).astype(LOW)
    joined[:, 768:] = (dot_second(pooled_low[...], stream[:, 768:]) + small[7:8]).astype(LOW)
    for k in range(3):
        go_on()
        taps = whole["MERGE"][:, :, :, :, pl.ds(1536 * k, 1536)].reshape(768, 1536)
        part = dot_second(window(joined, k), taps)
        merged[...] = part if k == 0 else merged[...] + part
    keep("MERGE").start()
    third = second[...] + merged[...] + small[8:9]
    output[...] = norm_forward(third, 2, small, 12, 9, norms, spreads).astype(LOW)

    def landed(t, carry):
        record_copy(t).wait()
        return carry

    lax.fori_loop(CHARS - RING, CHARS, landed, 0)
    gather.run([("drain", p) for p in range(len(PIECES))])
    for kind in KINDS:
        keep(kind).wait()


GRU_TURNS = 8


def gather_and_read(own, codes, lengths, hidden, valid_keys, per_place):
    count = len(KINDS)
    in_vmem = pl.BlockSpec(memory_space=pltpu.VMEM)
    anywhere = pl.BlockSpec(memory_space=pl.ANY)
    whole_shapes = [(4, 2, 2) + BLOCKS[kind] for kind in KINDS]
    saved = {
        "output": ((TOKENS, 768), LOW),
        "projected": ((TOKENS, 2304), LOW),
        "context": ((TOKENS, 768), LOW),
        "active": ((TOKENS, 3072), LOW),
        "slope": ((TOKENS, 3072), LOW),
        "joined": ((TOKENS, 1536), LOW),
        "pooled": ((TOKENS, 768), LOW),
        "norms": ((3, TOKENS, 768), WIDE),
        "spreads": ((3, TOKENS, 128), WIDE),
        "small": ((32, 768), WIDE),
    }
    results = pl.pallas_call(
        partial(forward_kernel, per_place),
        out_shape=[jax.ShapeDtypeStruct(shape, LOW) for shape in whole_shapes]
        + [jax.ShapeDtypeStruct((CHARS, TOKENS, 2 * RECORD), LOW)]
        + [jax.ShapeDtypeStruct(shape, kind) for shape, kind in saved.values()],
        in_specs=[anywhere] * count + [in_vmem] * 3 + [pl.BlockSpec(memory_space=pltpu.SMEM)],
        out_specs=[anywhere] * (count + 1) + [in_vmem] * len(saved),
        scratch_shapes=[pltpu.VMEM(shape, LOW) for shape in whole_shapes]
        + [
            pltpu.VMEM((RING, TOKENS, 2 * RECORD), LOW),
            pltpu.VMEM((CHARS, TOKENS, EMB), LOW),
            pltpu.VMEM((TOKENS, 2 * HID), WIDE),
            pltpu.VMEM((TOKENS, 2 * HID), WIDE),
            pltpu.VMEM((2, 8, HID), WIDE),
            pltpu.VMEM((1, 3072), WIDE),
            pltpu.VMEM((8, 512), WIDE),
            pltpu.VMEM((TOKENS, 768), WIDE),
            pltpu.VMEM((TOKENS, 768), WIDE),
            pltpu.VMEM((TOKENS, 768), WIDE),
            pltpu.SemaphoreType.DMA((len(PIECES), 10)),
            pltpu.SemaphoreType.DMA((len(PIECES), 10)),
            pltpu.SemaphoreType.DMA((count,)),
            pltpu.SemaphoreType.DMA((count,)),
            pltpu.SemaphoreType.DMA((RING,)),
        ],
        compiler_params=pltpu.CompilerParams(collective_id=0, has_side_effects=True, vmem_limit_bytes=60 << 20),
    )(*[own[kind] for kind in KINDS], codes, lengths, hidden, valid_keys)
    return dict(zip(KINDS, results[:count])), results[count], dict(zip(saved, results[count + 1 :]))


def pack(shards, per_place):
    (attention_in, attention_out, feed_in, feed_bias, feed_out, char_table, cell_input, cell_recurrent, cell_bias,
     stream_weight, merging_kernel, norm_gains, biases) = shards

    def lanes(parts, width):
        together = jnp.concatenate(parts, axis=1)
        return jnp.pad(together, ((0, 0), (0, width - together.shape[1])))

    def flat(stacked):
        return [jnp.transpose(part) for part in stacked]

    rows = attention_out.shape[1]
    thin = lanes(
        [
            lanes([attention_out.T, biases.T, norm_gains.T, feed_bias.reshape(rows, 4)], 1024),
            feed_out.T,
            *flat(stream_weight),
            *flat(merging_kernel),
        ],
        10240,
    )
    middle = lanes([cell_input.T, cell_recurrent.T, cell_bias.T], 768)
    middle = jnp.concatenate([middle, attention_in.T], axis=1)
    parts = [thin, middle, feed_in.T, lanes([char_table.T], 1024)]
    if per_place == 2:
        size = lax.axis_size("wide")
        swap = [(i, i + 1 - 2 * (i % 2)) for i in range(size)]
        first = lax.axis_index("wide") % 2 == 0
        whole = []
        for part in parts:
            other = lax.ppermute(part, "wide", swap)
            whole.append(jnp.concatenate([jnp.where(first, part, other), jnp.where(first, other, part)], axis=0))
    else:
        size = lax.axis_size("wide")
        groups = [list(range(i, i + per_place)) for i in range(0, size, per_place)]
        whole = [lax.all_gather(part, "wide", axis=0, tiled=True, axis_index_groups=groups) for part in parts]
    thin, middle, feed, table = whole
    return {
        "CELL": middle[:, :768],
        "TABLE": table,
        "ATT": middle[:, 768:],
        "OUT": thin[:, :1024],
        "IN": feed,
        "FEED": thin[:, 1024:4096],
        "STREAM": thin[:, 4096:5632],
        "MERGE": thin[:, 5632:],
    }


def gru_backward_step(t, cell, record, state_grad, pool_grad, lengths):
    for way in (0, 1):
        base = way * RECORD
        place = t if way == 0 else CHARS - 1 - t
        live = lengths[...] > place
        lanes = pl.ds(way * HID, HID)

        def saved(at):
            return record[t, :, pl.ds(base + at, HID)].astype(WIDE)

        r, u, n, recur_n, h = saved(GATE_R), saved(GATE_Z), saved(GATE_N), saved(GATE_Q), saved(EMB)
        grad = state_grad[:, lanes]
        fresh = jnp.where(live, grad + pool_grad[:, lanes], 0.0)
        kept = jnp.where(live, 0.0, grad)
        grad_n = fresh * (1.0 - u) * (1.0 - n * n)
        grad_z = fresh * (h - n) * u * (1.0 - u)
        grad_r = grad_n * recur_n * r * (1.0 - r)
        low_r, low_z, low_n, low_q = (v.astype(LOW) for v in (grad_r, grad_z, grad_n, grad_n * r))
        record[t, :, pl.ds(base + GATE_R, HID)] = low_r
        record[t, :, pl.ds(base + GATE_Z, HID)] = low_z
        record[t, :, pl.ds(base + GATE_N, HID)] = low_n
        record[t, :, pl.ds(base + GATE_Q, HID)] = low_q
        weights = cell[pl.ds(2 * way, 2)].reshape(3 * HID, X_WIDTH)[:, EMB : EMB + HID]
        gates = jnp.concatenate([low_r, low_z, low_q], axis=1)
        state_grad[:, lanes] = kept + fresh * u + dot_plain(gates, weights)


def cell_gradient(way, record, result):
    base = way * RECORD
    rows = CHARS * TOKENS

    def every(at, width):
        return record[:, :, pl.ds(base + at, width)].reshape(rows, width)

    x = every(0, X_WIDTH)
    parts = [dot_first(every(at, HID), x).astype(LOW) for at in (GATE_R, GATE_Z)]
    drive, recur = dot_first(every(GATE_N, HID), x), dot_first(every(GATE_Q, HID), x)
    lane = lax.broadcasted_iota(jnp.int32, (HID, X_WIDTH), 1)
    parts.append(jnp.where((lane < EMB) | (lane == EMB + HID), drive, recur).astype(LOW))
    result[:, :, :, 0:144] = jnp.concatenate(parts, axis=0).reshape(2, 2, 2, 144, X_WIDTH)


def table_gradient(c, cell, record, codes, result):
    drive = jnp.zeros((TOKENS, EMB), WIDE)
    for way, t in ((0, c), (1, CHARS - 1 - c)):
        gates = record[t, :, pl.ds(way * RECORD + GATE_R, 3 * HID)]
        drive += dot_plain(gates, cell[pl.ds(2 * way, 2)].reshape(3 * HID, X_WIDTH)[:, :EMB])
    which = (lax.broadcasted_iota(jnp.int32, (1024, TOKENS), 0) == codes[pl.ds(c, 1)]).astype(LOW)
    result[...] += dot_plain(which, drive.astype(LOW))


ROWS, LANES = 48, 768
PARTS = (
    [("MERGE", 0, 48, 0, 768, 768, 0, 0, True)],
    [("MERGE", 0, 48, 1536, 2304, 768, 0, 0, True)],
    [("MERGE", 0, 48, 3072, 3840, 768, 0, 0, True)],
    [("STREAM", 0, 48, 0, 768, 768, 0, 0, True)],
    [("FEED", 0, 48, 0, 768, 768, 0, 0, True)],
    [("FEED", 0, 48, 1536, 2304, 768, 0, 0, True)],
    [("IN", 0, 48, 0, 384, 384, 0, 0, True), ("IN", 48, 48, 0, 384, 384, 0, 384, True)],
    [("IN", 96, 48, 0, 384, 384, 0, 0, True), ("IN", 144, 48, 0, 384, 384, 0, 384, True)],
    [("ATT", 0, 48, 0, 384, 384, 0, 0, True), ("ATT", 48, 48, 0, 384, 384, 0, 384, True)],
    [("ATT", 96, 48, 0, 384, 384, 0, 0, True), ("OUT", 0, 48, 0, 512, 384, 0, 384, True)],
    [("CELL", 0, 48, 0, 384, 384, 0, 0, True), ("CELL", 48, 48, 0, 384, 384, 0, 384, True)],
    [
        ("CELL", 96, 48, 0, 384, 384, 0, 0, True),
        ("OUT", 0, 48, 384, 896, 128, 0, 384, True),
        ("TABLE", 0, 16, 0, 512, 256, 0, 512, True),
        ("TABLE", 0, 16, 256, 768, 256, 16, 512, True),
        ("TABLE", 0, 16, 256, 768, 256, 32, 512, False),
    ],
)
SLOTS = 6
SUBS = 5
DENSE_PARTS = 10
AT_FIRST, AT_HOP, AT_NEXT, AT_LAST, AT_RESULT = SUBS, SUBS, SUBS + 4, SUBS + 5, SUBS + 6
MOVES = 2 * SUBS + 6


class Reduce:
    def __init__(self, spot, grads, landing, buffers, result, sems):
        self.spot, self.grads, self.landing, self.result = spot, grads, landing, result
        self.sums, self.other, self.one_in, self.next_in, self.final = buffers
        self.sent, self.got, self.load_sem, self.keep_sem, self.free = sems

    def move(self, source, target, p, j, device):
        return remote(source, target, self.sent.at[p, j], self.got.at[p, j], device)

    def outside(self, ref, sub, core):
        _, row, rows, first, second, width, _, _, _ = sub
        return ref.at[..., pl.ds(row, rows), pl.ds((first, second)[core], width)]

    def inside(self, ref, sub):
        _, _, rows, _, _, width, row, lane, _ = sub
        return ref.at[..., pl.ds(row, rows), pl.ds(lane, width)]

    def given(self, core, p):
        return [
            self.move(
                self.outside(self.grads[sub[0]], sub, 1 - core), self.inside(self.landing.at[p], sub), p, i, self.spot.sibling
            )
            for i, sub in enumerate(PARTS[p])
        ]

    def loads(self, core, p):
        own = [
            pltpu.make_async_copy(
                self.outside(self.grads[sub[0]], sub, core), self.inside(self.sums.at[p % SLOTS], sub), self.load_sem.at[p % 2, i]
            )
            for i, sub in enumerate(PARTS[p])
        ]
        return own + [pltpu.make_async_copy(self.landing.at[p], self.other.at[p % 2], self.load_sem.at[p % 2, SUBS])]

    def first(self, core, p):
        s, slot = self.spot, p % SLOTS
        if core == 0:
            return self.move(self.sums.at[slot, :, 1 - s.x], self.one_in.at[slot], p, AT_FIRST, s.to_x)
        return self.move(self.sums.at[slot, :, :, 1 - s.y], self.one_in.at[slot], p, AT_FIRST, s.to_y)

    def hop(self, core, p, k):
        s, slot = self.spot, p % SLOTS
        z = (s.z + k) % 4
        if core == 0:
            return self.move(self.sums.at[slot, z, s.x], self.next_in.at[slot, pl.ds(2 * k - 2, 2)], p, AT_HOP + k, s.hop(k))
        return self.move(self.sums.at[slot, z, s.x, s.y], self.next_in.at[slot, 3 + k], p, AT_HOP + k, s.hop(k))

    def next(self, core, p):
        s, slot = self.spot, p % SLOTS
        if core == 0:
            return self.move(self.sums.at[slot, s.z, s.x], self.next_in.at[slot, pl.ds(6, 2)], p, AT_NEXT, s.to_y)
        return self.move(self.sums.at[slot, :, 1 - s.x, s.y], self.next_in.at[slot, pl.ds(0, 4)], p, AT_NEXT, s.to_x)

    def last(self, p, mine):
        s, slot = self.spot, p % SLOTS
        part = self.final.at[slot, s.y if mine else 1 - s.y]
        return self.move(part, part, p, AT_LAST, s.to_y)

    def results(self, core, p):
        return [
            self.move(self.inside(self.final.at[p % SLOTS], sub), self.outside(self.result[sub[0]], sub, core), p, AT_RESULT + i, self.spot.sibling)
            for i, sub in enumerate(PARTS[p])
            if sub[-1]
        ]

    def kept(self, core, p):
        return [
            pltpu.make_async_copy(
                self.inside(self.final.at[p % SLOTS], sub), self.outside(self.result[sub[0]], sub, core), self.keep_sem.at[p, i]
            )
            for i, sub in enumerate(PARTS[p])
            if sub[-1]
        ]

    def give(self, core, p):
        for copy in self.given(core, p):
            copy.start()

    def fetch(self, core, p):
        for copy in self.given(core, p):
            copy.wait_recv()
        for copy in self.loads(core, p):
            copy.start()

    def stage_one(self, core, p):
        for copy in self.loads(core, p):
            copy.wait()
        slot = p % SLOTS

        def add(i, carry):
            at = (i // 4, i // 2 % 2, i % 2)
            self.sums[slot, at[0], at[1], at[2]] += self.other[p % 2, at[0], at[1], at[2]]
            return carry

        lax.fori_loop(0, 16, add, 0)
        if p >= SLOTS:
            for i in range(5):
                pl.semaphore_wait(self.free.at[i], 1)
        self.first(core, p).start()

    def stage_two(self, core, p):
        s, slot = self.spot, p % SLOTS
        self.first(core, p).wait_recv()

        def add(i, carry):
            if core == 0:
                self.sums[slot, i // 2, s.x, i % 2] += self.one_in[slot, i // 2, i % 2]
            else:
                self.sums[slot, i // 2, i % 2, s.y] += self.one_in[slot, i // 2, i % 2]
            return carry

        lax.fori_loop(0, 8, add, 0)
        if core == 0:
            for k in (1, 3, 2):
                self.hop(core, p, k).start()
        else:
            self.next(core, p).start()

    def stage_three(self, core, p):
        s, slot = self.spot, p % SLOTS
        if core == 0:
            for k in (1, 3, 2):
                self.hop(core, p, k).wait_recv()

            def add(i, carry):
                total = self.sums[slot, s.z, s.x, i].astype(WIDE)
                for k in range(3):
                    total += self.next_in[slot, 2 * k + i].astype(WIDE)
                self.sums[slot, s.z, s.x, i] = total.astype(LOW)
                return carry

            lax.fori_loop(0, 2, add, 0)
            self.next(core, p).start()
        else:
            self.next(core, p).wait_recv()

            def add(i, carry):
                self.sums[slot, i, s.x, s.y] += self.next_in[slot, i]
                return carry

            lax.fori_loop(0, 4, add, 0)
            for k in (1, 3, 2):
                self.hop(core, p, k).start()

    def stage_four(self, core, p):
        s, slot = self.spot, p % SLOTS
        if core == 0:
            self.next(core, p).wait_recv()

            def add(i, carry):
                self.final[slot, i] = self.sums[slot, s.z, s.x, i] + self.next_in[slot, 6 + i]
                return carry

            lax.fori_loop(0, 2, add, 0)
        else:
            for k in (1, 3, 2):
                self.hop(core, p, k).wait_recv()
            total = self.sums[slot, s.z, s.x, s.y].astype(WIDE)
            for k in range(3):
                total += self.next_in[slot, 4 + k].astype(WIDE)
            self.final[slot, s.y] = total.astype(LOW)
            self.last(p, True).start()

    def stage_five(self, core, p):
        if core == 1:
            self.last(p, False).wait_recv()
        for copy in self.results(core, p) + self.kept(core, p):
            copy.start()

    def release(self, core, p):
        self.first(core, p).wait_send()
        for k in (1, 2, 3):
            self.hop(core, p, k).wait_send()
        self.next(core, p).wait_send()
        if core == 1:
            self.last(p, True).wait_send()
        for copy in self.results(core, p):
            copy.wait_send()
        for copy in self.kept(core, p):
            copy.wait()
        if p + SLOTS < len(PARTS):
            s = self.spot
            for i, device in enumerate((s.to_x, s.to_y)):
                pl.semaphore_signal(self.free.at[i], 1, device_id=device, device_id_type=MESH)
            for k in (1, 2, 3):
                pl.semaphore_signal(self.free.at[1 + 4 - k], 1, device_id=s.hop(k), device_id_type=MESH)

    def finish(self, core, p):
        for copy in self.given(core, p):
            copy.wait_send()
        for copy in self.results(1 - core, p):
            copy.wait_recv()

    def program(self):
        count = len(PARTS)
        turns = [[("fetch", 0)]]
        for s in range(count + 6):
            turn = []
            for stage, p in (
                ("stage_one", s),
                ("release", s - 5),
                ("fetch", s + 1),
                ("stage_two", s - 1),
                ("stage_three", s - 2),
                ("stage_four", s - 3),
                ("stage_five", s - 4),
            ):
                if 0 <= p < count:
                    turn.append((stage, p))
            turns.append(turn)
        return turns

    def run(self, steps):
        for core in (0, 1):

            @pl.when(self.spot.core == core)
            def _():
                for stage, p in steps:
                    getattr(self, stage)(core, p)


def norm_backward(grad, i, gain, norms, spreads, small, gradients, gain_row, shift_row):
    unit, inverse = norms[i], spreads[i][:, :1]
    scaled = grad * small[gain : gain + 1]
    gradients[gain_row : gain_row + 1] = jnp.sum(grad * unit, axis=0, keepdims=True)
    gradients[shift_row : shift_row + 1] = jnp.sum(grad, axis=0, keepdims=True)
    centre = jnp.mean(scaled, axis=-1, keepdims=True)
    slope = jnp.mean(scaled * unit, axis=-1, keepdims=True)
    return inverse * (scaled - centre - unit * slope)


def attention_backward(projected, back, context_grad, valid, gradients):
    def pair(i, carry):
        def lanes(at):
            return pl.ds(pl.multiple_of(at * 768 + 128 * i, 128), 128)

        queries, keys, values = (projected[:, lanes(at)] for at in range(3))
        above = context_grad[:, lanes(0)]
        totals = [jnp.zeros((TOKENS, 128), WIDE) for _ in range(3)]
        for which in (0, 1):
            soft = soft_weights(queries, keys, which, valid)
            part = one_head(above, which)
            soft_grad = dot_second(part, values)
            score = soft * (soft_grad - jnp.sum(soft * soft_grad, axis=-1, keepdims=True))
            score = score.astype(LOW)
            totals[0] += dot_plain(score, one_head(keys, which))
            totals[1] += dot_first(score, one_head(queries, which))
            totals[2] += dot_first(soft.astype(LOW), part)
        totals[0] *= 0.125
        totals[1] *= 0.125
        for at in range(3):
            back[:, lanes(at)] = totals[at].astype(LOW)
        gradients[0:1, lanes(0)] = jnp.sum(totals[0], axis=0, keepdims=True)
        gradients[1:2, lanes(0)] = jnp.sum(totals[2], axis=0, keepdims=True)
        return carry

    lax.fori_loop(0, 6, pair, 0)


class Outbox:
    def __init__(self, thin, thick, sems):
        self.thin, self.thick, self.sems = thin, thick, sems
        self.count = 0
        self.flying = {}

    def settle(self, key):
        self.flying.pop(key).wait()

    def settle_all(self):
        for key in list(self.flying):
            self.settle(key)

    def send(self, key, source, target):
        copy = pltpu.make_async_copy(source, target, self.sems.at[key])
        copy.start()
        self.flying[key] = copy

    def room(self):
        key = self.count % THIN
        self.count += 1
        if key in self.flying:
            self.settle(key)
        return key

    def square(self, left, right, target):
        key = self.room()
        for half in (0, 1):
            rows = dot_first(left[:, 384 * half : 384 * half + 384], right).astype(LOW)
            self.thin[key, pl.ds(2 * half, 2)] = rows.reshape(2, 2, 2, 48, 768)
        self.send(key, self.thin.at[key], target)

    def block(self, left, right, target, shape):
        if THIN in self.flying:
            self.settle(THIN)
        rows = shape[0] * shape[1] * shape[2] * shape[3]
        parts = [
            dot_first(left[:, at : at + 384], right).astype(LOW) for at in range(0, rows, 384)
        ]
        self.thick[0 : shape[0], :, :, 0 : shape[3]] = jnp.concatenate(parts, axis=0).reshape(shape)
        self.send(THIN, self.thick.at[0 : shape[0], :, :, 0 : shape[3]], target)


THIN = 2
DENSE_KINDS = tuple(kind for kind in KINDS if kind not in ("CELL", "TABLE"))
SAVED = ("projected", "context", "active", "slope", "joined", "pooled", "norms", "spreads", "small")


def backward_kernel(per_place, *refs):
    weights = dict(zip(DENSE_KINDS, refs[:6]))
    record_in, cell, codes, lengths, hidden, cotangent, valid_keys = refs[6:13]
    saved = dict(zip(SAVED, refs[13:22]))
    outs = refs[22:]
    result = dict(zip(KINDS, outs[:8]))
    hidden_grad, landing = outs[8:10]
    grads = dict(zip(KINDS, outs[10:18]))
    scratch = outs[18:]
    record, state_grad, pool_grad, total, gradients, grad, inner, back, thin, thick = scratch[:10]
    table_part, columns, shuffle = scratch[10:13]
    buffers = scratch[13:18]
    record_sem, weight_sem, outbox_sem, column_sem = scratch[18:22]
    sems = scratch[22:27]
    spot = Spot(per_place)
    norms, spreads, small = saved["norms"], saved["spreads"], saved["small"]

    def weight_copies(kind):
        source = weights[kind]
        if kind == "MERGE":
            pairs = [(source, record.at[pl.ds(14, 6)])]
        elif kind == "FEED":
            pairs = [(source, record.at[pl.ds(8, 6), :, pl.ds(0, 3072)])]
        elif kind == "STREAM":
            pairs = [(source, record.at[pl.ds(8, 6), :, pl.ds(3072, 1536)])]
        elif kind == "OUT":
            pairs = [(source.at[j, :, pl.ds(0, 768)], record.at[0, :, pl.ds(768 * j, 768)]) for j in range(6)]
        else:
            first, count = (4, 4) if kind == "IN" else (1, 3)
            pairs = [(source.at[:, j], record.at[pl.ds(first, count), :, pl.ds(768 * j, 768)]) for j in range(6)]
        at = DENSE_KINDS.index(kind)
        return [pltpu.make_async_copy(a, b, weight_sem.at[at, j]) for j, (a, b) in enumerate(pairs)]

    def need(kind):
        for copy in weight_copies(kind):
            copy.wait()

    def rows_of(slot):
        return jnp.concatenate([record[slot, :, pl.ds(768 * j, 768)] for j in range(6)], axis=0)

    def record_copy(t):
        return pltpu.make_async_copy(record_in.at[t], record.at[t], record_sem.at[t])

    def fill(first, count):
        for t in range(first, first + count):
            record_copy(t).start()

    for kind in ("MERGE", "STREAM", "FEED", "IN", "OUT", "ATT"):
        for copy in weight_copies(kind):
            copy.start()
    spot.greet()
    reduce = Reduce(spot, grads, landing, buffers, result, sems)
    outbox = Outbox(thin, thick, outbox_sem)
    turns = iter(reduce.program())

    def give(*parts):
        outbox.settle_all()
        reduce.run([("give", p) for p in parts])

    def go_on():
        reduce.run(next(turns))

    gradients[...] = jnp.zeros_like(gradients)
    merged = norm_backward(cotangent[...].astype(WIDE), 2, 12, norms, spreads, small, gradients, 12, 9)
    gradients[8:9] = jnp.sum(merged, axis=0, keepdims=True)
    grad[...] = merged
    merged_low = merged.astype(LOW)
    joined = saved["joined"]
    for k in range(3):
        taps = window(joined, k)
        for half in (0, 1):
            lanes = pl.ds(1536 * k + 768 * half, 768)
            outbox.square(merged_low, taps[:, 768 * half : 768 * half + 768], grads["MERGE"].at[..., lanes])
        give(k)
    need("MERGE")
    parts = [
        dot_plain(merged_low, record[pl.ds(14, 6), :, pl.ds(1536 * k, 1536)].reshape(768, 1536)) for k in range(3)
    ]
    joined_grad = parts[1] + shifted(parts[0], False) + shifted(parts[2], True)
    fill(14, 6)
    gradients[6:7] = jnp.sum(joined_grad[:, :768], axis=0, keepdims=True)
    gradients[7:8] = jnp.sum(joined_grad[:, 768:], axis=0, keepdims=True)
    token_low, char_low = joined_grad[:, :768].astype(LOW), joined_grad[:, 768:].astype(LOW)
    second_low = (norms[1] * small[11:12] + small[5:6]).astype(LOW)
    outbox.square(token_low, second_low, grads["STREAM"].at[..., pl.ds(0, 768)])
    outbox.square(char_low, saved["pooled"][...], grads["STREAM"].at[..., pl.ds(768, 768)])
    give(3)
    go_on()
    need("STREAM")
    stream = record[pl.ds(8, 6), :, pl.ds(3072, 1536)].reshape(768, 1536)
    pool_grad[...] = dot_plain(char_low, stream[:, 768:]) / lengths[...].astype(WIDE)
    second_grad = grad[...] + dot_plain(token_low, stream[:, :768])
    two = norm_backward(second_grad, 1, 11, norms, spreads, small, gradients, 11, 5)
    gradients[4:5] = jnp.sum(two, axis=0, keepdims=True)
    grad[...] = two
    two_low = two.astype(LOW)
    for c in range(4):
        outbox.square(two_low, saved["active"][:, 768 * c : 768 * c + 768], grads["FEED"].at[..., pl.ds(768 * c, 768)])
        if c % 2 == 1:
            give(4 + c // 2)
    go_on()
    need("FEED")
    first_low = (norms[0] * small[10:11] + small[3:4]).astype(LOW)
    shuffle[...] = jnp.zeros_like(shuffle)
    for c in range(4):
        lanes = pl.ds(768 * c, 768)
        part = dot_plain(two_low, record[pl.ds(8, 6), :, lanes].reshape(768, 768))
        part = part * saved["slope"][:, lanes].astype(WIDE)
        inner[:, lanes] = part.astype(LOW)
        sums = jnp.sum(part, axis=0, keepdims=True)
        for half in (0, 1):
            at = 768 * c + 384 * half
            done = 0
            while done < 384:
                row, lane = (at + done) // 512, (at + done) % 512
                size = min(512 - lane, 384 - done)
                start = 384 * half + done
                shuffle[row : row + 1, lane : lane + size] = sums[:, start : start + size]
                done += size
        outbox.block(inner[:, lanes], first_low, grads["IN"].at[pl.ds(c, 1)], (1, 2, 2, 192, 768))
    fill(8, 6)
    give(6, 7)
    go_on()
    need("IN")
    first_grad = grad[...]
    for c in range(4):
        first_grad += dot_plain(inner[:, 768 * c : 768 * c + 768], rows_of(4 + c))
    one = norm_backward(first_grad, 0, 10, norms, spreads, small, gradients, 10, 3)
    fill(4, 4)
    gradients[2:3] = jnp.sum(one, axis=0, keepdims=True)
    grad[...] = one
    one_low = one.astype(LOW)
    need("OUT")
    context_grad = dot_plain(one_low, rows_of(0)).astype(LOW)
    inner[:, pl.ds(0, 768)] = context_grad
    attention_backward(saved["projected"], back, inner, key_mask(valid_keys[0]), gradients)
    outbox.square(one_low, saved["context"][...], grads["OUT"].at[..., pl.ds(0, 768)])
    flat = dot_second(shuffle[...].astype(LOW), spread_matrix())
    for c in range(6):
        for j in range(4):
            gradients[13 + j : 14 + j, 128 * c : 128 * c + 128] = flat[c : c + 1, 128 * j : 128 * j + 128]
    columns[:, :, :, :, pl.ds(0, 128)] = jnp.transpose(gradients[...]).astype(LOW).reshape(4, 2, 2, 48, 128)
    columns[:, :, :, :, pl.ds(128, 128)] = jnp.zeros((4, 2, 2, 48, 128), LOW)
    column_copy = pltpu.make_async_copy(columns, grads["OUT"].at[..., pl.ds(768, 256)], column_sem.at[0])
    column_copy.start()
    go_on()
    for i in range(2):
        outbox.block(back[:, pl.ds(1152 * i, 1152)], hidden[...], grads["ATT"].at[pl.ds(2 * i, 2)], (2, 2, 2, 144, 768))
    column_copy.wait()
    give(8, 9)
    need("ATT")
    hidden_back = grad[...]
    for i in range(3):
        hidden_back += dot_plain(back[:, pl.ds(768 * i, 768)], rows_of(1 + i))
    hidden_grad[...] = hidden_back.astype(LOW)
    fill(0, 4)

    state_grad[...] = jnp.zeros_like(state_grad)
    total[...] = jnp.zeros_like(total)
    steps = [step for _ in range(TURNS_IN_LOOP) for step in next(turns)]
    share = -(-len(steps) // CHARS)

    def retreat(i, carry):
        t = CHARS - 1 - i
        record_copy(t).wait()
        gru_backward_step(t, cell, record, state_grad, pool_grad, lengths)
        for k in range(CHARS):
            if steps[k * share : (k + 1) * share]:

                @pl.when(i == k)
                def _():
                    reduce.run(steps[k * share : (k + 1) * share])

        return carry

    lax.fori_loop(0, CHARS, retreat, 0)
    for way in (0, 1):
        outbox.settle_all()
        cell_gradient(way, record, thick)
        outbox.send(THIN, thick.at[:, :, :, 0:144], grads["CELL"].at[pl.ds(2 * way, 2)])
        go_on()

    def look_up(c, carry):
        table_gradient(c, cell, record, codes, total)
        return carry

    lax.fori_loop(0, CHARS, look_up, 0)
    table_part[...] = jnp.transpose(total[...]).astype(LOW).reshape((4, 2, 2) + BLOCKS["TABLE"])
    outbox.send(0, table_part, grads["TABLE"])
    give(10, 11)
    for turn in turns:
        reduce.run(turn)
    reduce.run([("finish", p) for p in range(len(PARTS))])


TURNS_IN_LOOP = 3


def reduce_and_return(whole, saved, record, codes, lengths, hidden, cotangent, valid_keys, per_place):
    in_vmem = pl.BlockSpec(memory_space=pltpu.VMEM)
    anywhere = pl.BlockSpec(memory_space=pl.ANY)
    count = len(PARTS)
    shapes = [jax.ShapeDtypeStruct((2,) + BLOCKS[kind], LOW) for kind in KINDS]
    shapes += [
        jax.ShapeDtypeStruct((TOKENS, 768), LOW),
        jax.ShapeDtypeStruct((count, 4, 2, 2, ROWS, LANES), LOW),
    ]
    shapes += [jax.ShapeDtypeStruct((4, 2, 2) + BLOCKS[kind], LOW) for kind in KINDS]
    views = {
        "ATT": (3, 6, 128, 768),
        "OUT": (6, 128, 1024),
        "IN": (4, 6, 128, 768),
        "FEED": (6, 128, 3072),
        "STREAM": (6, 128, 1536),
        "MERGE": (6, 128, 4608),
    }
    results = pl.pallas_call(
        partial(backward_kernel, per_place),
        out_shape=shapes,
        in_specs=[anywhere] * 7 + [in_vmem] * 5 + [pl.BlockSpec(memory_space=pltpu.SMEM)] + [in_vmem] * len(SAVED),
        out_specs=[anywhere] * 8 + [in_vmem] + [anywhere] * 9,
        scratch_shapes=[
            pltpu.VMEM((CHARS, TOKENS, 2 * RECORD), LOW),
            pltpu.VMEM((TOKENS, 2 * HID), WIDE),
            pltpu.VMEM((TOKENS, 2 * HID), WIDE),
            pltpu.VMEM((1024, EMB), WIDE),
            pltpu.VMEM((128, 768), WIDE),
            pltpu.VMEM((TOKENS, 768), WIDE),
            pltpu.VMEM((TOKENS, 3072), LOW),
            pltpu.VMEM((TOKENS, 2304), LOW),
            pltpu.VMEM((THIN, 4, 2, 2, 48, 768), LOW),
            pltpu.VMEM((2, 2, 2, 192, 768), LOW),
            pltpu.VMEM((4, 2, 2) + BLOCKS["TABLE"], LOW),
            pltpu.VMEM((4, 2, 2, 48, 256), LOW),
            pltpu.VMEM((8, 512), WIDE),
            pltpu.VMEM((SLOTS, 4, 2, 2, ROWS, LANES), LOW),
            pltpu.VMEM((2, 4, 2, 2, ROWS, LANES), LOW),
            pltpu.VMEM((SLOTS, 4, 2, ROWS, LANES), LOW),
            pltpu.VMEM((SLOTS, 8, ROWS, LANES), LOW),
            pltpu.VMEM((SLOTS, 2, ROWS, LANES), LOW),
            pltpu.SemaphoreType.DMA((CHARS,)),
            pltpu.SemaphoreType.DMA((6, 6)),
            pltpu.SemaphoreType.DMA((THIN + 1,)),
            pltpu.SemaphoreType.DMA((1,)),
            pltpu.SemaphoreType.DMA((count, MOVES)),
            pltpu.SemaphoreType.DMA((count, MOVES)),
            pltpu.SemaphoreType.DMA((2, SUBS + 1)),
            pltpu.SemaphoreType.DMA((count, SUBS)),
            pltpu.SemaphoreType.REGULAR((5,)),
        ],
        compiler_params=pltpu.CompilerParams(collective_id=1, has_side_effects=True, vmem_limit_bytes=63 << 20),
    )(
        *[whole[kind].reshape(views[kind]) for kind in DENSE_KINDS],
        record,
        whole["CELL"],
        codes,
        lengths,
        hidden,
        cotangent,
        valid_keys,
        *[saved[name] for name in SAVED],
    )
    return dict(zip(KINDS, results[:8])), results[8]


def unpack(final):
    part = {kind: value.reshape(-1, value.shape[-1]).astype(WIDE) for kind, value in final.items()}
    cell, table, out, stream, merge = (part[kind] for kind in ("CELL", "TABLE", "OUT", "STREAM", "MERGE"))
    small = out[:, 768:785]
    return (
        part["ATT"].T,
        out[:, :768].T,
        part["IN"].T,
        small[:, 13:].reshape(-1),
        part["FEED"].T,
        table[:, :1000].T,
        cell[:, :EMB].T,
        cell[:, EMB : EMB + HID].T,
        cell[:, EMB + HID : EMB + HID + 2].T,
        jnp.stack([stream[:, :768].T, stream[:, 768:].T]),
        jnp.stack([merge[:, k * 1536 : (k + 1) * 1536].T for k in range(3)]),
        small[:, 10:13].T,
        small[:, :10].T,
    )


def shards(hidden, char_codes, word_length, sequence_length, cotangent, *parameters):
    wide = lax.axis_size("wide")
    per_place = wide // 2
    own = pack(parameters, per_place)
    codes = jnp.transpose(char_codes)
    lengths = word_length[:, None]
    whole, record, saved = gather_and_read(own, codes, lengths, hidden, sequence_length, per_place)
    final, hidden_grad = reduce_and_return(
        whole, saved, record, codes, lengths, hidden, cotangent, sequence_length, per_place
    )
    output = saved["output"]
    return (output, hidden_grad, *unpack(final))


def solution(mesh):
    rows = P(("grp", "wide"), None)
    flat = P(("grp", "wide"))
    last = P(None, ("grp", "wide"))
    deep = P(None, None, ("grp", "wide"))
    in_specs = (rows, rows, flat, flat, rows, last, last, last, flat, last, last, last, last, last, deep, deep, last, last)
    out_specs = (rows, rows) + (P(None, "grp"),) * 3 + (P("grp"),) + (P(None, "grp"),) * 5 + (P(None, None, "grp"),) * 2 + (P(None, "grp"),) * 2
    return jax.shard_map(shards, mesh=mesh, in_specs=in_specs, out_specs=out_specs, check_vma=False)
```

```python
from functools import partial

import jax
import jax.numpy as jnp
from jax import lax
from jax.experimental import pallas as pl
from jax.experimental.pallas import tpu as pltpu
from jax.sharding import PartitionSpec as P

HEADS = 12
HID = 384
EMB = 256
CHARS = 20
TOKENS = 128
norm_eps = 1e-05
masked_score = -1e30
MESH = pl.DeviceIdType.MESH
EVERY = slice(None)
LOW = jnp.bfloat16
WIDE = jnp.float32

BLOCKS = {
    "CELL": (144, 768),
    "TABLE": (16, 1024),
    "ATT": (144, 768),
    "OUT": (48, 1024),
    "IN": (192, 768),
    "FEED": (48, 3072),
    "STREAM": (48, 1536),
    "MERGE": (48, 4608),
}
KINDS = tuple(BLOCKS)
PACKED = (("CELL", "ATT"), ("TABLE",), ("OUT", "FEED", "STREAM", "MERGE"), ("IN",))
PIECES = (
    ("CELL", 0, 384, 128, True),
    ("CELL", 128, 512, 256, True),
    ("TABLE", 0, 512, 512, False),
    ("ATT", 0, 384, 384, False),
    ("OUT", 0, 512, 512, True),
    ("IN", 0, 128, 128, False),
    ("IN", 256, 512, 256, False),
    ("FEED", 0, 768, 768, False),
    ("FEED", 1536, 2304, 768, True),
    ("STREAM", 0, 768, 768, False),
    ("MERGE", 0, 768, 768, False),
    ("MERGE", 1536, 2304, 768, True),
    ("MERGE", 3072, 3840, 768, False),
)
GATHER_MOVES = 11
AHEAD = 3
LAGS = (0, 1, 3, 4)

X_WIDTH = 768
RECORD = X_WIDTH + 4 * HID
GATE_R, GATE_Z, GATE_N, GATE_Q = (X_WIDTH + i * HID for i in range(4))


def dot_plain(left_side, right_side):
    return jnp.dot(left_side, right_side, preferred_element_type=WIDE)


def dot_first(left_side, right_side):
    return lax.dot_general(left_side, right_side, (((0,), (0,)), ((), ())), preferred_element_type=WIDE)


def dot_second(left_side, right_side):
    return lax.dot_general(left_side, right_side, (((1,), (1,)), ((), ())), preferred_element_type=WIDE)


def lanes_of(ref, start, width):
    return ref[:, pl.ds(start, width)]


def sigmoid(inputs):
    return 0.5 * jnp.tanh(0.5 * inputs) + 0.5


class Spot:
    def __init__(self, per_place):
        self.grp, self.wide = lax.axis_index("grp"), lax.axis_index("wide")
        self.z, self.x = self.grp // 2, self.grp % 2
        self.y, self.core = self.wide // per_place, self.wide % 2
        self.to_x = (self.grp + 1 - 2 * self.x, self.wide)
        self.to_y = (self.grp, self.wide + per_place - 2 * per_place * self.y)
        self.sibling = (self.grp, self.wide + 1 - 2 * self.core)

    def hop(self, k):
        return (2 * ((self.z + k) % 4) + self.x, self.wide)

    def greet(self):
        barrier = pltpu.get_barrier_semaphore()
        for other in [self.to_x, self.to_y, self.sibling] + [self.hop(k) for k in (1, 2, 3)]:
            pl.semaphore_signal(barrier, 1, device_id=other, device_id_type=MESH)
        pl.semaphore_wait(barrier, 6)

    def near(self, core):
        if core == 0:
            return self.x, self.y, self.to_x, self.to_y
        return self.y, self.x, self.to_y, self.to_x


def remote(source, target, sent, received, device):
    return pltpu.make_async_remote_copy(
        src_ref=source, dst_ref=target, send_sem=sent, recv_sem=received, device_id=device, device_id_type=MESH
    )


class Gather:
    def __init__(self, spot, whole, sems):
        self.spot, self.whole = spot, whole
        self.sent, self.got = sems

    def region(self, core, p, z, f, l):
        kind, first, second, width, _ = PIECES[p]
        lanes = pl.ds((first, second)[core], width)
        return self.whole[kind].at[z, f, l, :, lanes] if core == 0 else self.whole[kind].at[z, l, f, :, lanes]

    def move(self, part, p, j, device, at_sent=None):
        return remote(part, part, self.sent.at[p, j if at_sent is None else at_sent], self.got.at[p, j], device)

    def hop_part(self, core, p, z):
        f, l, _, _ = self.spot.near(core)
        return self.region(core, p, z, f if PIECES[p][4] else EVERY, l)

    def near_part(self, core, p, mine):
        f, l, _, _ = self.spot.near(core)
        return self.region(core, p, EVERY if PIECES[p][4] else self.spot.z, f if mine else 1 - f, l)

    def far_part(self, core, p, mine):
        _, l, _, _ = self.spot.near(core)
        return self.region(core, p, EVERY, EVERY, l if mine else 1 - l)

    def hop(self, core, p, k):
        return self.move(self.hop_part(core, p, self.spot.z), p, k - 1, self.spot.hop(k))

    def hop_in(self, core, p, k):
        return self.move(self.hop_part(core, p, (self.spot.z + 4 - k) % 4), p, k - 1, self.spot.hop(k))

    def relay(self, core, p, z):
        if z == 2:
            return self.move(self.hop_part(core, p, 0), p, 2, self.spot.hop(1), 10)
        return self.move(self.hop_part(core, p, 3), p, 0, self.spot.hop(3), 10)

    def near(self, core, p, mine):
        return self.move(self.near_part(core, p, mine), p, 3, self.spot.near(core)[2])

    def far(self, core, p, mine):
        return self.move(self.far_part(core, p, mine), p, 4, self.spot.near(core)[3])

    def aside(self, core, p, j):
        if j < 3:
            part = self.hop_part(core, p, (self.spot.z + 3 - j) % 4)
        else:
            part = self.near_part(core, p, False) if j == 3 else self.far_part(core, p, False)
        return self.move(part, p, 5 + j, self.spot.sibling)

    def own_hops(self, core, p, act):
        for k, end in ((2, None), (1, 3), (3, 0)):
            if end is None:
                act(self.hop(core, p, k))
            else:

                @pl.when(self.spot.z != end)
                def _():
                    act(self.hop(core, p, k))

    def relays(self, core, p, act):
        for z in (1, 2):

            @pl.when(self.spot.z == z)
            def _():
                act(self.relay(core, p, z))

    def start_hops(self, core, p):
        self.own_hops(core, p, lambda copy: copy.start())

    def take_hops(self, core, p):
        self.hop_in(core, p, 2).wait_recv()
        self.relays(core, p, lambda copy: copy.start())
        for k in (1, 3):
            self.hop_in(core, p, k).wait_recv()

    def start(self, core, p):
        if PIECES[p][4]:
            self.start_hops(core, p)
        else:
            self.near(core, p, True).start()

    def second(self, core, p):
        if PIECES[p][4]:
            self.take_hops(core, p)
            self.near(core, p, True).start()
            for j in (0, 2, 1):
                self.aside(core, p, j).start()
        else:
            self.near(core, p, False).wait_recv()
            self.start_hops(core, p)
            self.aside(core, p, 3).start()

    def third(self, core, p):
        if PIECES[p][4]:
            self.near(core, p, False).wait_recv()
            self.far(core, p, True).start()
            self.aside(core, p, 3).start()
        else:
            self.take_hops(core, p)
            self.far(core, p, True).start()
            for j in (0, 2, 1):
                self.aside(core, p, j).start()

    def fourth(self, core, p):
        self.far(core, p, False).wait_recv()
        self.aside(core, p, 4).start()

    def fifth(self, core, p):
        for j in range(5):
            self.aside(1 - core, p, j).wait_recv()

    def drain(self, core, p):
        self.own_hops(core, p, lambda copy: copy.wait_send())
        self.relays(core, p, lambda copy: copy.wait_send())
        self.near(core, p, True).wait_send()
        self.far(core, p, True).wait_send()
        for j in range(5):
            self.aside(core, p, j).wait_send()

    def turns(self):
        count = len(PIECES)
        turns = []
        for s in range(count + LAGS[-1]):
            ahead = range(AHEAD + 1) if s == 0 else [s + AHEAD]
            turn = [("start", p) for p in ahead if p < count]
            for lag, stage in zip(LAGS, ("second", "third", "fourth", "fifth")):
                if 0 <= s - lag < count:
                    turn.append((stage, s - lag))
            turns.append(turn)
        return turns

    def run(self, steps):
        for core in (0, 1):

            @pl.when(self.spot.core == core)
            def _():
                for stage, p in steps:
                    getattr(self, stage)(core, p)


RING = 4


def gru_forward_step(t, cell, spelled, record, state, total, shifts, lengths):
    slot = t % RING
    for way in (0, 1):
        base = way * RECORD
        place = t if way == 0 else CHARS - 1 - t
        live = lengths[...] > place
        lanes = pl.ds(way * HID, HID)
        h = state[:, lanes]
        record[slot, :, pl.ds(base, EMB)] = spelled[place]
        record[slot, :, pl.ds(base + EMB, HID)] = h.astype(LOW)
        x = record[slot, :, pl.ds(base, X_WIDTH)]
        weights = cell[pl.ds(2 * way, 2)].reshape(3 * HID, X_WIDTH)
        both = dot_second(x, weights[: 2 * HID])
        drive_n = dot_second(x[:, :EMB], weights[2 * HID :, :EMB]) + shifts[way, 0:1]
        recur_n = dot_second(x[:, EMB : EMB + HID], weights[2 * HID :, EMB : EMB + HID]) + shifts[way, 1:2]
        r = sigmoid(both[:, :HID])
        u = sigmoid(both[:, HID:])
        n = jnp.tanh(drive_n + r * recur_n)
        fresh = jnp.where(live, n + u * (h - n), h)
        state[:, lanes] = fresh
        total[:, lanes] += jnp.where(live, fresh, 0.0)
        record[slot, :, pl.ds(base + GATE_R, HID)] = r.astype(LOW)
        record[slot, :, pl.ds(base + GATE_Z, HID)] = u.astype(LOW)
        record[slot, :, pl.ds(base + GATE_N, HID)] = n.astype(LOW)
        record[slot, :, pl.ds(base + GATE_Q, HID)] = recur_n.astype(LOW)


def spread_matrix():
    shape = (512, 512)
    row, lane = lax.broadcasted_iota(jnp.int32, shape, 0), lax.broadcasted_iota(jnp.int32, shape, 1)
    return (4 * (row % 128) + row // 128 == lane).astype(LOW)


def read_small(out, small, feed_row, shuffle):
    columns = out[:, :, :, :, pl.ds(768, 128)].reshape(768, 128).astype(WIDE)
    rows = jnp.transpose(columns)
    small[...] = rows[:32]
    shuffle[...] = jnp.zeros_like(shuffle)
    for c in range(6):
        for j in range(4):
            shuffle[c : c + 1, 128 * j : 128 * j + 128] = rows[13 + j : 14 + j, 128 * c : 128 * c + 128]
    flat = dot_plain(shuffle[...].astype(LOW), spread_matrix())
    for c in range(6):
        feed_row[:, 512 * c : 512 * c + 512] = flat[c : c + 1]


def norm_forward(inputs, i, small, gain, shift, norms, spreads):
    centred = inputs - jnp.mean(inputs, axis=-1, keepdims=True)
    inverse = lax.rsqrt(jnp.mean(centred * centred, axis=-1, keepdims=True) + norm_eps)
    unit = centred * inverse
    norms[i] = unit
    spreads[i] = jnp.broadcast_to(inverse, spreads.shape[1:])
    return unit * small[gain : gain + 1] + small[shift : shift + 1]


def head_mask(which):
    lane = lax.broadcasted_iota(jnp.int32, (TOKENS, 128), 1)
    return (lane < 64) if which == 0 else (lane >= 64)


def one_head(pair, which):
    return jnp.where(head_mask(which), pair, jnp.zeros_like(pair))


def soft_weights(queries, keys, which, valid):
    scores = dot_second(one_head(queries, which), keys) * 0.125 + valid
    weight = jnp.exp(scores - jnp.max(scores, axis=-1, keepdims=True))
    return weight / jnp.sum(weight, axis=-1, keepdims=True)


def key_mask(count):
    lane = lax.broadcasted_iota(jnp.int32, (TOKENS, TOKENS), 1)
    return jnp.where(lane < count, 0.0, masked_score).astype(WIDE)


def attention_forward(projected, context, valid):
    def pair(i, carry):
        def part(at):
            return projected[:, pl.ds(pl.multiple_of(at * 768 + 128 * i, 128), 128)]

        queries, keys, values = part(0), part(1), part(2)
        total = jnp.zeros((TOKENS, 128), WIDE)
        for which in (0, 1):
            soft = soft_weights(queries, keys, which, valid).astype(LOW)
            total += dot_plain(soft, one_head(values, which))
        context[:, pl.ds(pl.multiple_of(128 * i, 128), 128)] = total.astype(LOW)
        return carry

    lax.fori_loop(0, 6, pair, 0)


def shifted(rows, down):
    turned = pltpu.roll(rows, 1 if down else TOKENS - 1, 0)
    row = lax.broadcasted_iota(jnp.int32, rows.shape, 0)
    return jnp.where(row == (0 if down else TOKENS - 1), 0.0, turned)


def window(joined, k):
    if k == 1:
        return joined[...]
    return shifted(joined[...].astype(WIDE), k == 0).astype(LOW)


def forward_kernel(per_place, *refs):
    count = len(KINDS)
    packed = refs[: len(PACKED)]
    codes, lengths, hidden, valid_keys = refs[len(PACKED) : len(PACKED) + 4]
    outs = refs[len(PACKED) + 4 :]
    kept = dict(zip(KINDS, outs[:count]))
    (record_out, output, projected, context, active, slope, joined, pooled_low, norms, spreads, small) = outs[count : count + 11]
    scratch = outs[count + 11 :]
    whole = dict(zip(KINDS, scratch[:count]))
    (record, spelled, state, pooled, shifts, feed_row, shuffle, first, second, merged, sent, got, own_sem, kept_sem, record_sem) = scratch[count:]
    spot = Spot(per_place)
    own_copies = []
    for ref, kinds in zip(packed, PACKED):
        lane = 0
        for kind in kinds:
            source = ref.at[:, pl.ds(lane, BLOCKS[kind][1])]
            own_copies.append(
                pltpu.make_async_copy(source, whole[kind].at[spot.z, spot.x, spot.y], own_sem.at[len(own_copies)])
            )
            lane += BLOCKS[kind][1]
    for copy in own_copies:
        copy.start()
    spot.greet()
    for copy in own_copies:
        copy.wait()
    gather = Gather(spot, whole, (sent, got))
    turns = gather.turns()

    def keep(kind):
        return pltpu.make_async_copy(whole[kind], kept[kind], kept_sem.at[KINDS.index(kind)])

    def weights(kind):
        value = whole[kind][...]
        return value.reshape(-1, value.shape[-1])

    last_of = {kind: max(p for p, piece in enumerate(PIECES) if piece[0] == kind) for kind in KINDS}
    steps = [step for turn in turns for step in turn]

    def after(kind):
        return steps.index(("fifth", last_of[kind])) + 1

    lead = max(after("CELL"), after("TABLE"))
    gather.run(steps[:lead])
    for kind in ("CELL", "TABLE"):
        keep(kind).start()
    cell, table = whole["CELL"], weights("TABLE")

    def embed(c, carry):
        which = (lax.broadcasted_iota(jnp.int32, (1024, TOKENS), 0) == codes[pl.ds(c, 1)]).astype(LOW)
        spelled[c] = jnp.transpose(dot_plain(table, which)).astype(LOW)
        return carry

    lax.fori_loop(0, CHARS, embed, 0)
    pick = (
        lax.broadcasted_iota(jnp.int32, (8, 128), 0) == lax.broadcasted_iota(jnp.int32, (8, 128), 1)
    ).astype(LOW)
    ones = (lax.broadcasted_iota(jnp.int32, (TOKENS, 128), 1) < 2).astype(LOW)
    for way in (0, 1):
        late = cell[pl.ds(2 * way, 2)].reshape(3 * HID, X_WIDTH)[2 * HID :, EMB + HID :]
        shifts[way] = dot_second(pick, late)
        for slot in range(RING):
            record[slot, :, pl.ds(way * RECORD + EMB + HID, 128)] = ones
    state[...] = jnp.zeros_like(state)
    pooled[...] = jnp.zeros_like(pooled)

    def attend():
        for kind in ("ATT", "OUT"):
            keep(kind).start()
        read_small(whole["OUT"], small, feed_row, shuffle)
        attention_in = weights("ATT")
        for i, bias in enumerate((0, None, 1)):
            block = dot_second(hidden[...], attention_in[768 * i : 768 * i + 768])
            if bias is not None:
                block = block + small[bias : bias + 1]
            projected[:, 768 * i : 768 * i + 768] = block.astype(LOW)
        attention_forward(projected, context, key_mask(valid_keys[0]))

    def add_attended():
        attended = dot_second(context[...], weights("OUT")[:, :768]) + small[2:3]
        first[...] = norm_forward(hidden[...].astype(WIDE) + attended, 0, small, 10, 3, norms, spreads)

    def feed(c):
        if c == 0:
            keep("IN").start()
        rows = whole["IN"][c].reshape(768, 768)
        inner = dot_second(first[...].astype(LOW), rows) + feed_row[:, 768 * c : 768 * c + 768]
        share_below = 0.5 * (1.0 + lax.erf(inner * 0.7071067811865476))
        active[:, 768 * c : 768 * c + 768] = (inner * share_below).astype(LOW)
        slope[:, 768 * c : 768 * c + 768] = (
            share_below + inner * (0.3989422804014327 * jnp.exp(-0.5 * inner * inner))
        ).astype(LOW)

    def feed_back():
        keep("FEED").start()
        two = first[...] + dot_second(active[...], weights("FEED")) + small[4:5]
        second[...] = norm_forward(two, 1, small, 11, 5, norms, spreads)

    def token_side():
        stream = whole["STREAM"][:, :, :, :, pl.ds(0, 768)].reshape(768, 768)
        joined[:, :768] = (dot_second(second[...].astype(LOW), stream) + small[6:7]).astype(LOW)

    def record_copy(t):
        return pltpu.make_async_copy(record.at[t % RING], record_out.at[t], record_sem.at[t % RING])

    jobs = [(after("OUT"), attend), (0, add_attended)]
    jobs += [(after("IN"), partial(feed, c)) for c in range(4)]
    jobs += [(after("FEED"), feed_back), (after("STREAM"), token_side)]
    shares = [lead + -(-(GRU_END - lead) * (k + 1) // CHARS) for k in range(CHARS)]
    during = {k: [] for k in range(CHARS)}
    late_jobs = []
    at = 0
    for need, job in jobs:
        ready = [k for k in range(CHARS) if shares[k] >= need]
        at = max([at] + ready[:1]) if ready else CHARS
        if at < CHARS:
            during[at].append(job)
            at += 1
        else:
            late_jobs.append((need, job))

    def advance(t, carry):
        @pl.when(t >= RING)
        def _():
            record_copy(t - RING).wait()

        gru_forward_step(t, cell, spelled, record, state, pooled, shifts, lengths)
        record_copy(t).start()
        for k in range(CHARS):
            part = steps[shares[k - 1] if k else lead : shares[k]]
            if part or during[k]:

                @pl.when(t == k)
                def _():
                    gather.run(part)
                    for job in during[k]:
                        job()

        return carry

    lax.fori_loop(0, CHARS, advance, 0)
    pooled_low[...] = (pooled[...] / lengths[...].astype(WIDE)).astype(LOW)
    done = shares[-1]
    for need, job in late_jobs:
        gather.run(steps[done:need])
        done = max(done, need)
        job()
    gather.run(steps[done : after("STREAM")])
    done = max(done, after("STREAM"))
    keep("STREAM").start()
    stream = whole["STREAM"][:, :, :, :, pl.ds(768, 768)].reshape(768, 768)
    joined[:, 768:] = (dot_second(pooled_low[...], stream) + small[7:8]).astype(LOW)
    taps_at = [p for p, piece in enumerate(PIECES) if piece[0] == "MERGE"]
    for k in range(3):
        until = steps.index(("fifth", taps_at[k])) + 1
        gather.run(steps[done:until])
        done = until
        taps = whole["MERGE"][:, :, :, :, pl.ds(1536 * k, 1536)].reshape(768, 1536)
        part = dot_second(window(joined, k), taps)
        merged[...] = part if k == 0 else merged[...] + part
    keep("MERGE").start()
    third = second[...] + merged[...] + small[8:9]
    output[...] = norm_forward(third, 2, small, 12, 9, norms, spreads).astype(LOW)

    def landed(t, carry):
        record_copy(t).wait()
        return carry

    lax.fori_loop(CHARS - RING, CHARS, landed, 0)
    gather.run([("drain", p) for p in range(len(PIECES))])
    for kind in KINDS:
        keep(kind).wait()


GRU_END = 60


def gather_and_read(packed, codes, lengths, hidden, valid_keys, per_place):
    count = len(KINDS)
    in_vmem = pl.BlockSpec(memory_space=pltpu.VMEM)
    anywhere = pl.BlockSpec(memory_space=pl.ANY)
    whole_shapes = [(4, 2, 2) + BLOCKS[kind] for kind in KINDS]
    saved = {
        "output": ((TOKENS, 768), LOW),
        "projected": ((TOKENS, 2304), LOW),
        "context": ((TOKENS, 768), LOW),
        "active": ((TOKENS, 3072), LOW),
        "slope": ((TOKENS, 3072), LOW),
        "joined": ((TOKENS, 1536), LOW),
        "pooled": ((TOKENS, 768), LOW),
        "norms": ((3, TOKENS, 768), WIDE),
        "spreads": ((3, TOKENS, 128), WIDE),
        "small": ((32, 768), WIDE),
    }
    results = pl.pallas_call(
        partial(forward_kernel, per_place),
        out_shape=[jax.ShapeDtypeStruct(shape, LOW) for shape in whole_shapes]
        + [jax.ShapeDtypeStruct((CHARS, TOKENS, 2 * RECORD), LOW)]
        + [jax.ShapeDtypeStruct(shape, kind) for shape, kind in saved.values()],
        in_specs=[anywhere] * len(PACKED) + [in_vmem] * 3 + [pl.BlockSpec(memory_space=pltpu.SMEM)],
        out_specs=[anywhere] * (count + 1) + [in_vmem] * len(saved),
        scratch_shapes=[pltpu.VMEM(shape, LOW) for shape in whole_shapes]
        + [
            pltpu.VMEM((RING, TOKENS, 2 * RECORD), LOW),
            pltpu.VMEM((CHARS, TOKENS, EMB), LOW),
            pltpu.VMEM((TOKENS, 2 * HID), WIDE),
            pltpu.VMEM((TOKENS, 2 * HID), WIDE),
            pltpu.VMEM((2, 8, HID), WIDE),
            pltpu.VMEM((1, 3072), WIDE),
            pltpu.VMEM((8, 512), WIDE),
            pltpu.VMEM((TOKENS, 768), WIDE),
            pltpu.VMEM((TOKENS, 768), WIDE),
            pltpu.VMEM((TOKENS, 768), WIDE),
            pltpu.SemaphoreType.DMA((len(PIECES), GATHER_MOVES)),
            pltpu.SemaphoreType.DMA((len(PIECES), GATHER_MOVES)),
            pltpu.SemaphoreType.DMA((count,)),
            pltpu.SemaphoreType.DMA((count,)),
            pltpu.SemaphoreType.DMA((RING,)),
        ],
        compiler_params=pltpu.CompilerParams(collective_id=0, has_side_effects=True, vmem_limit_bytes=60 << 20),
    )(*packed, codes, lengths, hidden, valid_keys)
    return dict(zip(KINDS, results[:count])), results[count], dict(zip(saved, results[count + 1 :]))


def pack(shards, per_place):
    (attention_in, attention_out, feed_in, feed_bias, feed_out, char_table, cell_input, cell_recurrent, cell_bias,
     stream_weight, merging_kernel, norm_gains, biases) = shards

    def lanes(parts, width):
        together = jnp.concatenate(parts, axis=1)
        return jnp.pad(together, ((0, 0), (0, width - together.shape[1])))

    def flat(stacked):
        return [jnp.transpose(part) for part in stacked]

    rows = attention_out.shape[1]
    thin = lanes(
        [
            lanes([attention_out.T, biases.T, norm_gains.T, feed_bias.reshape(rows, 4)], 1024),
            feed_out.T,
            *flat(stream_weight),
            *flat(merging_kernel),
        ],
        10240,
    )
    middle = lanes([cell_input.T, cell_recurrent.T, cell_bias.T], 768)
    middle = jnp.concatenate([middle, attention_in.T], axis=1)
    parts = [middle, lanes([char_table.T], 1024), thin, feed_in.T]
    if per_place == 2:
        size = lax.axis_size("wide")
        swap = [(i, i + 1 - 2 * (i % 2)) for i in range(size)]
        first = lax.axis_index("wide") % 2 == 0
        whole = []
        for part in parts:
            other = lax.ppermute(part, "wide", swap)
            whole.append(jnp.concatenate([jnp.where(first, part, other), jnp.where(first, other, part)], axis=0))
    else:
        size = lax.axis_size("wide")
        groups = [list(range(i, i + per_place)) for i in range(0, size, per_place)]
        whole = [lax.all_gather(part, "wide", axis=0, tiled=True, axis_index_groups=groups) for part in parts]
    return whole


def gru_backward_step(t, cell, record, state_grad, pool_grad, lengths):
    for way in (0, 1):
        base = way * RECORD
        place = t if way == 0 else CHARS - 1 - t
        live = lengths[...] > place
        lanes = pl.ds(way * HID, HID)

        def saved(at):
            return record[t, :, pl.ds(base + at, HID)].astype(WIDE)

        r, u, n, recur_n, h = saved(GATE_R), saved(GATE_Z), saved(GATE_N), saved(GATE_Q), saved(EMB)
        grad = state_grad[:, lanes]
        fresh = jnp.where(live, grad + pool_grad[:, lanes], 0.0)
        kept = jnp.where(live, 0.0, grad)
        grad_n = fresh * (1.0 - u) * (1.0 - n * n)
        grad_z = fresh * (h - n) * u * (1.0 - u)
        grad_r = grad_n * recur_n * r * (1.0 - r)
        low_r, low_z, low_n, low_q = (v.astype(LOW) for v in (grad_r, grad_z, grad_n, grad_n * r))
        record[t, :, pl.ds(base + GATE_R, HID)] = low_r
        record[t, :, pl.ds(base + GATE_Z, HID)] = low_z
        record[t, :, pl.ds(base + GATE_N, HID)] = low_n
        record[t, :, pl.ds(base + GATE_Q, HID)] = low_q
        weights = cell[pl.ds(2 * way, 2)].reshape(3 * HID, X_WIDTH)[:, EMB : EMB + HID]
        gates = jnp.concatenate([low_r, low_z, low_q], axis=1)
        state_grad[:, lanes] = kept + fresh * u + dot_plain(gates, weights)


def cell_gradient(way, record, result):
    base = way * RECORD
    rows = CHARS * TOKENS

    def every(at, width):
        return record[:, :, pl.ds(base + at, width)].reshape(rows, width)

    x = every(0, X_WIDTH)
    parts = [dot_first(every(at, HID), x).astype(LOW) for at in (GATE_R, GATE_Z)]
    ends = EMB + HID
    drive, recur = every(GATE_N, HID), every(GATE_Q, HID)
    late = dot_first(recur, x[:, EMB:])
    lane = lax.broadcasted_iota(jnp.int32, (HID, 128), 1)
    shift = jnp.where(lane == 0, dot_first(drive, x[:, ends:]), late[:, HID:])
    parts.append(jnp.concatenate([dot_first(drive, x[:, :EMB]), late[:, :HID], shift], axis=1).astype(LOW))
    result[:, :, :, 0:144] = jnp.concatenate(parts, axis=0).reshape(2, 2, 2, 144, X_WIDTH)


def table_gradient(i, cell, record, codes, result):
    c = 2 * i

    def drive(way, t):
        gates = record[pl.ds(t, 2), :, pl.ds(way * RECORD + GATE_R, 3 * HID)].reshape(2 * TOKENS, 3 * HID)
        return dot_plain(gates, cell[pl.ds(2 * way, 2)].reshape(3 * HID, X_WIDTH)[:, :EMB])

    behind = drive(1, CHARS - 2 - c)
    both = drive(0, c) + jnp.concatenate([behind[TOKENS:], behind[:TOKENS]], axis=0)
    character = lax.broadcasted_iota(jnp.int32, (1024, TOKENS), 0)
    which = [(character == codes[pl.ds(c + k, 1)]).astype(LOW) for k in (0, 1)]
    result[...] += dot_plain(jnp.concatenate(which, axis=1), both.astype(LOW))


ROWS, LANES = 48, 768
PARTS = (
    [("MERGE", 0, 48, 0, 768, 768, 0, 0, True)],
    [("MERGE", 0, 48, 1536, 2304, 768, 0, 0, True)],
    [("MERGE", 0, 48, 3072, 3840, 768, 0, 0, True)],
    [("STREAM", 0, 48, 0, 768, 768, 0, 0, True)],
    [("FEED", 0, 48, 0, 768, 768, 0, 0, True)],
    [("FEED", 0, 48, 1536, 2304, 768, 0, 0, True)],
    [("IN", 0, 48, 0, 384, 384, 0, 0, True), ("IN", 48, 48, 0, 384, 384, 0, 384, True)],
    [("IN", 96, 48, 0, 384, 384, 0, 0, True), ("IN", 144, 48, 0, 384, 384, 0, 384, True)],
    [("ATT", 0, 48, 0, 384, 384, 0, 0, True), ("ATT", 48, 48, 0, 384, 384, 0, 384, True)],
    [("ATT", 96, 48, 0, 384, 384, 0, 0, True), ("OUT", 0, 48, 0, 512, 384, 0, 384, True)],
    [("CELL", 0, 48, 0, 384, 384, 0, 0, True)],
    [("CELL", 48, 48, 0, 384, 384, 0, 0, True)],
    [("CELL", 96, 48, 0, 384, 384, 0, 0, True)],
    [
        ("OUT", 0, 48, 384, 896, 128, 0, 0, True),
        ("TABLE", 0, 16, 0, 512, 256, 0, 128, True),
        ("TABLE", 0, 16, 256, 768, 256, 16, 128, True),
        ("TABLE", 0, 16, 256, 768, 256, 32, 128, False),
    ],
)
WIDTHS = (768,) * 10 + (384,) * 4
SLOTS = 6
SUBS = 4
DENSE_PARTS = 10
AT_FIRST, AT_HOP, AT_NEXT, AT_LAST, AT_RESULT = SUBS, SUBS, SUBS + 4, SUBS + 5, SUBS + 6
MOVES = 2 * SUBS + 6


class Reduce:
    def __init__(self, spot, grads, landing, buffers, result, sems):
        self.spot, self.grads, self.landing, self.result = spot, grads, landing, result
        self.sums, self.other, self.one_in, self.next_in, self.final = buffers
        self.sent, self.got, self.load_sem, self.keep_sem, self.free = sems

    def lanes(self, p):
        return pl.ds(0, WIDTHS[p])

    def move(self, source, target, p, j, device):
        return remote(source, target, self.sent.at[p, j], self.got.at[p, j], device)

    def outside(self, ref, sub, core):
        _, row, rows, first, second, width, _, _, _ = sub
        return ref.at[..., pl.ds(row, rows), pl.ds((first, second)[core], width)]

    def inside(self, ref, sub):
        _, _, rows, _, _, width, row, lane, _ = sub
        return ref.at[..., pl.ds(row, rows), pl.ds(lane, width)]

    def given(self, core, p):
        return [
            self.move(
                self.outside(self.grads[sub[0]], sub, 1 - core), self.inside(self.landing.at[p], sub), p, i, self.spot.sibling
            )
            for i, sub in enumerate(PARTS[p])
        ]

    def loads(self, core, p):
        w = self.lanes(p)
        own = [
            pltpu.make_async_copy(
                self.outside(self.grads[sub[0]], sub, core), self.inside(self.sums.at[p % SLOTS], sub), self.load_sem.at[p % 2, i]
            )
            for i, sub in enumerate(PARTS[p])
        ]
        return own + [pltpu.make_async_copy(self.landing.at[p, ..., w], self.other.at[p % 2, ..., w], self.load_sem.at[p % 2, SUBS])]

    def first(self, core, p):
        s, slot, w = self.spot, p % SLOTS, self.lanes(p)
        if core == 0:
            return self.move(self.sums.at[slot, :, 1 - s.x, :, :, w], self.one_in.at[slot, ..., w], p, AT_FIRST, s.to_x)
        return self.move(self.sums.at[slot, :, :, 1 - s.y, :, w], self.one_in.at[slot, ..., w], p, AT_FIRST, s.to_y)

    def hop(self, core, p, k):
        s, slot, w = self.spot, p % SLOTS, self.lanes(p)
        z = (s.z + k) % 4
        if core == 0:
            return self.move(self.sums.at[slot, z, s.x, :, :, w], self.next_in.at[slot, pl.ds(2 * k - 2, 2), :, w], p, AT_HOP + k, s.hop(k))
        return self.move(self.sums.at[slot, z, s.x, s.y, :, w], self.next_in.at[slot, 3 + k, :, w], p, AT_HOP + k, s.hop(k))

    def next(self, core, p):
        s, slot, w = self.spot, p % SLOTS, self.lanes(p)
        if core == 0:
            return self.move(self.sums.at[slot, s.z, s.x, :, :, w], self.next_in.at[slot, pl.ds(6, 2), :, w], p, AT_NEXT, s.to_y)
        return self.move(self.sums.at[slot, :, 1 - s.x, s.y, :, w], self.next_in.at[slot, pl.ds(0, 4), :, w], p, AT_NEXT, s.to_x)

    def last(self, p, mine):
        s, slot, w = self.spot, p % SLOTS, self.lanes(p)
        part = self.final.at[slot, s.y if mine else 1 - s.y, :, w]
        return self.move(part, part, p, AT_LAST, s.to_y)

    def results(self, core, p):
        return [
            self.move(self.inside(self.final.at[p % SLOTS], sub), self.outside(self.result[sub[0]], sub, core), p, AT_RESULT + i, self.spot.sibling)
            for i, sub in enumerate(PARTS[p])
            if sub[-1]
        ]

    def kept(self, core, p):
        return [
            pltpu.make_async_copy(
                self.inside(self.final.at[p % SLOTS], sub), self.outside(self.result[sub[0]], sub, core), self.keep_sem.at[p, i]
            )
            for i, sub in enumerate(PARTS[p])
            if sub[-1]
        ]

    def give(self, core, p):
        for copy in self.given(core, p):
            copy.start()

    def fetch(self, core, p):
        for copy in self.given(core, p):
            copy.wait_recv()
        for copy in self.loads(core, p):
            copy.start()

    def stage_one(self, core, p):
        for copy in self.loads(core, p):
            copy.wait()
        slot, w = p % SLOTS, self.lanes(p)

        def add(i, carry):
            at = (i // 4, i // 2 % 2, i % 2)
            self.sums[slot, at[0], at[1], at[2], :, w] += self.other[p % 2, at[0], at[1], at[2], :, w]
            return carry

        lax.fori_loop(0, 16, add, 0)
        if p >= SLOTS:
            for i in range(5):
                pl.semaphore_wait(self.free.at[i], 1)
        self.first(core, p).start()

    def stage_two(self, core, p):
        s, slot, w = self.spot, p % SLOTS, self.lanes(p)
        self.first(core, p).wait_recv()

        def add(i, carry):
            if core == 0:
                self.sums[slot, i // 2, s.x, i % 2, :, w] += self.one_in[slot, i // 2, i % 2, :, w]
            else:
                self.sums[slot, i // 2, i % 2, s.y, :, w] += self.one_in[slot, i // 2, i % 2, :, w]
            return carry

        lax.fori_loop(0, 8, add, 0)
        if core == 0:
            for k in (1, 3, 2):
                self.hop(core, p, k).start()
        else:
            self.next(core, p).start()

    def stage_three(self, core, p):
        s, slot, w = self.spot, p % SLOTS, self.lanes(p)
        if core == 0:
            for k in (1, 3, 2):
                self.hop(core, p, k).wait_recv()

            def add(i, carry):
                total = self.sums[slot, s.z, s.x, i, :, w].astype(WIDE)
                for k in range(3):
                    total += self.next_in[slot, 2 * k + i, :, w].astype(WIDE)
                self.sums[slot, s.z, s.x, i, :, w] = total.astype(LOW)
                return carry

            lax.fori_loop(0, 2, add, 0)
            self.next(core, p).start()
        else:
            self.next(core, p).wait_recv()

            def add(i, carry):
                self.sums[slot, i, s.x, s.y, :, w] += self.next_in[slot, i, :, w]
                return carry

            lax.fori_loop(0, 4, add, 0)
            for k in (1, 3, 2):
                self.hop(core, p, k).start()

    def stage_four(self, core, p):
        s, slot, w = self.spot, p % SLOTS, self.lanes(p)
        if core == 0:
            self.next(core, p).wait_recv()

            def add(i, carry):
                self.final[slot, i, :, w] = self.sums[slot, s.z, s.x, i, :, w] + self.next_in[slot, 6 + i, :, w]
                return carry

            lax.fori_loop(0, 2, add, 0)
        else:
            for k in (1, 3, 2):
                self.hop(core, p, k).wait_recv()
            total = self.sums[slot, s.z, s.x, s.y, :, w].astype(WIDE)
            for k in range(3):
                total += self.next_in[slot, 4 + k, :, w].astype(WIDE)
            self.final[slot, s.y, :, w] = total.astype(LOW)
            self.last(p, True).start()

    def stage_five(self, core, p):
        if core == 1:
            self.last(p, False).wait_recv()
        for copy in self.results(core, p) + self.kept(core, p):
            copy.start()

    def release(self, core, p):
        self.first(core, p).wait_send()
        for k in (1, 2, 3):
            self.hop(core, p, k).wait_send()
        self.next(core, p).wait_send()
        if core == 1:
            self.last(p, True).wait_send()
        for copy in self.results(core, p):
            copy.wait_send()
        for copy in self.kept(core, p):
            copy.wait()
        if p + SLOTS < len(PARTS):
            s = self.spot
            for i, device in enumerate((s.to_x, s.to_y)):
                pl.semaphore_signal(self.free.at[i], 1, device_id=device, device_id_type=MESH)
            for k in (1, 2, 3):
                pl.semaphore_signal(self.free.at[1 + 4 - k], 1, device_id=s.hop(k), device_id_type=MESH)

    def finish(self, core, p):
        for copy in self.given(core, p):
            copy.wait_send()
        for copy in self.results(1 - core, p):
            copy.wait_recv()

    def program(self):
        count = len(PARTS)
        turns = [[("fetch", 0)]]
        for s in range(count + 6):
            turn = []
            for stage, p in (
                ("stage_one", s),
                ("release", s - 5),
                ("fetch", s + 1),
                ("stage_two", s - 1),
                ("stage_three", s - 2),
                ("stage_four", s - 3),
                ("stage_five", s - 4),
            ):
                if 0 <= p < count:
                    turn.append((stage, p))
            turns.append(turn)
        return turns

    def run(self, steps):
        for core in (0, 1):

            @pl.when(self.spot.core == core)
            def _():
                for stage, p in steps:
                    getattr(self, stage)(core, p)


def norm_backward(grad, i, gain, norms, spreads, small, gradients, gain_row, shift_row):
    unit, inverse = norms[i], spreads[i][:, :1]
    scaled = grad * small[gain : gain + 1]
    gradients[gain_row : gain_row + 1] = jnp.sum(grad * unit, axis=0, keepdims=True)
    gradients[shift_row : shift_row + 1] = jnp.sum(grad, axis=0, keepdims=True)
    centre = jnp.mean(scaled, axis=-1, keepdims=True)
    slope = jnp.mean(scaled * unit, axis=-1, keepdims=True)
    return inverse * (scaled - centre - unit * slope)


def attention_backward(projected, back, context_grad, valid, gradients):
    def pair(i, carry):
        def lanes(at):
            return pl.ds(pl.multiple_of(at * 768 + 128 * i, 128), 128)

        queries, keys, values = (projected[:, lanes(at)] for at in range(3))
        above = context_grad[:, lanes(0)]
        totals = [jnp.zeros((TOKENS, 128), WIDE) for _ in range(3)]
        for which in (0, 1):
            soft = soft_weights(queries, keys, which, valid)
            part = one_head(above, which)
            soft_grad = dot_second(part, values)
            score = soft * (soft_grad - jnp.sum(soft * soft_grad, axis=-1, keepdims=True))
            score = score.astype(LOW)
            totals[0] += dot_plain(score, one_head(keys, which))
            totals[1] += dot_first(score, one_head(queries, which))
            totals[2] += dot_first(soft.astype(LOW), part)
        totals[0] *= 0.125
        totals[1] *= 0.125
        for at in range(3):
            back[:, lanes(at)] = totals[at].astype(LOW)
        gradients[0:1, lanes(0)] = jnp.sum(totals[0], axis=0, keepdims=True)
        gradients[1:2, lanes(0)] = jnp.sum(totals[2], axis=0, keepdims=True)
        return carry

    lax.fori_loop(0, 6, pair, 0)


class Outbox:
    def __init__(self, thin, thick, sems):
        self.thin, self.thick, self.sems = thin, thick, sems
        self.count = 0
        self.flying = {}

    def settle(self, key):
        self.flying.pop(key).wait()

    def settle_all(self):
        for key in list(self.flying):
            self.settle(key)

    def send(self, key, source, target):
        copy = pltpu.make_async_copy(source, target, self.sems.at[key])
        copy.start()
        self.flying[key] = copy

    def room(self):
        key = self.count % THIN
        self.count += 1
        if key in self.flying:
            self.settle(key)
        return key

    def square(self, left, right, target):
        key = self.room()
        for half in (0, 1):
            rows = dot_first(left[:, 384 * half : 384 * half + 384], right).astype(LOW)
            self.thin[key, pl.ds(2 * half, 2)] = rows.reshape(2, 2, 2, 48, 768)
        self.send(key, self.thin.at[key], target)

    def block(self, left, right, target, shape):
        if THIN in self.flying:
            self.settle(THIN)
        rows = shape[0] * shape[1] * shape[2] * shape[3]
        parts = [
            dot_first(left[:, at : at + 384], right).astype(LOW) for at in range(0, rows, 384)
        ]
        self.thick[0 : shape[0], :, :, 0 : shape[3]] = jnp.concatenate(parts, axis=0).reshape(shape)
        self.send(THIN, self.thick.at[0 : shape[0], :, :, 0 : shape[3]], target)


THIN = 2
DENSE_KINDS = tuple(kind for kind in KINDS if kind not in ("CELL", "TABLE"))
SAVED = ("projected", "context", "active", "slope", "joined", "pooled", "norms", "spreads", "small")


def backward_kernel(per_place, *refs):
    weights = dict(zip(DENSE_KINDS, refs[:6]))
    record_in, cell, codes, lengths, hidden, cotangent, valid_keys = refs[6:13]
    saved = dict(zip(SAVED, refs[13:22]))
    outs = refs[22:]
    result = dict(zip(KINDS, outs[:8]))
    hidden_grad, landing = outs[8:10]
    grads = dict(zip(KINDS, outs[10:18]))
    scratch = outs[18:]
    record, state_grad, pool_grad, total, gradients, grad, inner, back, thin, thick = scratch[:10]
    table_part, columns, shuffle = scratch[10:13]
    buffers = scratch[13:18]
    record_sem, weight_sem, outbox_sem, column_sem = scratch[18:22]
    sems = scratch[22:27]
    spot = Spot(per_place)
    norms, spreads, small = saved["norms"], saved["spreads"], saved["small"]

    def weight_copies(kind):
        source = weights[kind]
        if kind == "MERGE":
            pairs = [(source, record.at[pl.ds(14, 6)])]
        elif kind == "FEED":
            pairs = [(source, record.at[pl.ds(8, 6), :, pl.ds(0, 3072)])]
        elif kind == "STREAM":
            pairs = [(source, record.at[pl.ds(8, 6), :, pl.ds(3072, 1536)])]
        elif kind == "OUT":
            pairs = [(source.at[j, :, pl.ds(0, 768)], record.at[0, :, pl.ds(768 * j, 768)]) for j in range(6)]
        else:
            first, count = (4, 4) if kind == "IN" else (1, 3)
            pairs = [(source.at[:, j], record.at[pl.ds(first, count), :, pl.ds(768 * j, 768)]) for j in range(6)]
        at = DENSE_KINDS.index(kind)
        return [pltpu.make_async_copy(a, b, weight_sem.at[at, j]) for j, (a, b) in enumerate(pairs)]

    def need(kind):
        for copy in weight_copies(kind):
            copy.wait()

    def rows_of(slot):
        return jnp.concatenate([record[slot, :, pl.ds(768 * j, 768)] for j in range(6)], axis=0)

    def record_copy(t):
        return pltpu.make_async_copy(record_in.at[t], record.at[t], record_sem.at[t])

    def fill(first, count):
        for t in range(first, first + count):
            record_copy(t).start()

    for kind in ("MERGE", "STREAM", "FEED", "IN", "OUT", "ATT"):
        for copy in weight_copies(kind):
            copy.start()
    spot.greet()
    reduce = Reduce(spot, grads, landing, buffers, result, sems)
    outbox = Outbox(thin, thick, outbox_sem)
    turns = iter(reduce.program())

    def give(*parts):
        outbox.settle_all()
        reduce.run([("give", p) for p in parts])

    def go_on():
        reduce.run(next(turns))

    gradients[...] = jnp.zeros_like(gradients)
    merged = norm_backward(cotangent[...].astype(WIDE), 2, 12, norms, spreads, small, gradients, 12, 9)
    gradients[8:9] = jnp.sum(merged, axis=0, keepdims=True)
    grad[...] = merged
    merged_low = merged.astype(LOW)
    joined = saved["joined"]
    for k in range(3):
        taps = window(joined, k)
        for half in (0, 1):
            lanes = pl.ds(1536 * k + 768 * half, 768)
            outbox.square(merged_low, taps[:, 768 * half : 768 * half + 768], grads["MERGE"].at[..., lanes])
        give(k)
    need("MERGE")
    parts = [
        dot_plain(merged_low, record[pl.ds(14, 6), :, pl.ds(1536 * k, 1536)].reshape(768, 1536)) for k in range(3)
    ]
    joined_grad = parts[1] + shifted(parts[0], False) + shifted(parts[2], True)
    fill(14, 6)
    gradients[6:7] = jnp.sum(joined_grad[:, :768], axis=0, keepdims=True)
    gradients[7:8] = jnp.sum(joined_grad[:, 768:], axis=0, keepdims=True)
    token_low, char_low = joined_grad[:, :768].astype(LOW), joined_grad[:, 768:].astype(LOW)
    second_low = (norms[1] * small[11:12] + small[5:6]).astype(LOW)
    outbox.square(token_low, second_low, grads["STREAM"].at[..., pl.ds(0, 768)])
    outbox.square(char_low, saved["pooled"][...], grads["STREAM"].at[..., pl.ds(768, 768)])
    give(3)
    go_on()
    need("STREAM")
    stream = record[pl.ds(8, 6), :, pl.ds(3072, 1536)].reshape(768, 1536)
    pool_grad[...] = dot_plain(char_low, stream[:, 768:]) / lengths[...].astype(WIDE)
    second_grad = grad[...] + dot_plain(token_low, stream[:, :768])
    two = norm_backward(second_grad, 1, 11, norms, spreads, small, gradients, 11, 5)
    gradients[4:5] = jnp.sum(two, axis=0, keepdims=True)
    grad[...] = two
    two_low = two.astype(LOW)
    for c in range(4):
        outbox.square(two_low, saved["active"][:, 768 * c : 768 * c + 768], grads["FEED"].at[..., pl.ds(768 * c, 768)])
        if c % 2 == 1:
            give(4 + c // 2)
    go_on()
    need("FEED")
    first_low = (norms[0] * small[10:11] + small[3:4]).astype(LOW)
    shuffle[...] = jnp.zeros_like(shuffle)
    for c in range(4):
        lanes = pl.ds(768 * c, 768)
        part = dot_plain(two_low, record[pl.ds(8, 6), :, lanes].reshape(768, 768))
        part = part * saved["slope"][:, lanes].astype(WIDE)
        inner[:, lanes] = part.astype(LOW)
        sums = jnp.sum(part, axis=0, keepdims=True)
        for half in (0, 1):
            at = 768 * c + 384 * half
            done = 0
            while done < 384:
                row, lane = (at + done) // 512, (at + done) % 512
                size = min(512 - lane, 384 - done)
                start = 384 * half + done
                shuffle[row : row + 1, lane : lane + size] = sums[:, start : start + size]
                done += size
        outbox.block(inner[:, lanes], first_low, grads["IN"].at[pl.ds(c, 1)], (1, 2, 2, 192, 768))
    fill(8, 6)
    give(6, 7)
    go_on()
    need("IN")
    first_grad = grad[...]
    for c in range(4):
        first_grad += dot_plain(inner[:, 768 * c : 768 * c + 768], rows_of(4 + c))
    one = norm_backward(first_grad, 0, 10, norms, spreads, small, gradients, 10, 3)
    fill(4, 4)
    gradients[2:3] = jnp.sum(one, axis=0, keepdims=True)
    grad[...] = one
    one_low = one.astype(LOW)
    need("OUT")
    context_grad = dot_plain(one_low, rows_of(0)).astype(LOW)
    inner[:, pl.ds(0, 768)] = context_grad
    attention_backward(saved["projected"], back, inner, key_mask(valid_keys[0]), gradients)
    outbox.square(one_low, saved["context"][...], grads["OUT"].at[..., pl.ds(0, 768)])
    flat = dot_second(shuffle[...].astype(LOW), spread_matrix())
    for c in range(6):
        for j in range(4):
            gradients[13 + j : 14 + j, 128 * c : 128 * c + 128] = flat[c : c + 1, 128 * j : 128 * j + 128]
    columns[:, :, :, :, pl.ds(0, 128)] = jnp.transpose(gradients[...]).astype(LOW).reshape(4, 2, 2, 48, 128)
    columns[:, :, :, :, pl.ds(128, 128)] = jnp.zeros((4, 2, 2, 48, 128), LOW)
    column_copy = pltpu.make_async_copy(columns, grads["OUT"].at[..., pl.ds(768, 256)], column_sem.at[0])
    column_copy.start()
    go_on()
    for i in range(2):
        outbox.block(back[:, pl.ds(1152 * i, 1152)], hidden[...], grads["ATT"].at[pl.ds(2 * i, 2)], (2, 2, 2, 144, 768))
    column_copy.wait()
    give(8, 9)
    need("ATT")
    hidden_back = grad[...]
    for i in range(3):
        hidden_back += dot_plain(back[:, pl.ds(768 * i, 768)], rows_of(1 + i))
    hidden_grad[...] = hidden_back.astype(LOW)
    fill(0, 4)

    state_grad[...] = jnp.zeros_like(state_grad)
    total[...] = jnp.zeros_like(total)
    steps = [step for _ in range(TURNS_IN_LOOP) for step in next(turns)]
    share = -(-len(steps) // CHARS)

    def retreat(i, carry):
        t = CHARS - 1 - i
        record_copy(t).wait()
        gru_backward_step(t, cell, record, state_grad, pool_grad, lengths)
        for k in range(CHARS):
            if steps[k * share : (k + 1) * share]:

                @pl.when(i == k)
                def _():
                    reduce.run(steps[k * share : (k + 1) * share])

        return carry

    lax.fori_loop(0, CHARS, retreat, 0)
    for way in (0, 1):
        outbox.settle_all()
        cell_gradient(way, record, thick)
        outbox.send(THIN, thick.at[:, :, :, 0:144], grads["CELL"].at[pl.ds(2 * way, 2)])
        if way == 1:
            give(10, 11, 12)
        go_on()

    def look_up(i, carry):
        table_gradient(i, cell, record, codes, total)
        return carry

    lax.fori_loop(0, CHARS // 4, look_up, 0)
    go_on()
    lax.fori_loop(CHARS // 4, CHARS // 2, look_up, 0)
    table_part[...] = jnp.transpose(total[...]).astype(LOW).reshape((4, 2, 2) + BLOCKS["TABLE"])
    outbox.send(0, table_part, grads["TABLE"])
    give(13)
    for turn in turns:
        reduce.run(turn)
    reduce.run([("finish", p) for p in range(len(PARTS))])


TURNS_IN_LOOP = 3


def reduce_and_return(whole, saved, record, codes, lengths, hidden, cotangent, valid_keys, per_place):
    in_vmem = pl.BlockSpec(memory_space=pltpu.VMEM)
    anywhere = pl.BlockSpec(memory_space=pl.ANY)
    count = len(PARTS)
    shapes = [jax.ShapeDtypeStruct((2,) + BLOCKS[kind], LOW) for kind in KINDS]
    shapes += [
        jax.ShapeDtypeStruct((TOKENS, 768), LOW),
        jax.ShapeDtypeStruct((count, 4, 2, 2, ROWS, LANES), LOW),
    ]
    shapes += [jax.ShapeDtypeStruct((4, 2, 2) + BLOCKS[kind], LOW) for kind in KINDS]
    views = {
        "ATT": (3, 6, 128, 768),
        "OUT": (6, 128, 1024),
        "IN": (4, 6, 128, 768),
        "FEED": (6, 128, 3072),
        "STREAM": (6, 128, 1536),
        "MERGE": (6, 128, 4608),
    }
    results = pl.pallas_call(
        partial(backward_kernel, per_place),
        out_shape=shapes,
        in_specs=[anywhere] * 7 + [in_vmem] * 5 + [pl.BlockSpec(memory_space=pltpu.SMEM)] + [in_vmem] * len(SAVED),
        out_specs=[anywhere] * 8 + [in_vmem] + [anywhere] * 9,
        scratch_shapes=[
            pltpu.VMEM((CHARS, TOKENS, 2 * RECORD), LOW),
            pltpu.VMEM((TOKENS, 2 * HID), WIDE),
            pltpu.VMEM((TOKENS, 2 * HID), WIDE),
            pltpu.VMEM((1024, EMB), WIDE),
            pltpu.VMEM((128, 768), WIDE),
            pltpu.VMEM((TOKENS, 768), WIDE),
            pltpu.VMEM((TOKENS, 3072), LOW),
            pltpu.VMEM((TOKENS, 2304), LOW),
            pltpu.VMEM((THIN, 4, 2, 2, 48, 768), LOW),
            pltpu.VMEM((2, 2, 2, 192, 768), LOW),
            pltpu.VMEM((4, 2, 2) + BLOCKS["TABLE"], LOW),
            pltpu.VMEM((4, 2, 2, 48, 256), LOW),
            pltpu.VMEM((8, 512), WIDE),
            pltpu.VMEM((SLOTS, 4, 2, 2, ROWS, LANES), LOW),
            pltpu.VMEM((2, 4, 2, 2, ROWS, LANES), LOW),
            pltpu.VMEM((SLOTS, 4, 2, ROWS, LANES), LOW),
            pltpu.VMEM((SLOTS, 8, ROWS, LANES), LOW),
            pltpu.VMEM((SLOTS, 2, ROWS, LANES), LOW),
            pltpu.SemaphoreType.DMA((CHARS,)),
            pltpu.SemaphoreType.DMA((6, 6)),
            pltpu.SemaphoreType.DMA((THIN + 1,)),
            pltpu.SemaphoreType.DMA((1,)),
            pltpu.SemaphoreType.DMA((count, MOVES)),
            pltpu.SemaphoreType.DMA((count, MOVES)),
            pltpu.SemaphoreType.DMA((2, SUBS + 1)),
            pltpu.SemaphoreType.DMA((count, SUBS)),
            pltpu.SemaphoreType.REGULAR((5,)),
        ],
        compiler_params=pltpu.CompilerParams(collective_id=1, has_side_effects=True, vmem_limit_bytes=63 << 20),
    )(
        *[whole[kind].reshape(views[kind]) for kind in DENSE_KINDS],
        record,
        whole["CELL"],
        codes,
        lengths,
        hidden,
        cotangent,
        valid_keys,
        *[saved[name] for name in SAVED],
    )
    return dict(zip(KINDS, results[:8])), results[8]


def unpack(final):
    part = {kind: value.reshape(-1, value.shape[-1]).astype(WIDE) for kind, value in final.items()}
    cell, table, out, stream, merge = (part[kind] for kind in ("CELL", "TABLE", "OUT", "STREAM", "MERGE"))
    small = out[:, 768:785]
    return (
        part["ATT"].T,
        out[:, :768].T,
        part["IN"].T,
        small[:, 13:].reshape(-1),
        part["FEED"].T,
        table[:, :1000].T,
        cell[:, :EMB].T,
        cell[:, EMB : EMB + HID].T,
        cell[:, EMB + HID : EMB + HID + 2].T,
        jnp.stack([stream[:, :768].T, stream[:, 768:].T]),
        jnp.stack([merge[:, k * 1536 : (k + 1) * 1536].T for k in range(3)]),
        small[:, 10:13].T,
        small[:, :10].T,
    )


def shards(hidden, char_codes, word_length, sequence_length, cotangent, *parameters):
    wide = lax.axis_size("wide")
    per_place = wide // 2
    packed = pack(parameters, per_place)
    codes = jnp.transpose(char_codes)
    lengths = word_length[:, None]
    whole, record, saved = gather_and_read(packed, codes, lengths, hidden, sequence_length, per_place)
    final, hidden_grad = reduce_and_return(
        whole, saved, record, codes, lengths, hidden, cotangent, sequence_length, per_place
    )
    output = saved["output"]
    return (output, hidden_grad, *unpack(final))


def solution(mesh):
    rows = P(("grp", "wide"), None)
    flat = P(("grp", "wide"))
    last = P(None, ("grp", "wide"))
    deep = P(None, None, ("grp", "wide"))
    in_specs = (rows, rows, flat, flat, rows, last, last, last, flat, last, last, last, last, last, deep, deep, last, last)
    out_specs = (rows, rows) + (P(None, "grp"),) * 3 + (P("grp"),) + (P(None, "grp"),) * 5 + (P(None, None, "grp"),) * 2 + (P(None, "grp"),) * 2
    return jax.shard_map(shards, mesh=mesh, in_specs=in_specs, out_specs=out_specs, check_vma=False)
```

```python
from functools import partial

import jax
import jax.numpy as jnp
from jax import lax
from jax.experimental import pallas as pl
from jax.experimental.pallas import tpu as pltpu
from jax.sharding import PartitionSpec as P

HEADS = 12
HID = 384
EMB = 256
CHARS = 20
TOKENS = 128
norm_eps = 1e-05
masked_score = -1e30
MESH = pl.DeviceIdType.MESH
EVERY = slice(None)
LOW = jnp.bfloat16
WIDE = jnp.float32

BLOCKS = {
    "CELL": (144, 768),
    "TABLE": (16, 1024),
    "ATT": (144, 768),
    "OUT": (48, 1024),
    "IN": (192, 768),
    "FEED": (48, 3072),
    "STREAM": (48, 1536),
    "MERGE": (48, 4608),
}
KINDS = tuple(BLOCKS)
STARTS = (
    ("CELL", 0, 256, 1),
    ("CELL", 256, 384, 1),
    ("CELL", 640, 128, 1),
    ("TABLE", 0, 1000, 1),
    ("ATT", 0, 768, 1),
    ("OUT", 0, 768, 1),
    ("OUT", 768, 128, 1),
    ("IN", 0, 768, 1),
    ("FEED", 0, 3072, 1),
    ("STREAM", 0, 768, 2),
    ("MERGE", 0, 1536, 3),
)
PIECES = (
    ("CELL", 0, 384, 128, True),
    ("CELL", 128, 512, 256, True),
    ("TABLE", 0, 512, 512, False),
    ("ATT", 0, 384, 384, False),
    ("OUT", 0, 512, 512, True),
    ("IN", 0, 128, 128, False),
    ("IN", 256, 512, 256, False),
    ("FEED", 0, 768, 768, False),
    ("FEED", 1536, 2304, 768, True),
    ("STREAM", 0, 768, 768, False),
    ("MERGE", 0, 768, 768, False),
    ("MERGE", 1536, 2304, 768, True),
    ("MERGE", 3072, 3840, 768, False),
)
GATHER_MOVES = 11
AHEAD = 3
LAGS = (0, 1, 3, 4)

X_WIDTH = 768
RECORD = X_WIDTH + 4 * HID
GATE_R, GATE_Z, GATE_N, GATE_Q = (X_WIDTH + i * HID for i in range(4))


def dot_plain(left_side, right_side):
    return jnp.dot(left_side, right_side, preferred_element_type=WIDE)


def dot_first(left_side, right_side):
    return lax.dot_general(left_side, right_side, (((0,), (0,)), ((), ())), preferred_element_type=WIDE)


def dot_second(left_side, right_side):
    return lax.dot_general(left_side, right_side, (((1,), (1,)), ((), ())), preferred_element_type=WIDE)


def lanes_of(ref, start, width):
    return ref[:, pl.ds(start, width)]


def sigmoid(inputs):
    return 0.5 * jnp.tanh(0.5 * inputs) + 0.5


class Spot:
    def __init__(self, per_place):
        self.grp, self.wide = lax.axis_index("grp"), lax.axis_index("wide")
        self.z, self.x = self.grp // 2, self.grp % 2
        self.y, self.core = self.wide // per_place, self.wide % 2
        self.to_x = (self.grp + 1 - 2 * self.x, self.wide)
        self.to_y = (self.grp, self.wide + per_place - 2 * per_place * self.y)
        self.sibling = (self.grp, self.wide + 1 - 2 * self.core)

    def hop(self, k):
        return (2 * ((self.z + k) % 4) + self.x, self.wide)

    def greet(self):
        barrier = pltpu.get_barrier_semaphore()
        for other in [self.to_x, self.to_y, self.sibling] + [self.hop(k) for k in (1, 2, 3)]:
            pl.semaphore_signal(barrier, 1, device_id=other, device_id_type=MESH)
        pl.semaphore_wait(barrier, 6)

    def near(self, core):
        if core == 0:
            return self.x, self.y, self.to_x, self.to_y
        return self.y, self.x, self.to_y, self.to_x


def remote(source, target, sent, received, device):
    return pltpu.make_async_remote_copy(
        src_ref=source, dst_ref=target, send_sem=sent, recv_sem=received, device_id=device, device_id_type=MESH
    )


class Gather:
    def __init__(self, spot, whole, sems):
        self.spot, self.whole = spot, whole
        self.sent, self.got = sems

    def region(self, core, p, z, f, l):
        kind, first, second, width, _ = PIECES[p]
        lanes = pl.ds((first, second)[core], width)
        return self.whole[kind].at[z, f, l, :, lanes] if core == 0 else self.whole[kind].at[z, l, f, :, lanes]

    def move(self, part, p, j, device, at_sent=None):
        return remote(part, part, self.sent.at[p, j if at_sent is None else at_sent], self.got.at[p, j], device)

    def hop_part(self, core, p, z):
        f, l, _, _ = self.spot.near(core)
        return self.region(core, p, z, f if PIECES[p][4] else EVERY, l)

    def near_part(self, core, p, mine):
        f, l, _, _ = self.spot.near(core)
        return self.region(core, p, EVERY if PIECES[p][4] else self.spot.z, f if mine else 1 - f, l)

    def far_part(self, core, p, mine):
        _, l, _, _ = self.spot.near(core)
        return self.region(core, p, EVERY, EVERY, l if mine else 1 - l)

    def hop(self, core, p, k):
        return self.move(self.hop_part(core, p, self.spot.z), p, k - 1, self.spot.hop(k))

    def hop_in(self, core, p, k):
        return self.move(self.hop_part(core, p, (self.spot.z + 4 - k) % 4), p, k - 1, self.spot.hop(k))

    def relay(self, core, p, z):
        if z == 2:
            return self.move(self.hop_part(core, p, 0), p, 2, self.spot.hop(1), 10)
        return self.move(self.hop_part(core, p, 3), p, 0, self.spot.hop(3), 10)

    def near(self, core, p, mine):
        return self.move(self.near_part(core, p, mine), p, 3, self.spot.near(core)[2])

    def far(self, core, p, mine):
        return self.move(self.far_part(core, p, mine), p, 4, self.spot.near(core)[3])

    def aside(self, core, p, j):
        if j < 3:
            part = self.hop_part(core, p, (self.spot.z + 3 - j) % 4)
        else:
            part = self.near_part(core, p, False) if j == 3 else self.far_part(core, p, False)
        return self.move(part, p, 5 + j, self.spot.sibling)

    def own_hops(self, core, p, act):
        for k, end in ((2, None), (1, 3), (3, 0)):
            if end is None:
                act(self.hop(core, p, k))
            else:

                @pl.when(self.spot.z != end)
                def _():
                    act(self.hop(core, p, k))

    def relays(self, core, p, act):
        for z in (1, 2):

            @pl.when(self.spot.z == z)
            def _():
                act(self.relay(core, p, z))

    def start_hops(self, core, p):
        self.own_hops(core, p, lambda copy: copy.start())

    def take_hops(self, core, p):
        self.hop_in(core, p, 2).wait_recv()
        self.relays(core, p, lambda copy: copy.start())
        for k in (1, 3):
            self.hop_in(core, p, k).wait_recv()

    def start(self, core, p):
        if PIECES[p][4]:
            self.start_hops(core, p)
        else:
            self.near(core, p, True).start()

    def second(self, core, p):
        if PIECES[p][4]:
            self.take_hops(core, p)
            self.near(core, p, True).start()
            for j in (0, 2, 1):
                self.aside(core, p, j).start()
        else:
            self.near(core, p, False).wait_recv()
            self.start_hops(core, p)
            self.aside(core, p, 3).start()

    def third(self, core, p):
        if PIECES[p][4]:
            self.near(core, p, False).wait_recv()
            self.far(core, p, True).start()
            self.aside(core, p, 3).start()
        else:
            self.take_hops(core, p)
            self.far(core, p, True).start()
            for j in (0, 2, 1):
                self.aside(core, p, j).start()

    def fourth(self, core, p):
        self.far(core, p, False).wait_recv()
        self.aside(core, p, 4).start()

    def fifth(self, core, p):
        for j in range(5):
            self.aside(1 - core, p, j).wait_recv()

    def drain(self, core, p):
        self.own_hops(core, p, lambda copy: copy.wait_send())
        self.relays(core, p, lambda copy: copy.wait_send())
        self.near(core, p, True).wait_send()
        self.far(core, p, True).wait_send()
        for j in range(5):
            self.aside(core, p, j).wait_send()

    def turns(self):
        count = len(PIECES)
        turns = []
        for s in range(count + LAGS[-1]):
            ahead = range(AHEAD + 1) if s == 0 else [s + AHEAD]
            turn = [("start", p) for p in ahead if p < count]
            for lag, stage in zip(LAGS, ("second", "third", "fourth", "fifth")):
                if 0 <= s - lag < count:
                    turn.append((stage, s - lag))
            turns.append(turn)
        return turns

    def run(self, steps):
        for core in (0, 1):

            @pl.when(self.spot.core == core)
            def _():
                for stage, p in steps:
                    getattr(self, stage)(core, p)


RING = 4


def gru_forward_step(t, cell, spelled, record, state, total, shifts, lengths):
    slot = t % RING
    for way in (0, 1):
        base = way * RECORD
        place = t if way == 0 else CHARS - 1 - t
        live = lengths[...] > place
        lanes = pl.ds(way * HID, HID)
        h = state[:, lanes]
        record[slot, :, pl.ds(base, EMB)] = spelled[place]
        record[slot, :, pl.ds(base + EMB, HID)] = h.astype(LOW)
        x = record[slot, :, pl.ds(base, X_WIDTH)]
        weights = cell[pl.ds(2 * way, 2)].reshape(3 * HID, X_WIDTH)
        both = dot_second(x, weights[: 2 * HID])
        drive_n = dot_second(x[:, :EMB], weights[2 * HID :, :EMB]) + shifts[way, 0:1]
        recur_n = dot_second(x[:, EMB : EMB + HID], weights[2 * HID :, EMB : EMB + HID]) + shifts[way, 1:2]
        r = sigmoid(both[:, :HID])
        u = sigmoid(both[:, HID:])
        n = jnp.tanh(drive_n + r * recur_n)
        fresh = jnp.where(live, n + u * (h - n), h)
        state[:, lanes] = fresh
        total[:, lanes] += jnp.where(live, fresh, 0.0)
        record[slot, :, pl.ds(base + GATE_R, HID)] = r.astype(LOW)
        record[slot, :, pl.ds(base + GATE_Z, HID)] = u.astype(LOW)
        record[slot, :, pl.ds(base + GATE_N, HID)] = n.astype(LOW)
        record[slot, :, pl.ds(base + GATE_Q, HID)] = recur_n.astype(LOW)


def spread_matrix():
    shape = (512, 512)
    row, lane = lax.broadcasted_iota(jnp.int32, shape, 0), lax.broadcasted_iota(jnp.int32, shape, 1)
    return (4 * (row % 128) + row // 128 == lane).astype(LOW)


def read_small(out, small, feed_row, shuffle):
    columns = out[:, :, :, :, pl.ds(768, 128)].reshape(768, 128).astype(WIDE)
    rows = jnp.transpose(columns)
    small[...] = rows[:32]
    shuffle[...] = jnp.zeros_like(shuffle)
    for c in range(6):
        for j in range(4):
            shuffle[c : c + 1, 128 * j : 128 * j + 128] = rows[13 + j : 14 + j, 128 * c : 128 * c + 128]
    flat = dot_plain(shuffle[...].astype(LOW), spread_matrix())
    for c in range(6):
        feed_row[:, 512 * c : 512 * c + 512] = flat[c : c + 1]


def norm_forward(inputs, i, small, gain, shift, norms, spreads):
    centred = inputs - jnp.mean(inputs, axis=-1, keepdims=True)
    inverse = lax.rsqrt(jnp.mean(centred * centred, axis=-1, keepdims=True) + norm_eps)
    unit = centred * inverse
    norms[i] = unit
    spreads[i] = jnp.broadcast_to(inverse, spreads.shape[1:])
    return unit * small[gain : gain + 1] + small[shift : shift + 1]


def head_mask(which):
    lane = lax.broadcasted_iota(jnp.int32, (TOKENS, 128), 1)
    return (lane < 64) if which == 0 else (lane >= 64)


def one_head(pair, which):
    return jnp.where(head_mask(which), pair, jnp.zeros_like(pair))


def soft_weights(queries, keys, which, valid):
    scores = dot_second(one_head(queries, which), keys) * 0.125 + valid
    weight = jnp.exp(scores - jnp.max(scores, axis=-1, keepdims=True))
    return weight / jnp.sum(weight, axis=-1, keepdims=True)


def key_mask(count):
    lane = lax.broadcasted_iota(jnp.int32, (TOKENS, TOKENS), 1)
    return jnp.where(lane < count, 0.0, masked_score).astype(WIDE)


def attention_forward(projected, context, valid):
    def pair(i, carry):
        def part(at):
            return projected[:, pl.ds(pl.multiple_of(at * 768 + 128 * i, 128), 128)]

        queries, keys, values = part(0), part(1), part(2)
        total = jnp.zeros((TOKENS, 128), WIDE)
        for which in (0, 1):
            soft = soft_weights(queries, keys, which, valid).astype(LOW)
            total += dot_plain(soft, one_head(values, which))
        context[:, pl.ds(pl.multiple_of(128 * i, 128), 128)] = total.astype(LOW)
        return carry

    lax.fori_loop(0, 6, pair, 0)


def shifted(rows, down):
    turned = pltpu.roll(rows, 1 if down else TOKENS - 1, 0)
    row = lax.broadcasted_iota(jnp.int32, rows.shape, 0)
    return jnp.where(row == (0 if down else TOKENS - 1), 0.0, turned)


def window(joined, k):
    if k == 1:
        return joined[...]
    return shifted(joined[...].astype(WIDE), k == 0).astype(LOW)


def forward_kernel(per_place, *refs):
    count = len(KINDS)
    starts = refs[: len(STARTS)]
    codes, lengths, hidden, valid_keys = refs[len(STARTS) : len(STARTS) + 4]
    outs = refs[len(STARTS) + 4 :]
    kept = dict(zip(KINDS, outs[:count]))
    (record_out, output, projected, context, active, slope, joined, pooled_low, norms, spreads, small) = outs[count : count + 11]
    scratch = outs[count + 11 :]
    whole = dict(zip(KINDS, scratch[:count]))
    (record, spelled, state, pooled, shifts, feed_row, shuffle, first, second, merged, sent, got, own_sent, own_got, kept_sem, record_sem) = scratch[count : count + 16]
    mine, theirs = (dict(zip(KINDS, scratch[at : at + count])) for at in (count + 16, 2 * count + 16))
    spot = Spot(per_place)
    halves = per_place == 2

    def lay(kind):
        if kind in ("TABLE", "OUT"):
            mine[kind][...] = jnp.zeros_like(mine[kind])
        for ref, (owner, first, width, parts) in zip(starts, STARTS):
            if owner != kind:
                continue
            for part in range(parts):
                rows = ref[...] if parts == 1 else ref[part]
                lanes = pl.ds(first + part * width, width)
                if not halves:
                    mine[kind][:, lanes] = rows
                    continue
                rows = rows.astype(WIDE)
                blank = jnp.zeros_like(rows)
                low = jnp.where(spot.core == 0, rows, blank)
                high = jnp.where(spot.core == 0, blank, rows)
                mine[kind][:, lanes] = jnp.concatenate([low, high], axis=0).astype(LOW)

    def swap(kind):
        at = KINDS.index(kind)
        return remote(mine[kind], theirs[kind], own_sent.at[at], own_got.at[at], spot.sibling)

    def ready(kind):
        if halves:
            swap(kind).wait_recv()
            whole[kind][spot.z, spot.x, spot.y] = mine[kind][...] + theirs[kind][...]
        else:
            whole[kind][spot.z, spot.x, spot.y] = mine[kind][...]

    def lay_and_swap(kinds):
        for kind in kinds:
            lay(kind)
            if halves:
                swap(kind).start()

    spot.greet()
    lay_and_swap(KINDS[:3])
    gather = Gather(spot, whole, (sent, got))
    turns = gather.turns()

    def keep(kind):
        return pltpu.make_async_copy(whole[kind], kept[kind], kept_sem.at[KINDS.index(kind)])

    def weights(kind):
        value = whole[kind][...]
        return value.reshape(-1, value.shape[-1])

    last_of = {kind: max(p for p, piece in enumerate(PIECES) if piece[0] == kind) for kind in KINDS}
    steps = [step for turn in turns for step in turn]

    def after(kind):
        return steps.index(("fifth", last_of[kind])) + 1

    lead = max(after("CELL"), after("TABLE"))
    waiting = list(KINDS)
    for stage, p in steps[:lead]:
        if stage == "start" and PIECES[p][0] in waiting:
            ready(PIECES[p][0])
            waiting.remove(PIECES[p][0])
        gather.run([(stage, p)])
        if (stage, p) == ("start", 3):
            lay_and_swap(KINDS[3:])
    for kind in waiting:
        ready(kind)
    for kind in ("CELL", "TABLE"):
        keep(kind).start()
    cell, table = whole["CELL"], weights("TABLE")

    def embed(c, carry):
        which = (lax.broadcasted_iota(jnp.int32, (1024, TOKENS), 0) == codes[pl.ds(c, 1)]).astype(LOW)
        spelled[c] = jnp.transpose(dot_plain(table, which)).astype(LOW)
        return carry

    lax.fori_loop(0, CHARS, embed, 0)
    pick = (
        lax.broadcasted_iota(jnp.int32, (8, 128), 0) == lax.broadcasted_iota(jnp.int32, (8, 128), 1)
    ).astype(LOW)
    ones = (lax.broadcasted_iota(jnp.int32, (TOKENS, 128), 1) < 2).astype(LOW)
    for way in (0, 1):
        late = cell[pl.ds(2 * way, 2)].reshape(3 * HID, X_WIDTH)[2 * HID :, EMB + HID :]
        shifts[way] = dot_second(pick, late)
        for slot in range(RING):
            record[slot, :, pl.ds(way * RECORD + EMB + HID, 128)] = ones
    state[...] = jnp.zeros_like(state)
    pooled[...] = jnp.zeros_like(pooled)

    def attend():
        for kind in ("ATT", "OUT"):
            keep(kind).start()
        read_small(whole["OUT"], small, feed_row, shuffle)
        attention_in = weights("ATT")
        for i, bias in enumerate((0, None, 1)):
            block = dot_second(hidden[...], attention_in[768 * i : 768 * i + 768])
            if bias is not None:
                block = block + small[bias : bias + 1]
            projected[:, 768 * i : 768 * i + 768] = block.astype(LOW)
        attention_forward(projected, context, key_mask(valid_keys[0]))

    def add_attended():
        attended = dot_second(context[...], weights("OUT")[:, :768]) + small[2:3]
        first[...] = norm_forward(hidden[...].astype(WIDE) + attended, 0, small, 10, 3, norms, spreads)

    def feed(c):
        if c == 0:
            keep("IN").start()
        rows = whole["IN"][c].reshape(768, 768)
        inner = dot_second(first[...].astype(LOW), rows) + feed_row[:, 768 * c : 768 * c + 768]
        share_below = 0.5 * (1.0 + lax.erf(inner * 0.7071067811865476))
        active[:, 768 * c : 768 * c + 768] = (inner * share_below).astype(LOW)
        slope[:, 768 * c : 768 * c + 768] = (
            share_below + inner * (0.3989422804014327 * jnp.exp(-0.5 * inner * inner))
        ).astype(LOW)

    def feed_back():
        keep("FEED").start()
        two = first[...] + dot_second(active[...], weights("FEED")) + small[4:5]
        second[...] = norm_forward(two, 1, small, 11, 5, norms, spreads)

    def token_side():
        stream = whole["STREAM"][:, :, :, :, pl.ds(0, 768)].reshape(768, 768)
        joined[:, :768] = (dot_second(second[...].astype(LOW), stream) + small[6:7]).astype(LOW)

    def record_copy(t):
        return pltpu.make_async_copy(record.at[t % RING], record_out.at[t], record_sem.at[t % RING])

    jobs = [(after("OUT"), attend), (0, add_attended)]
    jobs += [(after("IN"), partial(feed, c)) for c in range(4)]
    jobs += [(after("FEED"), feed_back), (after("STREAM"), token_side)]
    shares = [lead + -(-(GRU_END - lead) * (k + 1) // CHARS) for k in range(CHARS)]
    during = {k: [] for k in range(CHARS)}
    late_jobs = []
    at = 0
    for need, job in jobs:
        ready = [k for k in range(CHARS) if shares[k] >= need]
        at = max([at] + ready[:1]) if ready else CHARS
        if at < CHARS:
            during[at].append(job)
            at += 1
        else:
            late_jobs.append((need, job))

    def advance(t, carry):
        @pl.when(t >= RING)
        def _():
            record_copy(t - RING).wait()

        gru_forward_step(t, cell, spelled, record, state, pooled, shifts, lengths)
        record_copy(t).start()
        for k in range(CHARS):
            part = steps[shares[k - 1] if k else lead : shares[k]]
            if part or during[k]:

                @pl.when(t == k)
                def _():
                    gather.run(part)
                    for job in during[k]:
                        job()

        return carry

    lax.fori_loop(0, CHARS, advance, 0)
    pooled_low[...] = (pooled[...] / lengths[...].astype(WIDE)).astype(LOW)
    done = shares[-1]
    for need, job in late_jobs:
        gather.run(steps[done:need])
        done = max(done, need)
        job()
    gather.run(steps[done : after("STREAM")])
    done = max(done, after("STREAM"))
    keep("STREAM").start()
    stream = whole["STREAM"][:, :, :, :, pl.ds(768, 768)].reshape(768, 768)
    joined[:, 768:] = (dot_second(pooled_low[...], stream) + small[7:8]).astype(LOW)
    taps_at = [p for p, piece in enumerate(PIECES) if piece[0] == "MERGE"]
    for k in range(3):
        until = steps.index(("fifth", taps_at[k])) + 1
        gather.run(steps[done:until])
        done = until
        taps = whole["MERGE"][:, :, :, :, pl.ds(1536 * k, 1536)].reshape(768, 1536)
        part = dot_second(window(joined, k), taps)
        merged[...] = part if k == 0 else merged[...] + part
    keep("MERGE").start()
    third = second[...] + merged[...] + small[8:9]
    output[...] = norm_forward(third, 2, small, 12, 9, norms, spreads).astype(LOW)

    def landed(t, carry):
        record_copy(t).wait()
        return carry

    lax.fori_loop(CHARS - RING, CHARS, landed, 0)
    gather.run([("drain", p) for p in range(len(PIECES))])
    for kind in KINDS:
        keep(kind).wait()
        if halves:
            swap(kind).wait_send()


GRU_END = 60


def gather_and_read(starts, codes, lengths, hidden, valid_keys, per_place):
    count = len(KINDS)
    in_vmem = pl.BlockSpec(memory_space=pltpu.VMEM)
    anywhere = pl.BlockSpec(memory_space=pl.ANY)
    whole_shapes = [(4, 2, 2) + BLOCKS[kind] for kind in KINDS]
    saved = {
        "output": ((TOKENS, 768), LOW),
        "projected": ((TOKENS, 2304), LOW),
        "context": ((TOKENS, 768), LOW),
        "active": ((TOKENS, 3072), LOW),
        "slope": ((TOKENS, 3072), LOW),
        "joined": ((TOKENS, 1536), LOW),
        "pooled": ((TOKENS, 768), LOW),
        "norms": ((3, TOKENS, 768), WIDE),
        "spreads": ((3, TOKENS, 128), WIDE),
        "small": ((32, 768), WIDE),
    }
    results = pl.pallas_call(
        partial(forward_kernel, per_place),
        out_shape=[jax.ShapeDtypeStruct(shape, LOW) for shape in whole_shapes]
        + [jax.ShapeDtypeStruct((CHARS, TOKENS, 2 * RECORD), LOW)]
        + [jax.ShapeDtypeStruct(shape, kind) for shape, kind in saved.values()],
        in_specs=[in_vmem] * (len(STARTS) + 3) + [pl.BlockSpec(memory_space=pltpu.SMEM)],
        out_specs=[anywhere] * (count + 1) + [in_vmem] * len(saved),
        scratch_shapes=[pltpu.VMEM(shape, LOW) for shape in whole_shapes]
        + [
            pltpu.VMEM((RING, TOKENS, 2 * RECORD), LOW),
            pltpu.VMEM((CHARS, TOKENS, EMB), LOW),
            pltpu.VMEM((TOKENS, 2 * HID), WIDE),
            pltpu.VMEM((TOKENS, 2 * HID), WIDE),
            pltpu.VMEM((2, 8, HID), WIDE),
            pltpu.VMEM((1, 3072), WIDE),
            pltpu.VMEM((8, 512), WIDE),
            pltpu.VMEM((TOKENS, 768), WIDE),
            pltpu.VMEM((TOKENS, 768), WIDE),
            pltpu.VMEM((TOKENS, 768), WIDE),
            pltpu.SemaphoreType.DMA((len(PIECES), GATHER_MOVES)),
            pltpu.SemaphoreType.DMA((len(PIECES), GATHER_MOVES)),
            pltpu.SemaphoreType.DMA((count,)),
            pltpu.SemaphoreType.DMA((count,)),
            pltpu.SemaphoreType.DMA((count,)),
            pltpu.SemaphoreType.DMA((RING,)),
        ]
        + [pltpu.VMEM(BLOCKS[kind], LOW) for kind in KINDS + KINDS],
        compiler_params=pltpu.CompilerParams(collective_id=0, has_side_effects=True, vmem_limit_bytes=60 << 20),
    )(*starts, codes, lengths, hidden, valid_keys)
    return dict(zip(KINDS, results[:count])), results[count], dict(zip(saved, results[count + 1 :]))


def pack(shards, per_place):
    (attention_in, attention_out, feed_in, feed_bias, feed_out, char_table, cell_input, cell_recurrent, cell_bias,
     stream_weight, merging_kernel, norm_gains, biases) = shards

    def lanes(parts, width):
        together = jnp.concatenate(parts, axis=1)
        return jnp.pad(together, ((0, 0), (0, width - together.shape[1])))

    rows = attention_out.shape[1]
    starts = [
        cell_input.T,
        cell_recurrent.T,
        lanes([cell_bias.T], 128),
        char_table.T,
        attention_in.T,
        attention_out.T,
        lanes([biases.T, norm_gains.T, feed_bias.reshape(rows, 4)], 128),
        feed_in.T,
        feed_out.T,
        jnp.swapaxes(stream_weight, 1, 2),
        jnp.swapaxes(merging_kernel, 1, 2),
    ]
    if per_place == 2:
        return starts
    size = lax.axis_size("wide")
    groups = [list(range(i, i + per_place)) for i in range(0, size, per_place)]
    return [
        lax.all_gather(part, "wide", axis=part.ndim - 2, tiled=True, axis_index_groups=groups) for part in starts
    ]


def gru_backward_step(t, cell, record, state_grad, pool_grad, lengths):
    for way in (0, 1):
        base = way * RECORD
        place = t if way == 0 else CHARS - 1 - t
        live = lengths[...] > place
        lanes = pl.ds(way * HID, HID)

        def saved(at):
            return record[t, :, pl.ds(base + at, HID)].astype(WIDE)

        r, u, n, recur_n, h = saved(GATE_R), saved(GATE_Z), saved(GATE_N), saved(GATE_Q), saved(EMB)
        grad = state_grad[:, lanes]
        fresh = jnp.where(live, grad + pool_grad[:, lanes], 0.0)
        kept = jnp.where(live, 0.0, grad)
        grad_n = fresh * (1.0 - u) * (1.0 - n * n)
        grad_z = fresh * (h - n) * u * (1.0 - u)
        grad_r = grad_n * recur_n * r * (1.0 - r)
        low_r, low_z, low_n, low_q = (v.astype(LOW) for v in (grad_r, grad_z, grad_n, grad_n * r))
        record[t, :, pl.ds(base + GATE_R, HID)] = low_r
        record[t, :, pl.ds(base + GATE_Z, HID)] = low_z
        record[t, :, pl.ds(base + GATE_N, HID)] = low_n
        record[t, :, pl.ds(base + GATE_Q, HID)] = low_q
        weights = cell[pl.ds(2 * way, 2)].reshape(3 * HID, X_WIDTH)[:, EMB : EMB + HID]
        gates = jnp.concatenate([low_r, low_z, low_q], axis=1)
        state_grad[:, lanes] = kept + fresh * u + dot_plain(gates, weights)


def cell_gradient(way, record, result):
    base = way * RECORD
    rows = CHARS * TOKENS

    def every(at, width):
        return record[:, :, pl.ds(base + at, width)].reshape(rows, width)

    x = every(0, X_WIDTH)
    parts = [dot_first(every(at, HID), x).astype(LOW) for at in (GATE_R, GATE_Z)]
    ends = EMB + HID
    drive, recur = every(GATE_N, HID), every(GATE_Q, HID)
    late = dot_first(recur, x[:, EMB:])
    lane = lax.broadcasted_iota(jnp.int32, (HID, 128), 1)
    shift = jnp.where(lane == 0, dot_first(drive, x[:, ends:]), late[:, HID:])
    parts.append(jnp.concatenate([dot_first(drive, x[:, :EMB]), late[:, :HID], shift], axis=1).astype(LOW))
    result[:, :, :, 0:144] = jnp.concatenate(parts, axis=0).reshape(2, 2, 2, 144, X_WIDTH)


def table_gradient(i, cell, record, codes, result):
    c = 2 * i

    def drive(way, t):
        gates = record[pl.ds(t, 2), :, pl.ds(way * RECORD + GATE_R, 3 * HID)].reshape(2 * TOKENS, 3 * HID)
        return dot_plain(gates, cell[pl.ds(2 * way, 2)].reshape(3 * HID, X_WIDTH)[:, :EMB])

    behind = drive(1, CHARS - 2 - c)
    both = drive(0, c) + jnp.concatenate([behind[TOKENS:], behind[:TOKENS]], axis=0)
    character = lax.broadcasted_iota(jnp.int32, (1024, TOKENS), 0)
    which = [(character == codes[pl.ds(c + k, 1)]).astype(LOW) for k in (0, 1)]
    result[...] += dot_plain(jnp.concatenate(which, axis=1), both.astype(LOW))


ROWS, LANES = 48, 768
PARTS = (
    [("MERGE", 0, 48, 0, 768, 768, 0, 0, True)],
    [("MERGE", 0, 48, 1536, 2304, 768, 0, 0, True)],
    [("MERGE", 0, 48, 3072, 3840, 768, 0, 0, True)],
    [("STREAM", 0, 48, 0, 768, 768, 0, 0, True)],
    [("FEED", 0, 48, 0, 768, 768, 0, 0, True)],
    [("FEED", 0, 48, 1536, 2304, 768, 0, 0, True)],
    [("IN", 0, 48, 0, 384, 384, 0, 0, True), ("IN", 48, 48, 0, 384, 384, 0, 384, True)],
    [("IN", 96, 48, 0, 384, 384, 0, 0, True), ("IN", 144, 48, 0, 384, 384, 0, 384, True)],
    [("ATT", 0, 48, 0, 384, 384, 0, 0, True), ("ATT", 48, 48, 0, 384, 384, 0, 384, True)],
    [("ATT", 96, 48, 0, 384, 384, 0, 0, True), ("OUT", 0, 48, 0, 512, 384, 0, 384, True)],
    [("CELL", 0, 48, 0, 384, 384, 0, 0, True)],
    [("CELL", 48, 48, 0, 384, 384, 0, 0, True)],
    [("CELL", 96, 48, 0, 384, 384, 0, 0, True)],
    [
        ("OUT", 0, 48, 384, 896, 128, 0, 0, True),
        ("TABLE", 0, 16, 0, 512, 256, 0, 128, True),
        ("TABLE", 0, 16, 256, 768, 256, 16, 128, True),
        ("TABLE", 0, 16, 256, 768, 256, 32, 128, False),
    ],
)
WIDTHS = (768,) * 10 + (384,) * 4
SLOTS = 6
SUBS = 4
DENSE_PARTS = 10
AT_FIRST, AT_HOP, AT_NEXT, AT_LAST, AT_RESULT = SUBS, SUBS, SUBS + 4, SUBS + 5, SUBS + 6
MOVES = 2 * SUBS + 6


class Reduce:
    def __init__(self, spot, grads, landing, buffers, result, sems):
        self.spot, self.grads, self.landing, self.result = spot, grads, landing, result
        self.sums, self.other, self.one_in, self.next_in, self.final = buffers
        self.sent, self.got, self.load_sem, self.keep_sem, self.free = sems

    def lanes(self, p):
        return pl.ds(0, WIDTHS[p])

    def move(self, source, target, p, j, device):
        return remote(source, target, self.sent.at[p, j], self.got.at[p, j], device)

    def outside(self, ref, sub, core):
        _, row, rows, first, second, width, _, _, _ = sub
        return ref.at[..., pl.ds(row, rows), pl.ds((first, second)[core], width)]

    def inside(self, ref, sub):
        _, _, rows, _, _, width, row, lane, _ = sub
        return ref.at[..., pl.ds(row, rows), pl.ds(lane, width)]

    def given(self, core, p):
        return [
            self.move(
                self.outside(self.grads[sub[0]], sub, 1 - core), self.inside(self.landing.at[p], sub), p, i, self.spot.sibling
            )
            for i, sub in enumerate(PARTS[p])
        ]

    def loads(self, core, p):
        w = self.lanes(p)
        own = [
            pltpu.make_async_copy(
                self.outside(self.grads[sub[0]], sub, core), self.inside(self.sums.at[p % SLOTS], sub), self.load_sem.at[p % 2, i]
            )
            for i, sub in enumerate(PARTS[p])
        ]
        return own + [pltpu.make_async_copy(self.landing.at[p, ..., w], self.other.at[p % 2, ..., w], self.load_sem.at[p % 2, SUBS])]

    def first(self, core, p):
        s, slot, w = self.spot, p % SLOTS, self.lanes(p)
        if core == 0:
            return self.move(self.sums.at[slot, :, 1 - s.x, :, :, w], self.one_in.at[slot, ..., w], p, AT_FIRST, s.to_x)
        return self.move(self.sums.at[slot, :, :, 1 - s.y, :, w], self.one_in.at[slot, ..., w], p, AT_FIRST, s.to_y)

    def hop(self, core, p, k):
        s, slot, w = self.spot, p % SLOTS, self.lanes(p)
        z = (s.z + k) % 4
        if core == 0:
            return self.move(self.sums.at[slot, z, s.x, :, :, w], self.next_in.at[slot, pl.ds(2 * k - 2, 2), :, w], p, AT_HOP + k, s.hop(k))
        return self.move(self.sums.at[slot, z, s.x, s.y, :, w], self.next_in.at[slot, 3 + k, :, w], p, AT_HOP + k, s.hop(k))

    def next(self, core, p):
        s, slot, w = self.spot, p % SLOTS, self.lanes(p)
        if core == 0:
            return self.move(self.sums.at[slot, s.z, s.x, :, :, w], self.next_in.at[slot, pl.ds(6, 2), :, w], p, AT_NEXT, s.to_y)
        return self.move(self.sums.at[slot, :, 1 - s.x, s.y, :, w], self.next_in.at[slot, pl.ds(0, 4), :, w], p, AT_NEXT, s.to_x)

    def last(self, p, mine):
        s, slot, w = self.spot, p % SLOTS, self.lanes(p)
        part = self.final.at[slot, s.y if mine else 1 - s.y, :, w]
        return self.move(part, part, p, AT_LAST, s.to_y)

    def results(self, core, p):
        return [
            self.move(self.inside(self.final.at[p % SLOTS], sub), self.outside(self.result[sub[0]], sub, core), p, AT_RESULT + i, self.spot.sibling)
            for i, sub in enumerate(PARTS[p])
            if sub[-1]
        ]

    def kept(self, core, p):
        return [
            pltpu.make_async_copy(
                self.inside(self.final.at[p % SLOTS], sub), self.outside(self.result[sub[0]], sub, core), self.keep_sem.at[p, i]
            )
            for i, sub in enumerate(PARTS[p])
            if sub[-1]
        ]

    def give(self, core, p):
        for copy in self.given(core, p):
            copy.start()

    def fetch(self, core, p):
        for copy in self.given(core, p):
            copy.wait_recv()
        for copy in self.loads(core, p):
            copy.start()

    def stage_one(self, core, p):
        for copy in self.loads(core, p):
            copy.wait()
        slot, w = p % SLOTS, self.lanes(p)

        def add(i, carry):
            at = (i // 4, i // 2 % 2, i % 2)
            self.sums[slot, at[0], at[1], at[2], :, w] += self.other[p % 2, at[0], at[1], at[2], :, w]
            return carry

        lax.fori_loop(0, 16, add, 0)
        if p >= SLOTS:
            for i in range(5):
                pl.semaphore_wait(self.free.at[i], 1)
        self.first(core, p).start()

    def stage_two(self, core, p):
        s, slot, w = self.spot, p % SLOTS, self.lanes(p)
        self.first(core, p).wait_recv()

        def add(i, carry):
            if core == 0:
                self.sums[slot, i // 2, s.x, i % 2, :, w] += self.one_in[slot, i // 2, i % 2, :, w]
            else:
                self.sums[slot, i // 2, i % 2, s.y, :, w] += self.one_in[slot, i // 2, i % 2, :, w]
            return carry

        lax.fori_loop(0, 8, add, 0)
        if core == 0:
            for k in (1, 3, 2):
                self.hop(core, p, k).start()
        else:
            self.next(core, p).start()

    def stage_three(self, core, p):
        s, slot, w = self.spot, p % SLOTS, self.lanes(p)
        if core == 0:
            for k in (1, 3, 2):
                self.hop(core, p, k).wait_recv()

            def add(i, carry):
                total = self.sums[slot, s.z, s.x, i, :, w].astype(WIDE)
                for k in range(3):
                    total += self.next_in[slot, 2 * k + i, :, w].astype(WIDE)
                self.sums[slot, s.z, s.x, i, :, w] = total.astype(LOW)
                return carry

            lax.fori_loop(0, 2, add, 0)
            self.next(core, p).start()
        else:
            self.next(core, p).wait_recv()

            def add(i, carry):
                self.sums[slot, i, s.x, s.y, :, w] += self.next_in[slot, i, :, w]
                return carry

            lax.fori_loop(0, 4, add, 0)
            for k in (1, 3, 2):
                self.hop(core, p, k).start()

    def stage_four(self, core, p):
        s, slot, w = self.spot, p % SLOTS, self.lanes(p)
        if core == 0:
            self.next(core, p).wait_recv()

            def add(i, carry):
                self.final[slot, i, :, w] = self.sums[slot, s.z, s.x, i, :, w] + self.next_in[slot, 6 + i, :, w]
                return carry

            lax.fori_loop(0, 2, add, 0)
        else:
            for k in (1, 3, 2):
                self.hop(core, p, k).wait_recv()
            total = self.sums[slot, s.z, s.x, s.y, :, w].astype(WIDE)
            for k in range(3):
                total += self.next_in[slot, 4 + k, :, w].astype(WIDE)
            self.final[slot, s.y, :, w] = total.astype(LOW)
            self.last(p, True).start()

    def stage_five(self, core, p):
        if core == 1:
            self.last(p, False).wait_recv()
        for copy in self.results(core, p) + self.kept(core, p):
            copy.start()

    def release(self, core, p):
        self.first(core, p).wait_send()
        for k in (1, 2, 3):
            self.hop(core, p, k).wait_send()
        self.next(core, p).wait_send()
        if core == 1:
            self.last(p, True).wait_send()
        for copy in self.results(core, p):
            copy.wait_send()
        for copy in self.kept(core, p):
            copy.wait()
        if p + SLOTS < len(PARTS):
            s = self.spot
            for i, device in enumerate((s.to_x, s.to_y)):
                pl.semaphore_signal(self.free.at[i], 1, device_id=device, device_id_type=MESH)
            for k in (1, 2, 3):
                pl.semaphore_signal(self.free.at[1 + 4 - k], 1, device_id=s.hop(k), device_id_type=MESH)

    def finish(self, core, p):
        for copy in self.given(core, p):
            copy.wait_send()
        for copy in self.results(1 - core, p):
            copy.wait_recv()

    def program(self):
        count = len(PARTS)
        turns = [[("fetch", 0)]]
        for s in range(count + 6):
            turn = []
            for stage, p in (
                ("stage_one", s),
                ("release", s - 5),
                ("fetch", s + 1),
                ("stage_two", s - 1),
                ("stage_three", s - 2),
                ("stage_four", s - 3),
                ("stage_five", s - 4),
            ):
                if 0 <= p < count:
                    turn.append((stage, p))
            turns.append(turn)
        return turns

    def run(self, steps):
        for core in (0, 1):

            @pl.when(self.spot.core == core)
            def _():
                for stage, p in steps:
                    getattr(self, stage)(core, p)


def norm_backward(grad, i, gain, norms, spreads, small, gradients, gain_row, shift_row):
    unit, inverse = norms[i], spreads[i][:, :1]
    scaled = grad * small[gain : gain + 1]
    gradients[gain_row : gain_row + 1] = jnp.sum(grad * unit, axis=0, keepdims=True)
    gradients[shift_row : shift_row + 1] = jnp.sum(grad, axis=0, keepdims=True)
    centre = jnp.mean(scaled, axis=-1, keepdims=True)
    slope = jnp.mean(scaled * unit, axis=-1, keepdims=True)
    return inverse * (scaled - centre - unit * slope)


def attention_backward(projected, back, context_grad, valid, gradients):
    def pair(i, carry):
        def lanes(at):
            return pl.ds(pl.multiple_of(at * 768 + 128 * i, 128), 128)

        queries, keys, values = (projected[:, lanes(at)] for at in range(3))
        above = context_grad[:, lanes(0)]
        totals = [jnp.zeros((TOKENS, 128), WIDE) for _ in range(3)]
        for which in (0, 1):
            soft = soft_weights(queries, keys, which, valid)
            part = one_head(above, which)
            soft_grad = dot_second(part, values)
            score = soft * (soft_grad - jnp.sum(soft * soft_grad, axis=-1, keepdims=True))
            score = score.astype(LOW)
            totals[0] += dot_plain(score, one_head(keys, which))
            totals[1] += dot_first(score, one_head(queries, which))
            totals[2] += dot_first(soft.astype(LOW), part)
        totals[0] *= 0.125
        totals[1] *= 0.125
        for at in range(3):
            back[:, lanes(at)] = totals[at].astype(LOW)
        gradients[0:1, lanes(0)] = jnp.sum(totals[0], axis=0, keepdims=True)
        gradients[1:2, lanes(0)] = jnp.sum(totals[2], axis=0, keepdims=True)
        return carry

    lax.fori_loop(0, 6, pair, 0)


class Outbox:
    def __init__(self, thin, thick, sems):
        self.thin, self.thick, self.sems = thin, thick, sems
        self.count = 0
        self.flying = {}

    def settle(self, key):
        self.flying.pop(key).wait()

    def settle_all(self):
        for key in list(self.flying):
            self.settle(key)

    def send(self, key, source, target):
        copy = pltpu.make_async_copy(source, target, self.sems.at[key])
        copy.start()
        self.flying[key] = copy

    def room(self):
        key = self.count % THIN
        self.count += 1
        if key in self.flying:
            self.settle(key)
        return key

    def square(self, left, right, target):
        key = self.room()
        for half in (0, 1):
            rows = dot_first(left[:, 384 * half : 384 * half + 384], right).astype(LOW)
            self.thin[key, pl.ds(2 * half, 2)] = rows.reshape(2, 2, 2, 48, 768)
        self.send(key, self.thin.at[key], target)

    def block(self, left, right, target, shape):
        if THIN in self.flying:
            self.settle(THIN)
        rows = shape[0] * shape[1] * shape[2] * shape[3]
        parts = [
            dot_first(left[:, at : at + 384], right).astype(LOW) for at in range(0, rows, 384)
        ]
        self.thick[0 : shape[0], :, :, 0 : shape[3]] = jnp.concatenate(parts, axis=0).reshape(shape)
        self.send(THIN, self.thick.at[0 : shape[0], :, :, 0 : shape[3]], target)


THIN = 2
DENSE_KINDS = tuple(kind for kind in KINDS if kind not in ("CELL", "TABLE"))
SAVED = ("projected", "context", "active", "slope", "joined", "pooled", "norms", "spreads", "small")


def backward_kernel(per_place, *refs):
    weights = dict(zip(DENSE_KINDS, refs[:6]))
    record_in, cell, codes, lengths, hidden, cotangent, valid_keys = refs[6:13]
    saved = dict(zip(SAVED, refs[13:22]))
    outs = refs[22:]
    result = dict(zip(KINDS, outs[:8]))
    hidden_grad, landing = outs[8:10]
    grads = dict(zip(KINDS, outs[10:18]))
    scratch = outs[18:]
    record, state_grad, pool_grad, total, gradients, grad, inner, back, thin, thick = scratch[:10]
    table_part, columns, shuffle = scratch[10:13]
    buffers = scratch[13:18]
    record_sem, weight_sem, outbox_sem, column_sem = scratch[18:22]
    sems = scratch[22:27]
    spot = Spot(per_place)
    norms, spreads, small = saved["norms"], saved["spreads"], saved["small"]

    def weight_copies(kind):
        source = weights[kind]
        if kind == "MERGE":
            pairs = [(source, record.at[pl.ds(14, 6)])]
        elif kind == "FEED":
            pairs = [(source, record.at[pl.ds(8, 6), :, pl.ds(0, 3072)])]
        elif kind == "STREAM":
            pairs = [(source, record.at[pl.ds(8, 6), :, pl.ds(3072, 1536)])]
        elif kind == "OUT":
            pairs = [(source.at[j, :, pl.ds(0, 768)], record.at[0, :, pl.ds(768 * j, 768)]) for j in range(6)]
        else:
            first, count = (4, 4) if kind == "IN" else (1, 3)
            pairs = [(source.at[:, j], record.at[pl.ds(first, count), :, pl.ds(768 * j, 768)]) for j in range(6)]
        at = DENSE_KINDS.index(kind)
        return [pltpu.make_async_copy(a, b, weight_sem.at[at, j]) for j, (a, b) in enumerate(pairs)]

    def need(kind):
        for copy in weight_copies(kind):
            copy.wait()

    def rows_of(slot):
        return jnp.concatenate([record[slot, :, pl.ds(768 * j, 768)] for j in range(6)], axis=0)

    def record_copy(t):
        return pltpu.make_async_copy(record_in.at[t], record.at[t], record_sem.at[t])

    def fill(first, count):
        for t in range(first, first + count):
            record_copy(t).start()

    for kind in ("MERGE", "STREAM", "FEED", "IN", "OUT", "ATT"):
        for copy in weight_copies(kind):
            copy.start()
    spot.greet()
    reduce = Reduce(spot, grads, landing, buffers, result, sems)
    outbox = Outbox(thin, thick, outbox_sem)
    steps = [step for turn in reduce.program() for step in turn]
    given = set()

    def give(*parts):
        outbox.settle_all()
        reduce.run([("give", p) for p in parts])
        given.update(parts)

    def take(count):
        taken = []
        while steps and len(taken) < count and not (steps[0][0] == "fetch" and steps[0][1] not in given):
            taken.append(steps.pop(0))
        return taken

    def go_on(count):
        reduce.run(take(count))

    gradients[...] = jnp.zeros_like(gradients)
    merged = norm_backward(cotangent[...].astype(WIDE), 2, 12, norms, spreads, small, gradients, 12, 9)
    gradients[8:9] = jnp.sum(merged, axis=0, keepdims=True)
    grad[...] = merged
    merged_low = merged.astype(LOW)
    joined = saved["joined"]
    for k in range(3):
        taps = window(joined, k)
        for half in (0, 1):
            lanes = pl.ds(1536 * k + 768 * half, 768)
            outbox.square(merged_low, taps[:, 768 * half : 768 * half + 768], grads["MERGE"].at[..., lanes])
        give(k)
        if k > 0:
            go_on(PACE[0])
    need("MERGE")
    parts = [
        dot_plain(merged_low, record[pl.ds(14, 6), :, pl.ds(1536 * k, 1536)].reshape(768, 1536)) for k in range(3)
    ]
    joined_grad = parts[1] + shifted(parts[0], False) + shifted(parts[2], True)
    fill(14, 6)
    go_on(PACE[1])
    gradients[6:7] = jnp.sum(joined_grad[:, :768], axis=0, keepdims=True)
    gradients[7:8] = jnp.sum(joined_grad[:, 768:], axis=0, keepdims=True)
    token_low, char_low = joined_grad[:, :768].astype(LOW), joined_grad[:, 768:].astype(LOW)
    second_low = (norms[1] * small[11:12] + small[5:6]).astype(LOW)
    outbox.square(token_low, second_low, grads["STREAM"].at[..., pl.ds(0, 768)])
    outbox.square(char_low, saved["pooled"][...], grads["STREAM"].at[..., pl.ds(768, 768)])
    give(3)
    need("STREAM")
    stream = record[pl.ds(8, 6), :, pl.ds(3072, 1536)].reshape(768, 1536)
    pool_grad[...] = dot_plain(char_low, stream[:, 768:]) / lengths[...].astype(WIDE)
    second_grad = grad[...] + dot_plain(token_low, stream[:, :768])
    two = norm_backward(second_grad, 1, 11, norms, spreads, small, gradients, 11, 5)
    gradients[4:5] = jnp.sum(two, axis=0, keepdims=True)
    grad[...] = two
    two_low = two.astype(LOW)
    for c in range(4):
        outbox.square(two_low, saved["active"][:, 768 * c : 768 * c + 768], grads["FEED"].at[..., pl.ds(768 * c, 768)])
        if c % 2 == 1:
            give(4 + c // 2)
            go_on(PACE[2])
    need("FEED")
    first_low = (norms[0] * small[10:11] + small[3:4]).astype(LOW)
    shuffle[...] = jnp.zeros_like(shuffle)
    for c in range(4):
        lanes = pl.ds(768 * c, 768)
        part = dot_plain(two_low, record[pl.ds(8, 6), :, lanes].reshape(768, 768))
        part = part * saved["slope"][:, lanes].astype(WIDE)
        inner[:, lanes] = part.astype(LOW)
        sums = jnp.sum(part, axis=0, keepdims=True)
        for half in (0, 1):
            at = 768 * c + 384 * half
            done = 0
            while done < 384:
                row, lane = (at + done) // 512, (at + done) % 512
                size = min(512 - lane, 384 - done)
                start = 384 * half + done
                shuffle[row : row + 1, lane : lane + size] = sums[:, start : start + size]
                done += size
        outbox.block(inner[:, lanes], first_low, grads["IN"].at[pl.ds(c, 1)], (1, 2, 2, 192, 768))
        go_on(PACE[3])
    fill(8, 6)
    give(6, 7)
    need("IN")
    first_grad = grad[...]
    for c in range(4):
        first_grad += dot_plain(inner[:, 768 * c : 768 * c + 768], rows_of(4 + c))
    one = norm_backward(first_grad, 0, 10, norms, spreads, small, gradients, 10, 3)
    fill(4, 4)
    go_on(PACE[4])
    gradients[2:3] = jnp.sum(one, axis=0, keepdims=True)
    grad[...] = one
    one_low = one.astype(LOW)
    need("OUT")
    context_grad = dot_plain(one_low, rows_of(0)).astype(LOW)
    inner[:, pl.ds(0, 768)] = context_grad
    attention_backward(saved["projected"], back, inner, key_mask(valid_keys[0]), gradients)
    go_on(PACE[5])
    outbox.square(one_low, saved["context"][...], grads["OUT"].at[..., pl.ds(0, 768)])
    flat = dot_second(shuffle[...].astype(LOW), spread_matrix())
    for c in range(6):
        for j in range(4):
            gradients[13 + j : 14 + j, 128 * c : 128 * c + 128] = flat[c : c + 1, 128 * j : 128 * j + 128]
    columns[:, :, :, :, pl.ds(0, 128)] = jnp.transpose(gradients[...]).astype(LOW).reshape(4, 2, 2, 48, 128)
    columns[:, :, :, :, pl.ds(128, 128)] = jnp.zeros((4, 2, 2, 48, 128), LOW)
    column_copy = pltpu.make_async_copy(columns, grads["OUT"].at[..., pl.ds(768, 256)], column_sem.at[0])
    column_copy.start()
    for i in range(2):
        outbox.block(back[:, pl.ds(1152 * i, 1152)], hidden[...], grads["ATT"].at[pl.ds(2 * i, 2)], (2, 2, 2, 144, 768))
        go_on(PACE[6])
    column_copy.wait()
    give(8, 9)
    need("ATT")
    hidden_back = grad[...]
    for i in range(3):
        hidden_back += dot_plain(back[:, pl.ds(768 * i, 768)], rows_of(1 + i))
    hidden_grad[...] = hidden_back.astype(LOW)
    fill(0, 4)

    state_grad[...] = jnp.zeros_like(state_grad)
    total[...] = jnp.zeros_like(total)
    shares = [take(PACE[7]) for _ in range(CHARS)]

    def retreat(i, carry):
        t = CHARS - 1 - i
        record_copy(t).wait()
        gru_backward_step(t, cell, record, state_grad, pool_grad, lengths)
        for k in range(CHARS):
            if shares[k]:

                @pl.when(i == k)
                def _():
                    reduce.run(shares[k])

        return carry

    lax.fori_loop(0, CHARS, retreat, 0)
    for way in (0, 1):
        outbox.settle_all()
        cell_gradient(way, record, thick)
        outbox.send(THIN, thick.at[:, :, :, 0:144], grads["CELL"].at[pl.ds(2 * way, 2)])
        if way == 1:
            give(10, 11, 12)
        go_on(PACE[8])

    def look_up(i, carry):
        table_gradient(i, cell, record, codes, total)
        return carry

    lax.fori_loop(0, CHARS // 4, look_up, 0)
    go_on(PACE[9])
    lax.fori_loop(CHARS // 4, CHARS // 2, look_up, 0)
    table_part[...] = jnp.transpose(total[...]).astype(LOW).reshape((4, 2, 2) + BLOCKS["TABLE"])
    outbox.send(0, table_part, grads["TABLE"])
    give(13)
    reduce.run(steps)
    reduce.run([("finish", p) for p in range(len(PARTS))])


PACE = (1, 1, 1, 1, 2, 2, 2, 1, 7, 7)


def reduce_and_return(whole, saved, record, codes, lengths, hidden, cotangent, valid_keys, per_place):
    in_vmem = pl.BlockSpec(memory_space=pltpu.VMEM)
    anywhere = pl.BlockSpec(memory_space=pl.ANY)
    count = len(PARTS)
    shapes = [jax.ShapeDtypeStruct((2,) + BLOCKS[kind], LOW) for kind in KINDS]
    shapes += [
        jax.ShapeDtypeStruct((TOKENS, 768), LOW),
        jax.ShapeDtypeStruct((count, 4, 2, 2, ROWS, LANES), LOW),
    ]
    shapes += [jax.ShapeDtypeStruct((4, 2, 2) + BLOCKS[kind], LOW) for kind in KINDS]
    views = {
        "ATT": (3, 6, 128, 768),
        "OUT": (6, 128, 1024),
        "IN": (4, 6, 128, 768),
        "FEED": (6, 128, 3072),
        "STREAM": (6, 128, 1536),
        "MERGE": (6, 128, 4608),
    }
    results = pl.pallas_call(
        partial(backward_kernel, per_place),
        out_shape=shapes,
        in_specs=[anywhere] * 7 + [in_vmem] * 5 + [pl.BlockSpec(memory_space=pltpu.SMEM)] + [in_vmem] * len(SAVED),
        out_specs=[anywhere] * 8 + [in_vmem] + [anywhere] * 9,
        scratch_shapes=[
            pltpu.VMEM((CHARS, TOKENS, 2 * RECORD), LOW),
            pltpu.VMEM((TOKENS, 2 * HID), WIDE),
            pltpu.VMEM((TOKENS, 2 * HID), WIDE),
            pltpu.VMEM((1024, EMB), WIDE),
            pltpu.VMEM((128, 768), WIDE),
            pltpu.VMEM((TOKENS, 768), WIDE),
            pltpu.VMEM((TOKENS, 3072), LOW),
            pltpu.VMEM((TOKENS, 2304), LOW),
            pltpu.VMEM((THIN, 4, 2, 2, 48, 768), LOW),
            pltpu.VMEM((2, 2, 2, 192, 768), LOW),
            pltpu.VMEM((4, 2, 2) + BLOCKS["TABLE"], LOW),
            pltpu.VMEM((4, 2, 2, 48, 256), LOW),
            pltpu.VMEM((8, 512), WIDE),
            pltpu.VMEM((SLOTS, 4, 2, 2, ROWS, LANES), LOW),
            pltpu.VMEM((2, 4, 2, 2, ROWS, LANES), LOW),
            pltpu.VMEM((SLOTS, 4, 2, ROWS, LANES), LOW),
            pltpu.VMEM((SLOTS, 8, ROWS, LANES), LOW),
            pltpu.VMEM((SLOTS, 2, ROWS, LANES), LOW),
            pltpu.SemaphoreType.DMA((CHARS,)),
            pltpu.SemaphoreType.DMA((6, 6)),
            pltpu.SemaphoreType.DMA((THIN + 1,)),
            pltpu.SemaphoreType.DMA((1,)),
            pltpu.SemaphoreType.DMA((count, MOVES)),
            pltpu.SemaphoreType.DMA((count, MOVES)),
            pltpu.SemaphoreType.DMA((2, SUBS + 1)),
            pltpu.SemaphoreType.DMA((count, SUBS)),
            pltpu.SemaphoreType.REGULAR((5,)),
        ],
        compiler_params=pltpu.CompilerParams(collective_id=1, has_side_effects=True, vmem_limit_bytes=63 << 20),
    )(
        *[whole[kind].reshape(views[kind]) for kind in DENSE_KINDS],
        record,
        whole["CELL"],
        codes,
        lengths,
        hidden,
        cotangent,
        valid_keys,
        *[saved[name] for name in SAVED],
    )
    return dict(zip(KINDS, results[:8])), results[8]


def unpack_kernel(*refs):
    count = len(KINDS)
    sources, passed = refs[:count], refs[count : count + 2]
    targets = refs[count + 2 : count + 17]
    scratch = refs[count + 17 :]
    held, through = dict(zip(KINDS, scratch[:count])), scratch[count : count + 2]
    made, in_sem, out_sem = scratch[count + 2 : count + 15], scratch[count + 15], scratch[count + 16]
    loads = [
        pltpu.make_async_copy(source, target, in_sem.at[i])
        for i, (source, target) in enumerate(zip((*sources, *passed), (*held.values(), *through)))
    ]
    for copy in loads:
        copy.start()
    for copy in loads:
        copy.wait()
    stores = []

    def store(source, i):
        copy = pltpu.make_async_copy(source, targets[i], out_sem.at[i])
        copy.start()
        stores.append(copy)

    def keep(i, value):
        made[i][...] = value
        store(made[i], 2 + i)

    def rows(kind, first, width):
        value = held[kind][:, :, pl.ds(first, width)]
        return value.reshape(-1, width).astype(WIDE)

    store(through[0], 0)
    store(through[1], 1)
    for k in range(3):
        made[10][k] = rows("MERGE", 1536 * k, 1536)
    store(made[10], 12)
    keep(4, rows("FEED", 0, 3072))
    keep(2, jnp.transpose(rows("IN", 0, 768)))
    for k in range(2):
        made[9][k] = rows("STREAM", 768 * k, 768)
    store(made[9], 11)
    keep(0, rows("ATT", 0, 768))
    keep(1, rows("OUT", 0, 768))
    keep(5, rows("TABLE", 0, 1024)[:, :1000])
    keep(6, rows("CELL", 0, EMB))
    keep(7, rows("CELL", EMB, HID))
    keep(8, jnp.transpose(rows("CELL", EMB + HID, 128))[:2])
    small = jnp.transpose(rows("OUT", 768, 128))
    keep(11, small[10:13])
    keep(12, small[:10])
    low = small[8:24].astype(LOW)
    size = low.shape[1]
    row = lax.broadcasted_iota(jnp.int32, (size, 4 * size), 0)
    lane = lax.broadcasted_iota(jnp.int32, (size, 4 * size), 1)
    flat = jnp.zeros((1, 4 * size), WIDE)
    for j in range(4):
        flat += dot_plain(low, (4 * row + j == lane).astype(LOW))[5 + j : 6 + j]
    keep(3, flat)
    for copy in stores:
        copy.wait()


def unpack(final, output, hidden_grad):
    shapes = [
        (288, 768), (96, 768), (768, 384), (1, 384), (96, 3072), (32, 1000), (288, EMB), (288, HID), (2, 288),
        (2, 96, 768), (3, 96, 1536), (3, 96), (10, 96),
    ]
    anywhere = pl.BlockSpec(memory_space=pl.ANY)
    count = len(KINDS)
    results = pl.pallas_call(
        unpack_kernel,
        out_shape=[jax.ShapeDtypeStruct((TOKENS, 768), LOW)] * 2 + [jax.ShapeDtypeStruct(shape, WIDE) for shape in shapes],
        in_specs=[anywhere] * (count + 2),
        out_specs=[anywhere] * (2 + len(shapes)),
        scratch_shapes=[pltpu.VMEM((2,) + BLOCKS[kind], LOW) for kind in KINDS]
        + [pltpu.VMEM((TOKENS, 768), LOW)] * 2
        + [pltpu.VMEM(shape, WIDE) for shape in shapes]
        + [pltpu.SemaphoreType.DMA((count + 2,)), pltpu.SemaphoreType.DMA((2 + len(shapes),))],
        compiler_params=pltpu.CompilerParams(vmem_limit_bytes=60 << 20),
    )(*[final[kind] for kind in KINDS], output, hidden_grad)
    att, out, feed_in, feed_bias, feed, table, cell_in, cell_back, cell_bias, stream, merge, gains, biases = results[2:]
    return (
        results[0],
        results[1],
        att.T,
        out.T,
        feed_in,
        feed_bias.reshape(-1),
        feed.T,
        table.T,
        cell_in.T,
        cell_back.T,
        cell_bias,
        jnp.swapaxes(stream, 1, 2),
        jnp.swapaxes(merge, 1, 2),
        gains,
        biases,
    )


def shards(hidden, char_codes, word_length, sequence_length, cotangent, *parameters):
    wide = lax.axis_size("wide")
    per_place = wide // 2
    starts = pack(parameters, per_place)
    codes = jnp.transpose(char_codes)
    lengths = word_length[:, None]
    whole, record, saved = gather_and_read(starts, codes, lengths, hidden, sequence_length, per_place)
    final, hidden_grad = reduce_and_return(
        whole, saved, record, codes, lengths, hidden, cotangent, sequence_length, per_place
    )
    return unpack(final, saved["output"], hidden_grad)


def solution(mesh):
    rows = P(("grp", "wide"), None)
    flat = P(("grp", "wide"))
    last = P(None, ("grp", "wide"))
    deep = P(None, None, ("grp", "wide"))
    in_specs = (rows, rows, flat, flat, rows, last, last, last, flat, last, last, last, last, last, deep, deep, last, last)
    out_specs = (rows, rows) + (P(None, "grp"),) * 3 + (P("grp"),) + (P(None, "grp"),) * 5 + (P(None, None, "grp"),) * 2 + (P(None, "grp"),) * 2
    return jax.shard_map(shards, mesh=mesh, in_specs=in_specs, out_specs=out_specs, check_vma=False)
```

```python
from functools import partial

import jax
import jax.numpy as jnp
from jax import lax
from jax.experimental import pallas as pl
from jax.experimental.pallas import tpu as pltpu
from jax.sharding import PartitionSpec as P

HEADS = 12
HID = 384
EMB = 256
CHARS = 20
TOKENS = 128
norm_eps = 1e-05
masked_score = -1e30
MESH = pl.DeviceIdType.MESH
EVERY = slice(None)
LOW = jnp.bfloat16
WIDE = jnp.float32

BLOCKS = {
    "CELL": (144, 768),
    "TABLE": (16, 1024),
    "ATT": (144, 768),
    "OUT": (48, 1024),
    "IN": (192, 768),
    "FEED": (48, 3072),
    "STREAM": (48, 1536),
    "MERGE": (48, 4608),
}
KINDS = tuple(BLOCKS)
STARTS = (
    ("CELL", 0, 256, 1),
    ("CELL", 256, 384, 1),
    ("CELL", 640, 128, 1),
    ("TABLE", 0, 1000, 1),
    ("ATT", 0, 768, 1),
    ("OUT", 0, 768, 1),
    ("OUT", 768, 128, 1),
    ("IN", 0, 768, 1),
    ("FEED", 0, 3072, 1),
    ("STREAM", 0, 768, 2),
    ("MERGE", 0, 1536, 3),
)
PIECES = (
    ("CELL", 0, 384, 128, True),
    ("CELL", 128, 512, 256, True),
    ("TABLE", 0, 512, 512, False),
    ("ATT", 0, 384, 384, False),
    ("OUT", 0, 512, 512, True),
    ("IN", 0, 128, 128, False),
    ("IN", 256, 512, 256, False),
    ("FEED", 0, 768, 768, False),
    ("FEED", 1536, 2304, 768, True),
    ("STREAM", 0, 768, 768, False),
    ("MERGE", 0, 768, 768, False),
    ("MERGE", 1536, 2304, 768, True),
    ("MERGE", 3072, 3840, 768, False),
)
GATHER_MOVES = 11
AHEAD = 3
LAGS = (0, 2, 4, 6)

X_WIDTH = 768
RECORD = X_WIDTH + 4 * HID
GATE_R, GATE_Z, GATE_N, GATE_Q = (X_WIDTH + i * HID for i in range(4))


def dot_plain(left_side, right_side):
    return jnp.dot(left_side, right_side, preferred_element_type=WIDE)


def dot_first(left_side, right_side):
    return lax.dot_general(left_side, right_side, (((0,), (0,)), ((), ())), preferred_element_type=WIDE)


def dot_second(left_side, right_side):
    return lax.dot_general(left_side, right_side, (((1,), (1,)), ((), ())), preferred_element_type=WIDE)


def lanes_of(ref, start, width):
    return ref[:, pl.ds(start, width)]


def sigmoid(inputs):
    return 0.5 * jnp.tanh(0.5 * inputs) + 0.5


class Spot:
    def __init__(self, per_place):
        self.grp, self.wide = lax.axis_index("grp"), lax.axis_index("wide")
        self.z, self.x = self.grp // 2, self.grp % 2
        self.y, self.core = self.wide // per_place, self.wide % 2
        self.to_x = (self.grp + 1 - 2 * self.x, self.wide)
        self.to_y = (self.grp, self.wide + per_place - 2 * per_place * self.y)
        self.sibling = (self.grp, self.wide + 1 - 2 * self.core)

    def hop(self, k):
        return (2 * ((self.z + k) % 4) + self.x, self.wide)

    def greet(self):
        barrier = pltpu.get_barrier_semaphore()
        for other in [self.to_x, self.to_y, self.sibling] + [self.hop(k) for k in (1, 2, 3)]:
            pl.semaphore_signal(barrier, 1, device_id=other, device_id_type=MESH)
        pl.semaphore_wait(barrier, 6)

    def near(self, core):
        if core == 0:
            return self.x, self.y, self.to_x, self.to_y
        return self.y, self.x, self.to_y, self.to_x


def remote(source, target, sent, received, device):
    return pltpu.make_async_remote_copy(
        src_ref=source, dst_ref=target, send_sem=sent, recv_sem=received, device_id=device, device_id_type=MESH
    )


class Gather:
    def __init__(self, spot, whole, sems):
        self.spot, self.whole = spot, whole
        self.sent, self.got = sems

    def region(self, core, p, z, f, l):
        kind, first, second, width, _ = PIECES[p]
        lanes = pl.ds((first, second)[core], width)
        return self.whole[kind].at[z, f, l, :, lanes] if core == 0 else self.whole[kind].at[z, l, f, :, lanes]

    def move(self, part, p, j, device, at_sent=None):
        return remote(part, part, self.sent.at[p, j if at_sent is None else at_sent], self.got.at[p, j], device)

    def hop_part(self, core, p, z):
        f, l, _, _ = self.spot.near(core)
        return self.region(core, p, z, f if PIECES[p][4] else EVERY, l)

    def near_part(self, core, p, mine):
        f, l, _, _ = self.spot.near(core)
        return self.region(core, p, EVERY if PIECES[p][4] else self.spot.z, f if mine else 1 - f, l)

    def far_part(self, core, p, mine):
        _, l, _, _ = self.spot.near(core)
        return self.region(core, p, EVERY, EVERY, l if mine else 1 - l)

    def hop(self, core, p, k):
        return self.move(self.hop_part(core, p, self.spot.z), p, k - 1, self.spot.hop(k))

    def hop_in(self, core, p, k):
        return self.move(self.hop_part(core, p, (self.spot.z + 4 - k) % 4), p, k - 1, self.spot.hop(k))

    def relay(self, core, p, z):
        if z == 2:
            return self.move(self.hop_part(core, p, 0), p, 2, self.spot.hop(1), 10)
        return self.move(self.hop_part(core, p, 3), p, 0, self.spot.hop(3), 10)

    def near(self, core, p, mine):
        return self.move(self.near_part(core, p, mine), p, 3, self.spot.near(core)[2])

    def far(self, core, p, mine):
        return self.move(self.far_part(core, p, mine), p, 4, self.spot.near(core)[3])

    def aside(self, core, p, j):
        if j < 3:
            part = self.hop_part(core, p, (self.spot.z + 3 - j) % 4)
        else:
            part = self.near_part(core, p, False) if j == 3 else self.far_part(core, p, False)
        return self.move(part, p, 5 + j, self.spot.sibling)

    def own_hops(self, core, p, act):
        for k, end in ((2, None), (1, 3), (3, 0)):
            if end is None:
                act(self.hop(core, p, k))
            else:

                @pl.when(self.spot.z != end)
                def _():
                    act(self.hop(core, p, k))

    def relays(self, core, p, act):
        for z in (1, 2):

            @pl.when(self.spot.z == z)
            def _():
                act(self.relay(core, p, z))

    def start_hops(self, core, p):
        self.own_hops(core, p, lambda copy: copy.start())

    def take_hops(self, core, p):
        self.hop_in(core, p, 2).wait_recv()
        self.relays(core, p, lambda copy: copy.start())
        for k in (1, 3):
            self.hop_in(core, p, k).wait_recv()

    def start(self, core, p):
        if PIECES[p][4]:
            self.start_hops(core, p)
        else:
            self.near(core, p, True).start()

    def second(self, core, p):
        if PIECES[p][4]:
            self.take_hops(core, p)
            self.near(core, p, True).start()
            for j in (0, 2, 1):
                self.aside(core, p, j).start()
        else:
            self.near(core, p, False).wait_recv()
            self.start_hops(core, p)
            self.aside(core, p, 3).start()

    def third(self, core, p):
        if PIECES[p][4]:
            self.near(core, p, False).wait_recv()
            self.far(core, p, True).start()
            self.aside(core, p, 3).start()
        else:
            self.take_hops(core, p)
            self.far(core, p, True).start()
            for j in (0, 2, 1):
                self.aside(core, p, j).start()

    def fourth(self, core, p):
        self.far(core, p, False).wait_recv()
        self.aside(core, p, 4).start()

    def fifth(self, core, p):
        for j in range(5):
            self.aside(1 - core, p, j).wait_recv()

    def drain(self, core, p):
        self.own_hops(core, p, lambda copy: copy.wait_send())
        self.relays(core, p, lambda copy: copy.wait_send())
        self.near(core, p, True).wait_send()
        self.far(core, p, True).wait_send()
        for j in range(5):
            self.aside(core, p, j).wait_send()

    def turns(self):
        count = len(PIECES)
        turns = []
        for s in range(count + LAGS[-1]):
            ahead = range(AHEAD + 1) if s == 0 else [s + AHEAD]
            turn = [("start", p) for p in ahead if p < count]
            for lag, stage in zip(LAGS, ("second", "third", "fourth", "fifth")):
                if 0 <= s - lag < count:
                    turn.append((stage, s - lag))
            turns.append(turn)
        return turns

    def run(self, steps):
        for core in (0, 1):

            @pl.when(self.spot.core == core)
            def _():
                for stage, p in steps:
                    getattr(self, stage)(core, p)


RING = 4


def gru_forward_step(t, cell, spelled, record, state, total, shifts, lengths):
    slot = t % RING
    for way in (0, 1):
        base = way * RECORD
        place = t if way == 0 else CHARS - 1 - t
        live = lengths[:, :1] > place
        lanes = pl.ds(way * HID, HID)
        h = state[:, lanes]
        record[slot, :, pl.ds(base, EMB)] = spelled[place]
        record[slot, :, pl.ds(base + EMB, HID)] = h.astype(LOW)
        x = record[slot, :, pl.ds(base, X_WIDTH)]
        weights = cell[pl.ds(2 * way, 2)].reshape(3 * HID, X_WIDTH)
        both = dot_second(x, weights[: 2 * HID])
        drive_n = dot_second(x[:, :EMB], weights[2 * HID :, :EMB]) + shifts[way, 0:1]
        recur_n = dot_second(x[:, EMB : EMB + HID], weights[2 * HID :, EMB : EMB + HID]) + shifts[way, 1:2]
        r = sigmoid(both[:, :HID])
        u = sigmoid(both[:, HID:])
        n = jnp.tanh(drive_n + r * recur_n)
        fresh = jnp.where(live, n + u * (h - n), h)
        state[:, lanes] = fresh
        total[:, lanes] += jnp.where(live, fresh, 0.0)
        record[slot, :, pl.ds(base + GATE_R, HID)] = r.astype(LOW)
        record[slot, :, pl.ds(base + GATE_Z, HID)] = u.astype(LOW)
        record[slot, :, pl.ds(base + GATE_N, HID)] = n.astype(LOW)
        record[slot, :, pl.ds(base + GATE_Q, HID)] = recur_n.astype(LOW)


def spread_matrix():
    shape = (512, 512)
    row, lane = lax.broadcasted_iota(jnp.int32, shape, 0), lax.broadcasted_iota(jnp.int32, shape, 1)
    return (4 * (row % 128) + row // 128 == lane).astype(LOW)


def read_small(out, small, feed_row, shuffle):
    columns = out[:, :, :, :, pl.ds(768, 128)].reshape(768, 128).astype(WIDE)
    rows = jnp.transpose(columns)
    small[...] = rows[:32]
    shuffle[...] = jnp.zeros_like(shuffle)
    for c in range(6):
        for j in range(4):
            shuffle[c : c + 1, 128 * j : 128 * j + 128] = rows[13 + j : 14 + j, 128 * c : 128 * c + 128]
    flat = dot_plain(shuffle[...].astype(LOW), spread_matrix())
    for c in range(6):
        feed_row[:, 512 * c : 512 * c + 512] = flat[c : c + 1]


def norm_forward(inputs, i, small, gain, shift, norms, spreads):
    centred = inputs - jnp.mean(inputs, axis=-1, keepdims=True)
    inverse = lax.rsqrt(jnp.mean(centred * centred, axis=-1, keepdims=True) + norm_eps)
    unit = centred * inverse
    norms[i] = unit
    spreads[i] = jnp.broadcast_to(inverse, spreads.shape[1:])
    return unit * small[gain : gain + 1] + small[shift : shift + 1]


def head_mask(which):
    lane = lax.broadcasted_iota(jnp.int32, (TOKENS, 128), 1)
    return (lane < 64) if which == 0 else (lane >= 64)


def one_head(pair, which):
    return jnp.where(head_mask(which), pair, jnp.zeros_like(pair))


def soft_weights(queries, keys, which, valid):
    scores = dot_second(one_head(queries, which), keys) * 0.125 + valid
    weight = jnp.exp(scores - jnp.max(scores, axis=-1, keepdims=True))
    return weight / jnp.sum(weight, axis=-1, keepdims=True)


def key_mask(count):
    lane = lax.broadcasted_iota(jnp.int32, (TOKENS, TOKENS), 1)
    return jnp.where(lane < count, 0.0, masked_score).astype(WIDE)


def attention_forward(projected, context, valid):
    def pair(i, carry):
        def part(at):
            return projected[:, pl.ds(pl.multiple_of(at * 768 + 128 * i, 128), 128)]

        queries, keys, values = part(0), part(1), part(2)
        total = jnp.zeros((TOKENS, 128), WIDE)
        for which in (0, 1):
            soft = soft_weights(queries, keys, which, valid).astype(LOW)
            total += dot_plain(soft, one_head(values, which))
        context[:, pl.ds(pl.multiple_of(128 * i, 128), 128)] = total.astype(LOW)
        return carry

    lax.fori_loop(0, 6, pair, 0)


def shifted(rows, down):
    turned = pltpu.roll(rows, 1 if down else TOKENS - 1, 0)
    row = lax.broadcasted_iota(jnp.int32, rows.shape, 0)
    return jnp.where(row == (0 if down else TOKENS - 1), 0.0, turned)


def window(joined, k):
    if k == 1:
        return joined[...]
    return shifted(joined[...].astype(WIDE), k == 0).astype(LOW)


def spread_lengths(row, column):
    square = jnp.broadcast_to(row[...].astype(WIDE), (TOKENS, TOKENS))
    column[...] = jnp.transpose(square).astype(jnp.int32)


def forward_kernel(per_place, *refs):
    count = len(KINDS)
    starts = refs[: len(STARTS)]
    codes, length_row, hidden, valid_keys = refs[len(STARTS) : len(STARTS) + 4]
    outs = refs[len(STARTS) + 4 :]
    kept = dict(zip(KINDS, outs[:count]))
    record_out, output, joined, pooled_low, norms, spreads, small = outs[count : count + 7]
    early_out = outs[count + 7 : count + 11]
    scratch = outs[count + 11 :]
    whole = dict(zip(KINDS, scratch[:count]))
    (record, spelled, state, pooled, shifts, feed_row, shuffle, first, second, merged, sent, got, own_sent, own_got, kept_sem, record_sem, early_sem) = scratch[count : count + 17]
    lengths = scratch[3 * count + 17]
    projected, context, active, slope = early = scratch[3 * count + 18 :]
    spread_lengths(length_row, lengths)
    mine, theirs = (dict(zip(KINDS, scratch[at : at + count])) for at in (count + 17, 2 * count + 17))
    spot = Spot(per_place)
    halves = per_place == 2

    def lay(kind):
        if kind in ("TABLE", "OUT"):
            mine[kind][...] = jnp.zeros_like(mine[kind])
        for ref, (owner, first, width, parts) in zip(starts, STARTS):
            if owner != kind:
                continue
            for part in range(parts):
                rows = ref[...] if parts == 1 else ref[part]
                lanes = pl.ds(first + part * width, width)
                if not halves:
                    mine[kind][:, lanes] = rows
                    continue
                rows = rows.astype(WIDE)
                blank = jnp.zeros_like(rows)
                low = jnp.where(spot.core == 0, rows, blank)
                high = jnp.where(spot.core == 0, blank, rows)
                mine[kind][:, lanes] = jnp.concatenate([low, high], axis=0).astype(LOW)

    def swap(kind):
        at = KINDS.index(kind)
        return remote(mine[kind], theirs[kind], own_sent.at[at], own_got.at[at], spot.sibling)

    def ready(kind):
        if halves:
            swap(kind).wait_recv()
            whole[kind][spot.z, spot.x, spot.y] = mine[kind][...] + theirs[kind][...]
        else:
            whole[kind][spot.z, spot.x, spot.y] = mine[kind][...]

    for kind in KINDS[:3]:
        lay(kind)
    spot.greet()
    for kind in KINDS[:3]:
        if halves:
            swap(kind).start()
    for kind in KINDS[3:]:
        lay(kind)
        if halves:
            swap(kind).start()
    gather = Gather(spot, whole, (sent, got))
    turns = gather.turns()

    def keep(kind, part=None):
        at = KINDS.index(kind)
        if part is None:
            return pltpu.make_async_copy(whole[kind], kept[kind], kept_sem.at[at])
        lanes = pl.ds(1536 * part, 1536)
        return pltpu.make_async_copy(whole[kind].at[..., lanes], kept[kind].at[..., lanes], kept_sem.at[at + part])

    def weights(kind):
        value = whole[kind][...]
        return value.reshape(-1, value.shape[-1])

    last_of = {kind: max(p for p, piece in enumerate(PIECES) if piece[0] == kind) for kind in KINDS}
    steps = [step for turn in turns for step in turn]

    def after(kind):
        return steps.index(("fifth", last_of[kind])) + 1

    lead = max(after("CELL"), after("TABLE"))
    waiting = list(KINDS)
    for stage, p in steps[:lead]:
        if stage == "start" and PIECES[p][0] in waiting:
            ready(PIECES[p][0])
            waiting.remove(PIECES[p][0])
        gather.run([(stage, p)])
    for kind in waiting:
        ready(kind)
    for kind in ("CELL", "TABLE"):
        keep(kind).start()
    cell, table = whole["CELL"], weights("TABLE")

    def embed(c, carry):
        which = (lax.broadcasted_iota(jnp.int32, (1024, TOKENS), 0) == codes[pl.ds(c, 1)]).astype(LOW)
        spelled[c] = jnp.transpose(dot_plain(table, which)).astype(LOW)
        return carry

    lax.fori_loop(0, CHARS, embed, 0)
    pick = (
        lax.broadcasted_iota(jnp.int32, (8, 128), 0) == lax.broadcasted_iota(jnp.int32, (8, 128), 1)
    ).astype(LOW)
    ones = (lax.broadcasted_iota(jnp.int32, (TOKENS, 128), 1) < 2).astype(LOW)
    for way in (0, 1):
        late = cell[pl.ds(2 * way, 2)].reshape(3 * HID, X_WIDTH)[2 * HID :, EMB + HID :]
        shifts[way] = dot_second(pick, late)
        for slot in range(RING):
            record[slot, :, pl.ds(way * RECORD + EMB + HID, 128)] = ones
    state[...] = jnp.zeros_like(state)
    pooled[...] = jnp.zeros_like(pooled)

    def attend():
        for kind in ("ATT", "OUT"):
            keep(kind).start()
        read_small(whole["OUT"], small, feed_row, shuffle)
        attention_in = weights("ATT")
        for i, bias in enumerate((0, None, 1)):
            block = dot_second(hidden[...], attention_in[768 * i : 768 * i + 768])
            if bias is not None:
                block = block + small[bias : bias + 1]
            projected[:, 768 * i : 768 * i + 768] = block.astype(LOW)
        attention_forward(projected, context, key_mask(valid_keys[0]))
        store(0).start()
        store(1).start()

    def add_attended():
        attended = dot_second(context[...], weights("OUT")[:, :768]) + small[2:3]
        first[...] = norm_forward(hidden[...].astype(WIDE) + attended, 0, small, 10, 3, norms, spreads)

    def feed(c):
        if c == 0:
            keep("IN").start()
        rows = whole["IN"][c].reshape(768, 768)
        inner = dot_second(first[...].astype(LOW), rows) + feed_row[:, 768 * c : 768 * c + 768]
        share_below = 0.5 * (1.0 + lax.erf(inner * 0.7071067811865476))
        active[:, 768 * c : 768 * c + 768] = (inner * share_below).astype(LOW)
        slope[:, 768 * c : 768 * c + 768] = (
            share_below + inner * (0.3989422804014327 * jnp.exp(-0.5 * inner * inner))
        ).astype(LOW)

    def feed_back():
        store(2).start()
        store(3).start()
        keep("FEED").start()
        two = first[...] + dot_second(active[...], weights("FEED")) + small[4:5]
        second[...] = norm_forward(two, 1, small, 11, 5, norms, spreads)

    def token_side():
        stream = whole["STREAM"][:, :, :, :, pl.ds(0, 768)].reshape(768, 768)
        joined[:, :768] = (dot_second(second[...].astype(LOW), stream) + small[6:7]).astype(LOW)

    def store(i):
        return pltpu.make_async_copy(early[i], early_out[i], early_sem.at[i])

    def record_copy(t):
        return pltpu.make_async_copy(record.at[t % RING], record_out.at[t], record_sem.at[t % RING])

    jobs = [(after("OUT"), attend), (0, add_attended)]
    jobs += [(after("IN"), partial(feed, c)) for c in range(4)]
    jobs += [(after("FEED"), feed_back), (after("STREAM"), token_side)]
    shares = [lead + -(-(GRU_END - lead) * (k + 1) // CHARS) for k in range(CHARS)]
    during = {k: [] for k in range(CHARS)}
    late_jobs = []
    at = 0
    for need, job in jobs:
        ready = [k for k in range(CHARS) if shares[k] >= need]
        at = max([at] + ready[:1]) if ready else CHARS
        if at < CHARS:
            during[at].append(job)
            at += 1
        else:
            late_jobs.append((need, job))

    def advance(t, carry):
        @pl.when(t >= RING)
        def _():
            record_copy(t - RING).wait()

        gru_forward_step(t, cell, spelled, record, state, pooled, shifts, lengths)
        record_copy(t).start()
        for k in range(CHARS):
            part = steps[shares[k - 1] if k else lead : shares[k]]
            if part or during[k]:

                @pl.when(t == k)
                def _():
                    gather.run(part)
                    for job in during[k]:
                        job()

        return carry

    lax.fori_loop(0, CHARS, advance, 0)
    pooled_low[...] = (pooled[...] / lengths[:, :1].astype(WIDE)).astype(LOW)
    done = shares[-1]
    for need, job in late_jobs:
        gather.run(steps[done:need])
        done = max(done, need)
        job()
    gather.run(steps[done : after("STREAM")])
    done = max(done, after("STREAM"))
    keep("STREAM").start()
    stream = whole["STREAM"][:, :, :, :, pl.ds(768, 768)].reshape(768, 768)
    joined[:, 768:] = (dot_second(pooled_low[...], stream) + small[7:8]).astype(LOW)
    taps_at = [p for p, piece in enumerate(PIECES) if piece[0] == "MERGE"]
    for k in range(3):
        until = steps.index(("fifth", taps_at[k])) + 1
        gather.run(steps[done:until])
        done = max(done, until)
        keep("MERGE", k).start()
        taps = whole["MERGE"][:, :, :, :, pl.ds(1536 * k, 1536)].reshape(768, 1536)
        part = dot_second(window(joined, k), taps)
        merged[...] = part if k == 0 else merged[...] + part
    third = second[...] + merged[...] + small[8:9]
    output[...] = norm_forward(third, 2, small, 12, 9, norms, spreads).astype(LOW)

    def landed(t, carry):
        record_copy(t).wait()
        return carry

    lax.fori_loop(CHARS - RING, CHARS, landed, 0)
    gather.run([("drain", p) for p in range(len(PIECES))])
    for i in range(len(EARLY)):
        store(i).wait()
    for kind in KINDS:
        for part in range(3) if kind == "MERGE" else (None,):
            keep(kind, part).wait()
        if halves:
            swap(kind).wait_send()


GRU_END = 62
EARLY = {
    "projected": ((TOKENS, 2304), LOW),
    "context": ((TOKENS, 768), LOW),
    "active": ((TOKENS, 3072), LOW),
    "slope": ((TOKENS, 3072), LOW),
}


def gather_and_read(starts, codes, lengths, hidden, valid_keys, per_place):
    count = len(KINDS)
    in_vmem = pl.BlockSpec(memory_space=pltpu.VMEM)
    anywhere = pl.BlockSpec(memory_space=pl.ANY)
    whole_shapes = [(4, 2, 2) + BLOCKS[kind] for kind in KINDS]
    saved = {
        "output": ((TOKENS, 768), LOW),
        "joined": ((TOKENS, 1536), LOW),
        "pooled": ((TOKENS, 768), LOW),
        "norms": ((3, TOKENS, 768), WIDE),
        "spreads": ((3, TOKENS, 128), WIDE),
        "small": ((32, 768), WIDE),
        **EARLY,
    }
    results = pl.pallas_call(
        partial(forward_kernel, per_place),
        out_shape=[jax.ShapeDtypeStruct(shape, LOW) for shape in whole_shapes]
        + [jax.ShapeDtypeStruct((CHARS, TOKENS, 2 * RECORD), LOW)]
        + [jax.ShapeDtypeStruct(shape, kind) for shape, kind in saved.values()],
        in_specs=[in_vmem] * (len(STARTS) + 3) + [pl.BlockSpec(memory_space=pltpu.SMEM)],
        out_specs=[anywhere] * (count + 1) + [in_vmem] * (len(saved) - len(EARLY)) + [anywhere] * len(EARLY),
        scratch_shapes=[pltpu.VMEM(shape, LOW) for shape in whole_shapes]
        + [
            pltpu.VMEM((RING, TOKENS, 2 * RECORD), LOW),
            pltpu.VMEM((CHARS, TOKENS, EMB), LOW),
            pltpu.VMEM((TOKENS, 2 * HID), WIDE),
            pltpu.VMEM((TOKENS, 2 * HID), WIDE),
            pltpu.VMEM((2, 8, HID), WIDE),
            pltpu.VMEM((1, 3072), WIDE),
            pltpu.VMEM((8, 512), WIDE),
            pltpu.VMEM((TOKENS, 768), WIDE),
            pltpu.VMEM((TOKENS, 768), WIDE),
            pltpu.VMEM((TOKENS, 768), WIDE),
            pltpu.SemaphoreType.DMA((len(PIECES), GATHER_MOVES)),
            pltpu.SemaphoreType.DMA((len(PIECES), GATHER_MOVES)),
            pltpu.SemaphoreType.DMA((count,)),
            pltpu.SemaphoreType.DMA((count,)),
            pltpu.SemaphoreType.DMA((count + 2,)),
            pltpu.SemaphoreType.DMA((RING,)),
            pltpu.SemaphoreType.DMA((len(EARLY),)),
        ]
        + [pltpu.VMEM(BLOCKS[kind], LOW) for kind in KINDS + KINDS]
        + [pltpu.VMEM((TOKENS, TOKENS), jnp.int32)]
        + [pltpu.VMEM(shape, kind) for shape, kind in EARLY.values()],
        compiler_params=pltpu.CompilerParams(collective_id=0, has_side_effects=True, vmem_limit_bytes=60 << 20),
    )(*starts, codes, lengths, hidden, valid_keys)
    return dict(zip(KINDS, results[:count])), results[count], dict(zip(saved, results[count + 1 :]))


def pack(shards, per_place):
    (attention_in, attention_out, feed_in, feed_bias, feed_out, char_table, cell_input, cell_recurrent, cell_bias,
     stream_weight, merging_kernel, norm_gains, biases) = shards

    def lanes(parts, width):
        together = jnp.concatenate(parts, axis=1)
        return jnp.pad(together, ((0, 0), (0, width - together.shape[1])))

    rows = attention_out.shape[1]
    starts = [
        cell_input.T,
        cell_recurrent.T,
        lanes([cell_bias.T], 128),
        char_table.T,
        attention_in.T,
        attention_out.T,
        lanes([biases.T, norm_gains.T, feed_bias.reshape(rows, 4)], 128),
        feed_in.T,
        feed_out.T,
        jnp.swapaxes(stream_weight, 1, 2),
        jnp.swapaxes(merging_kernel, 1, 2),
    ]
    if per_place == 2:
        return starts
    size = lax.axis_size("wide")
    groups = [list(range(i, i + per_place)) for i in range(0, size, per_place)]
    return [
        lax.all_gather(part, "wide", axis=part.ndim - 2, tiled=True, axis_index_groups=groups) for part in starts
    ]


def gru_backward_step(t, cell, record, state_grad, pool_grad, lengths):
    for way in (0, 1):
        base = way * RECORD
        place = t if way == 0 else CHARS - 1 - t
        live = lengths[:, :1] > place
        lanes = pl.ds(way * HID, HID)

        def saved(at):
            return record[t, :, pl.ds(base + at, HID)].astype(WIDE)

        r, u, n, recur_n, h = saved(GATE_R), saved(GATE_Z), saved(GATE_N), saved(GATE_Q), saved(EMB)
        grad = state_grad[:, lanes]
        fresh = jnp.where(live, grad + pool_grad[:, lanes], 0.0)
        kept = jnp.where(live, 0.0, grad)
        grad_n = fresh * (1.0 - u) * (1.0 - n * n)
        grad_z = fresh * (h - n) * u * (1.0 - u)
        grad_r = grad_n * recur_n * r * (1.0 - r)
        low_r, low_z, low_n, low_q = (v.astype(LOW) for v in (grad_r, grad_z, grad_n, grad_n * r))
        record[t, :, pl.ds(base + GATE_R, HID)] = low_r
        record[t, :, pl.ds(base + GATE_Z, HID)] = low_z
        record[t, :, pl.ds(base + GATE_N, HID)] = low_n
        record[t, :, pl.ds(base + GATE_Q, HID)] = low_q
        weights = cell[pl.ds(2 * way, 2)].reshape(3 * HID, X_WIDTH)[:, EMB : EMB + HID]
        gates = jnp.concatenate([low_r, low_z, low_q], axis=1)
        state_grad[:, lanes] = kept + fresh * u + dot_plain(gates, weights)


def cell_gradient(way, record, result):
    base = way * RECORD
    rows = CHARS * TOKENS

    def every(at, width):
        return record[:, :, pl.ds(base + at, width)].reshape(rows, width)

    x = every(0, X_WIDTH)
    parts = [dot_first(every(at, HID), x).astype(LOW) for at in (GATE_R, GATE_Z)]
    ends = EMB + HID
    drive, recur = every(GATE_N, HID), every(GATE_Q, HID)
    late = dot_first(recur, x[:, EMB:])
    lane = lax.broadcasted_iota(jnp.int32, (HID, 128), 1)
    shift = jnp.where(lane == 0, dot_first(drive, x[:, ends:]), late[:, HID:])
    parts.append(jnp.concatenate([dot_first(drive, x[:, :EMB]), late[:, :HID], shift], axis=1).astype(LOW))
    result[:, :, :, 0:144] = jnp.concatenate(parts, axis=0).reshape(2, 2, 2, 144, X_WIDTH)


def table_gradient(i, cell, record, codes, result):
    c = 2 * i

    def drive(way, t):
        gates = record[pl.ds(t, 2), :, pl.ds(way * RECORD + GATE_R, 3 * HID)].reshape(2 * TOKENS, 3 * HID)
        return dot_plain(gates, cell[pl.ds(2 * way, 2)].reshape(3 * HID, X_WIDTH)[:, :EMB])

    behind = drive(1, CHARS - 2 - c)
    both = drive(0, c) + jnp.concatenate([behind[TOKENS:], behind[:TOKENS]], axis=0)
    character = lax.broadcasted_iota(jnp.int32, (1024, TOKENS), 0)
    which = [(character == codes[pl.ds(c + k, 1)]).astype(LOW) for k in (0, 1)]
    result[...] += dot_plain(jnp.concatenate(which, axis=1), both.astype(LOW))


ROWS, LANES = 48, 768
PARTS = (
    [("MERGE", 0, 48, 0, 768, 768, 0, 0, True)],
    [("MERGE", 0, 48, 1536, 2304, 768, 0, 0, True)],
    [("MERGE", 0, 48, 3072, 3840, 768, 0, 0, True)],
    [("STREAM", 0, 48, 0, 768, 768, 0, 0, True)],
    [("FEED", 0, 48, 0, 768, 768, 0, 0, True)],
    [("FEED", 0, 48, 1536, 2304, 768, 0, 0, True)],
    [("IN", 0, 48, 0, 384, 384, 0, 0, True), ("IN", 48, 48, 0, 384, 384, 0, 384, True)],
    [("IN", 96, 48, 0, 384, 384, 0, 0, True), ("IN", 144, 48, 0, 384, 384, 0, 384, True)],
    [("ATT", 0, 48, 0, 384, 384, 0, 0, True), ("ATT", 48, 48, 0, 384, 384, 0, 384, True)],
    [("ATT", 96, 48, 0, 384, 384, 0, 0, True), ("OUT", 0, 48, 0, 512, 384, 0, 384, True)],
    [("CELL", 0, 48, 0, 384, 384, 0, 0, True)],
    [("CELL", 48, 48, 0, 384, 384, 0, 0, True)],
    [("CELL", 96, 48, 0, 384, 384, 0, 0, True)],
    [
        ("OUT", 0, 48, 384, 896, 128, 0, 0, True),
        ("TABLE", 0, 16, 0, 512, 256, 0, 128, True),
        ("TABLE", 0, 16, 256, 768, 256, 16, 128, True),
        ("TABLE", 0, 16, 256, 768, 256, 32, 128, False),
    ],
)
WIDTHS = (768,) * 10 + (384,) * 4
SLOTS = 7
SUBS = 4
DENSE_PARTS = 10
AT_FIRST, AT_HOP, AT_NEXT, AT_LAST, AT_RESULT = SUBS, SUBS, SUBS + 4, SUBS + 5, SUBS + 6
MOVES = 2 * SUBS + 6


class Reduce:
    def __init__(self, spot, grads, landing, buffers, result, sems):
        self.spot, self.grads, self.landing, self.result = spot, grads, landing, result
        self.sums, self.other, self.one_in, self.next_in, self.final = buffers
        self.sent, self.got, self.load_sem, self.keep_sem, self.free = sems

    def lanes(self, p):
        return pl.ds(0, WIDTHS[p])

    def move(self, source, target, p, j, device):
        return remote(source, target, self.sent.at[p, j], self.got.at[p, j], device)

    def outside(self, ref, sub, core):
        _, row, rows, first, second, width, _, _, _ = sub
        return ref.at[..., pl.ds(row, rows), pl.ds((first, second)[core], width)]

    def inside(self, ref, sub):
        _, _, rows, _, _, width, row, lane, _ = sub
        return ref.at[..., pl.ds(row, rows), pl.ds(lane, width)]

    def given(self, core, p):
        return [
            self.move(
                self.outside(self.grads[sub[0]], sub, 1 - core), self.inside(self.landing.at[p], sub), p, i, self.spot.sibling
            )
            for i, sub in enumerate(PARTS[p])
        ]

    def loads(self, core, p):
        w = self.lanes(p)
        own = [
            pltpu.make_async_copy(
                self.outside(self.grads[sub[0]], sub, core), self.inside(self.sums.at[p % SLOTS], sub), self.load_sem.at[p % 2, i]
            )
            for i, sub in enumerate(PARTS[p])
        ]
        return own + [pltpu.make_async_copy(self.landing.at[p, ..., w], self.other.at[p % 2, ..., w], self.load_sem.at[p % 2, SUBS])]

    def first(self, core, p):
        s, slot, w = self.spot, p % SLOTS, self.lanes(p)
        if core == 0:
            return self.move(self.sums.at[slot, :, 1 - s.x, :, :, w], self.one_in.at[slot, ..., w], p, AT_FIRST, s.to_x)
        return self.move(self.sums.at[slot, :, :, 1 - s.y, :, w], self.one_in.at[slot, ..., w], p, AT_FIRST, s.to_y)

    def hop(self, core, p, k):
        s, slot, w = self.spot, p % SLOTS, self.lanes(p)
        z = (s.z + k) % 4
        if core == 0:
            return self.move(self.sums.at[slot, z, s.x, :, :, w], self.next_in.at[slot, pl.ds(2 * k - 2, 2), :, w], p, AT_HOP + k, s.hop(k))
        return self.move(self.sums.at[slot, z, s.x, s.y, :, w], self.next_in.at[slot, 3 + k, :, w], p, AT_HOP + k, s.hop(k))

    def next(self, core, p):
        s, slot, w = self.spot, p % SLOTS, self.lanes(p)
        if core == 0:
            return self.move(self.sums.at[slot, s.z, s.x, :, :, w], self.next_in.at[slot, pl.ds(6, 2), :, w], p, AT_NEXT, s.to_y)
        return self.move(self.sums.at[slot, :, 1 - s.x, s.y, :, w], self.next_in.at[slot, pl.ds(0, 4), :, w], p, AT_NEXT, s.to_x)

    def last(self, p, mine):
        s, slot, w = self.spot, p % SLOTS, self.lanes(p)
        part = self.final.at[slot, s.y if mine else 1 - s.y, :, w]
        return self.move(part, part, p, AT_LAST, s.to_y)

    def results(self, core, p):
        return [
            self.move(self.inside(self.final.at[p % SLOTS], sub), self.outside(self.result[sub[0]], sub, core), p, AT_RESULT + i, self.spot.sibling)
            for i, sub in enumerate(PARTS[p])
            if sub[-1]
        ]

    def kept(self, core, p):
        return [
            pltpu.make_async_copy(
                self.inside(self.final.at[p % SLOTS], sub), self.outside(self.result[sub[0]], sub, core), self.keep_sem.at[p, i]
            )
            for i, sub in enumerate(PARTS[p])
            if sub[-1]
        ]

    def give(self, core, p):
        for copy in self.given(core, p):
            copy.start()

    def fetch(self, core, p):
        for copy in self.given(core, p):
            copy.wait_recv()
        for copy in self.loads(core, p):
            copy.start()

    def stage_one(self, core, p):
        for copy in self.loads(core, p):
            copy.wait()
        slot, w = p % SLOTS, self.lanes(p)

        def add(i, carry):
            at = (i // 4, i // 2 % 2, i % 2)
            self.sums[slot, at[0], at[1], at[2], :, w] += self.other[p % 2, at[0], at[1], at[2], :, w]
            return carry

        lax.fori_loop(0, 16, add, 0)
        if p >= SLOTS:
            for i in range(5):
                pl.semaphore_wait(self.free.at[i], 1)
        self.first(core, p).start()

    def stage_two(self, core, p):
        s, slot, w = self.spot, p % SLOTS, self.lanes(p)
        self.first(core, p).wait_recv()

        def add(i, carry):
            if core == 0:
                self.sums[slot, i // 2, s.x, i % 2, :, w] += self.one_in[slot, i // 2, i % 2, :, w]
            else:
                self.sums[slot, i // 2, i % 2, s.y, :, w] += self.one_in[slot, i // 2, i % 2, :, w]
            return carry

        lax.fori_loop(0, 8, add, 0)
        if core == 0:
            for k in (1, 3, 2):
                self.hop(core, p, k).start()
        else:
            self.next(core, p).start()

    def stage_three(self, core, p):
        s, slot, w = self.spot, p % SLOTS, self.lanes(p)
        if core == 0:
            for k in (1, 3, 2):
                self.hop(core, p, k).wait_recv()

            def add(i, carry):
                total = self.sums[slot, s.z, s.x, i, :, w].astype(WIDE)
                for k in range(3):
                    total += self.next_in[slot, 2 * k + i, :, w].astype(WIDE)
                self.sums[slot, s.z, s.x, i, :, w] = total.astype(LOW)
                return carry

            lax.fori_loop(0, 2, add, 0)
            self.next(core, p).start()
        else:
            self.next(core, p).wait_recv()

            def add(i, carry):
                self.sums[slot, i, s.x, s.y, :, w] += self.next_in[slot, i, :, w]
                return carry

            lax.fori_loop(0, 4, add, 0)
            for k in (1, 3, 2):
                self.hop(core, p, k).start()

    def stage_four(self, core, p):
        s, slot, w = self.spot, p % SLOTS, self.lanes(p)
        if core == 0:
            self.next(core, p).wait_recv()

            def add(i, carry):
                self.final[slot, i, :, w] = self.sums[slot, s.z, s.x, i, :, w] + self.next_in[slot, 6 + i, :, w]
                return carry

            lax.fori_loop(0, 2, add, 0)
        else:
            for k in (1, 3, 2):
                self.hop(core, p, k).wait_recv()
            total = self.sums[slot, s.z, s.x, s.y, :, w].astype(WIDE)
            for k in range(3):
                total += self.next_in[slot, 4 + k, :, w].astype(WIDE)
            self.final[slot, s.y, :, w] = total.astype(LOW)
            self.last(p, True).start()

    def stage_five(self, core, p):
        if core == 1:
            self.last(p, False).wait_recv()
        for copy in self.results(core, p) + self.kept(core, p):
            copy.start()

    def release(self, core, p):
        self.first(core, p).wait_send()
        for k in (1, 2, 3):
            self.hop(core, p, k).wait_send()
        self.next(core, p).wait_send()
        if core == 1:
            self.last(p, True).wait_send()
        for copy in self.results(core, p):
            copy.wait_send()
        for copy in self.kept(core, p):
            copy.wait()
        if p + SLOTS < len(PARTS):
            s = self.spot
            for i, device in enumerate((s.to_x, s.to_y)):
                pl.semaphore_signal(self.free.at[i], 1, device_id=device, device_id_type=MESH)
            for k in (1, 2, 3):
                pl.semaphore_signal(self.free.at[1 + 4 - k], 1, device_id=s.hop(k), device_id_type=MESH)

    def finish(self, core, p):
        for copy in self.given(core, p):
            copy.wait_send()
        for copy in self.results(1 - core, p):
            copy.wait_recv()

    def program(self):
        count = len(PARTS)
        turns = [[("fetch", 0)]]
        for s in range(count + 7):
            turn = []
            for stage, p in (
                ("stage_one", s),
                ("release", s - 6),
                ("fetch", s + 1),
                ("stage_two", s - 2),
                ("stage_three", s - 3),
                ("stage_four", s - 4),
                ("stage_five", s - 5),
            ):
                if 0 <= p < count:
                    turn.append((stage, p))
            turns.append(turn)
        return turns

    def run(self, steps):
        for core in (0, 1):

            @pl.when(self.spot.core == core)
            def _():
                for stage, p in steps:
                    getattr(self, stage)(core, p)


def norm_backward(grad, i, gain, norms, spreads, small, gradients, gain_row, shift_row):
    unit, inverse = norms[i], spreads[i][:, :1]
    scaled = grad * small[gain : gain + 1]
    gradients[gain_row : gain_row + 1] = jnp.sum(grad * unit, axis=0, keepdims=True)
    gradients[shift_row : shift_row + 1] = jnp.sum(grad, axis=0, keepdims=True)
    centre = jnp.mean(scaled, axis=-1, keepdims=True)
    slope = jnp.mean(scaled * unit, axis=-1, keepdims=True)
    return inverse * (scaled - centre - unit * slope)


def attention_backward(projected, back, context_grad, valid, gradients):
    def pair(i, carry):
        def lanes(at):
            return pl.ds(pl.multiple_of(at * 768 + 128 * i, 128), 128)

        queries, keys, values = (projected[:, lanes(at)] for at in range(3))
        above = context_grad[:, lanes(0)]
        totals = [jnp.zeros((TOKENS, 128), WIDE) for _ in range(3)]
        for which in (0, 1):
            soft = soft_weights(queries, keys, which, valid)
            part = one_head(above, which)
            soft_grad = dot_second(part, values)
            score = soft * (soft_grad - jnp.sum(soft * soft_grad, axis=-1, keepdims=True))
            score = score.astype(LOW)
            totals[0] += dot_plain(score, one_head(keys, which))
            totals[1] += dot_first(score, one_head(queries, which))
            totals[2] += dot_first(soft.astype(LOW), part)
        totals[0] *= 0.125
        totals[1] *= 0.125
        for at in range(3):
            back[:, lanes(at)] = totals[at].astype(LOW)
        gradients[0:1, lanes(0)] = jnp.sum(totals[0], axis=0, keepdims=True)
        gradients[1:2, lanes(0)] = jnp.sum(totals[2], axis=0, keepdims=True)
        return carry

    lax.fori_loop(0, 6, pair, 0)


class Outbox:
    def __init__(self, thin, thick, sems):
        self.thin, self.thick, self.sems = thin, thick, sems
        self.count = 0
        self.flying = {}

    def settle(self, key):
        self.flying.pop(key).wait()

    def settle_all(self):
        for key in list(self.flying):
            self.settle(key)

    def send(self, key, source, target):
        copy = pltpu.make_async_copy(source, target, self.sems.at[key])
        copy.start()
        self.flying[key] = copy

    def room(self):
        key = self.count % THIN
        self.count += 1
        if key in self.flying:
            self.settle(key)
        return key

    def square(self, left, right, target):
        key = self.room()
        for half in (0, 1):
            rows = dot_first(left[:, 384 * half : 384 * half + 384], right).astype(LOW)
            self.thin[key, pl.ds(2 * half, 2)] = rows.reshape(2, 2, 2, 48, 768)
        self.send(key, self.thin.at[key], target)

    def block(self, left, right, target, shape):
        if THIN in self.flying:
            self.settle(THIN)
        rows = shape[0] * shape[1] * shape[2] * shape[3]
        parts = [
            dot_first(left[:, at : at + 384], right).astype(LOW) for at in range(0, rows, 384)
        ]
        self.thick[0 : shape[0], :, :, 0 : shape[3]] = jnp.concatenate(parts, axis=0).reshape(shape)
        self.send(THIN, self.thick.at[0 : shape[0], :, :, 0 : shape[3]], target)


THIN = 2
DENSE_KINDS = tuple(kind for kind in KINDS if kind not in ("CELL", "TABLE"))
SAVED = ("joined", "pooled", "norms", "spreads", "small")


def backward_kernel(per_place, *refs):
    weights = dict(zip(DENSE_KINDS, refs[:6]))
    record_in, cell_in, codes, length_row, hidden, cotangent, valid_keys = refs[6:13]
    saved = dict(zip(SAVED, refs[13:18]))
    early_in = refs[18:22]
    outs = refs[22:]
    result = dict(zip(KINDS, outs[:8]))
    hidden_grad, landing = outs[8:10]
    grads = dict(zip(KINDS, outs[10:18]))
    scratch = outs[18:]
    record, state_grad, pool_grad, total, gradients, grad, inner, back, thin, thick = scratch[:10]
    table_part, columns, shuffle = scratch[10:13]
    buffers = scratch[13:18]
    record_sem, weight_sem, outbox_sem, column_sem = scratch[18:22]
    sems = scratch[22:27]
    late_sem, cell, lengths = scratch[27:30]
    saved.update(zip(EARLY, scratch[30:34]))
    spread_lengths(length_row, lengths)
    spot = Spot(per_place)
    norms, spreads, small = saved["norms"], saved["spreads"], saved["small"]

    def weight_copies(kind):
        source = weights[kind]
        if kind == "MERGE":
            pairs = [(source, record.at[pl.ds(14, 6)])]
        elif kind == "FEED":
            pairs = [(source, record.at[pl.ds(8, 6), :, pl.ds(0, 3072)])]
        elif kind == "STREAM":
            pairs = [(source, record.at[pl.ds(8, 6), :, pl.ds(3072, 1536)])]
        elif kind == "OUT":
            pairs = [(source.at[j, :, pl.ds(0, 768)], record.at[0, :, pl.ds(768 * j, 768)]) for j in range(6)]
        else:
            first, count = (4, 4) if kind == "IN" else (1, 3)
            pairs = [(source.at[:, j], record.at[pl.ds(first, count), :, pl.ds(768 * j, 768)]) for j in range(6)]
        at = DENSE_KINDS.index(kind)
        return [pltpu.make_async_copy(a, b, weight_sem.at[at, j]) for j, (a, b) in enumerate(pairs)]

    late = {name: (source, saved[name]) for name, source in zip(EARLY, early_in)}
    late["cell"] = (cell_in, cell)
    late = {name: pltpu.make_async_copy(*pair, late_sem.at[i]) for i, (name, pair) in enumerate(late.items())}

    def need(kind):
        for copy in weight_copies(kind):
            copy.wait()

    def rows_of(slot):
        return jnp.concatenate([record[slot, :, pl.ds(768 * j, 768)] for j in range(6)], axis=0)

    def record_copy(t):
        return pltpu.make_async_copy(record_in.at[t], record.at[t], record_sem.at[t])

    def fill(first, count):
        for t in range(first, first + count):
            record_copy(t).start()

    for kind in ("MERGE", "STREAM", "FEED", "IN", "OUT", "ATT"):
        for copy in weight_copies(kind):
            copy.start()
    for name in ("active", "slope", "context", "projected", "cell"):
        late[name].start()
    spot.greet()
    reduce = Reduce(spot, grads, landing, buffers, result, sems)
    outbox = Outbox(thin, thick, outbox_sem)
    steps = [step for turn in reduce.program() for step in turn]
    given = set()

    def give(*parts):
        outbox.settle_all()
        reduce.run([("give", p) for p in parts])
        given.update(parts)

    def take(count):
        taken = []
        while steps and len(taken) < count and not (steps[0][0] == "fetch" and steps[0][1] not in given):
            taken.append(steps.pop(0))
        return taken

    def go_on(count):
        reduce.run(take(count))

    gradients[...] = jnp.zeros_like(gradients)
    merged = norm_backward(cotangent[...].astype(WIDE), 2, 12, norms, spreads, small, gradients, 12, 9)
    gradients[8:9] = jnp.sum(merged, axis=0, keepdims=True)
    grad[...] = merged
    merged_low = merged.astype(LOW)
    joined = saved["joined"]
    for k in range(3):
        taps = window(joined, k)
        for half in (0, 1):
            lanes = pl.ds(1536 * k + 768 * half, 768)
            outbox.square(merged_low, taps[:, 768 * half : 768 * half + 768], grads["MERGE"].at[..., lanes])
        give(k)
        if k > 0:
            go_on(PACE[0])
    need("MERGE")
    parts = [
        dot_plain(merged_low, record[pl.ds(14, 6), :, pl.ds(1536 * k, 1536)].reshape(768, 1536)) for k in range(3)
    ]
    joined_grad = parts[1] + shifted(parts[0], False) + shifted(parts[2], True)
    fill(14, 6)
    go_on(PACE[1])
    gradients[6:7] = jnp.sum(joined_grad[:, :768], axis=0, keepdims=True)
    gradients[7:8] = jnp.sum(joined_grad[:, 768:], axis=0, keepdims=True)
    token_low, char_low = joined_grad[:, :768].astype(LOW), joined_grad[:, 768:].astype(LOW)
    second_low = (norms[1] * small[11:12] + small[5:6]).astype(LOW)
    outbox.square(token_low, second_low, grads["STREAM"].at[..., pl.ds(0, 768)])
    outbox.square(char_low, saved["pooled"][...], grads["STREAM"].at[..., pl.ds(768, 768)])
    give(3)
    need("STREAM")
    stream = record[pl.ds(8, 6), :, pl.ds(3072, 1536)].reshape(768, 1536)
    pool_grad[...] = dot_plain(char_low, stream[:, 768:]) / lengths[:, :1].astype(WIDE)
    second_grad = grad[...] + dot_plain(token_low, stream[:, :768])
    two = norm_backward(second_grad, 1, 11, norms, spreads, small, gradients, 11, 5)
    gradients[4:5] = jnp.sum(two, axis=0, keepdims=True)
    grad[...] = two
    two_low = two.astype(LOW)
    late["active"].wait()
    for c in range(4):
        outbox.square(two_low, saved["active"][:, 768 * c : 768 * c + 768], grads["FEED"].at[..., pl.ds(768 * c, 768)])
        if c % 2 == 1:
            give(4 + c // 2)
            go_on(PACE[2])
    need("FEED")
    late["slope"].wait()
    first_low = (norms[0] * small[10:11] + small[3:4]).astype(LOW)
    shuffle[...] = jnp.zeros_like(shuffle)
    for c in range(4):
        lanes = pl.ds(768 * c, 768)
        part = dot_plain(two_low, record[pl.ds(8, 6), :, lanes].reshape(768, 768))
        part = part * saved["slope"][:, lanes].astype(WIDE)
        inner[:, lanes] = part.astype(LOW)
        sums = jnp.sum(part, axis=0, keepdims=True)
        for half in (0, 1):
            at = 768 * c + 384 * half
            done = 0
            while done < 384:
                row, lane = (at + done) // 512, (at + done) % 512
                size = min(512 - lane, 384 - done)
                start = 384 * half + done
                shuffle[row : row + 1, lane : lane + size] = sums[:, start : start + size]
                done += size
        outbox.block(inner[:, lanes], first_low, grads["IN"].at[pl.ds(c, 1)], (1, 2, 2, 192, 768))
        go_on(PACE[3])
    fill(8, 6)
    give(6, 7)
    need("IN")
    first_grad = grad[...]
    for c in range(4):
        first_grad += dot_plain(inner[:, 768 * c : 768 * c + 768], rows_of(4 + c))
    one = norm_backward(first_grad, 0, 10, norms, spreads, small, gradients, 10, 3)
    fill(4, 4)
    go_on(PACE[4])
    gradients[2:3] = jnp.sum(one, axis=0, keepdims=True)
    grad[...] = one
    one_low = one.astype(LOW)
    need("OUT")
    context_grad = dot_plain(one_low, rows_of(0)).astype(LOW)
    inner[:, pl.ds(0, 768)] = context_grad
    late["context"].wait()
    late["projected"].wait()
    attention_backward(saved["projected"], back, inner, key_mask(valid_keys[0]), gradients)
    go_on(PACE[5])
    outbox.square(one_low, saved["context"][...], grads["OUT"].at[..., pl.ds(0, 768)])
    flat = dot_second(shuffle[...].astype(LOW), spread_matrix())
    for c in range(6):
        for j in range(4):
            gradients[13 + j : 14 + j, 128 * c : 128 * c + 128] = flat[c : c + 1, 128 * j : 128 * j + 128]
    columns[:, :, :, :, pl.ds(0, 128)] = jnp.transpose(gradients[...]).astype(LOW).reshape(4, 2, 2, 48, 128)
    columns[:, :, :, :, pl.ds(128, 128)] = jnp.zeros((4, 2, 2, 48, 128), LOW)
    column_copy = pltpu.make_async_copy(columns, grads["OUT"].at[..., pl.ds(768, 256)], column_sem.at[0])
    column_copy.start()
    for i in range(2):
        outbox.block(back[:, pl.ds(1152 * i, 1152)], hidden[...], grads["ATT"].at[pl.ds(2 * i, 2)], (2, 2, 2, 144, 768))
        go_on(PACE[6])
    column_copy.wait()
    give(8, 9)
    need("ATT")
    hidden_back = grad[...]
    for i in range(3):
        hidden_back += dot_plain(back[:, pl.ds(768 * i, 768)], rows_of(1 + i))
    hidden_grad[...] = hidden_back.astype(LOW)
    fill(0, 4)

    late["cell"].wait()
    state_grad[...] = jnp.zeros_like(state_grad)
    total[...] = jnp.zeros_like(total)
    shares = [take(PACE[7]) for _ in range(CHARS)]

    def retreat(i, carry):
        t = CHARS - 1 - i
        record_copy(t).wait()
        gru_backward_step(t, cell, record, state_grad, pool_grad, lengths)
        for k in range(CHARS):
            if shares[k]:

                @pl.when(i == k)
                def _():
                    reduce.run(shares[k])

        return carry

    lax.fori_loop(0, CHARS, retreat, 0)
    for way in (0, 1):
        outbox.settle_all()
        cell_gradient(way, record, thick)
        outbox.send(THIN, thick.at[:, :, :, 0:144], grads["CELL"].at[pl.ds(2 * way, 2)])
        if way == 1:
            give(10, 11, 12)
        go_on(PACE[8])

    def look_up(i, carry):
        table_gradient(i, cell, record, codes, total)
        return carry

    lax.fori_loop(0, CHARS // 4, look_up, 0)
    go_on(PACE[9])
    lax.fori_loop(CHARS // 4, CHARS // 2, look_up, 0)
    table_part[...] = jnp.transpose(total[...]).astype(LOW).reshape((4, 2, 2) + BLOCKS["TABLE"])
    outbox.send(0, table_part, grads["TABLE"])
    give(13)
    reduce.run(steps)
    reduce.run([("finish", p) for p in range(len(PARTS))])


PACE = (1, 1, 1, 1, 2, 2, 2, 1, 7, 7)


def reduce_and_return(whole, saved, record, codes, lengths, hidden, cotangent, valid_keys, per_place):
    in_vmem = pl.BlockSpec(memory_space=pltpu.VMEM)
    anywhere = pl.BlockSpec(memory_space=pl.ANY)
    count = len(PARTS)
    shapes = [jax.ShapeDtypeStruct((2,) + BLOCKS[kind], LOW) for kind in KINDS]
    shapes += [
        jax.ShapeDtypeStruct((TOKENS, 768), LOW),
        jax.ShapeDtypeStruct((count, 4, 2, 2, ROWS, LANES), LOW),
    ]
    shapes += [jax.ShapeDtypeStruct((4, 2, 2) + BLOCKS[kind], LOW) for kind in KINDS]
    views = {
        "ATT": (3, 6, 128, 768),
        "OUT": (6, 128, 1024),
        "IN": (4, 6, 128, 768),
        "FEED": (6, 128, 3072),
        "STREAM": (6, 128, 1536),
        "MERGE": (6, 128, 4608),
    }
    results = pl.pallas_call(
        partial(backward_kernel, per_place),
        out_shape=shapes,
        in_specs=[anywhere] * 8
        + [in_vmem] * 4
        + [pl.BlockSpec(memory_space=pltpu.SMEM)]
        + [in_vmem] * len(SAVED)
        + [anywhere] * len(EARLY),
        out_specs=[anywhere] * 8 + [in_vmem] + [anywhere] * 9,
        scratch_shapes=[
            pltpu.VMEM((CHARS, TOKENS, 2 * RECORD), LOW),
            pltpu.VMEM((TOKENS, 2 * HID), WIDE),
            pltpu.VMEM((TOKENS, 2 * HID), WIDE),
            pltpu.VMEM((1024, EMB), WIDE),
            pltpu.VMEM((128, 768), WIDE),
            pltpu.VMEM((TOKENS, 768), WIDE),
            pltpu.VMEM((TOKENS, 3072), LOW),
            pltpu.VMEM((TOKENS, 2304), LOW),
            pltpu.VMEM((THIN, 4, 2, 2, 48, 768), LOW),
            pltpu.VMEM((2, 2, 2, 192, 768), LOW),
            pltpu.VMEM((4, 2, 2) + BLOCKS["TABLE"], LOW),
            pltpu.VMEM((4, 2, 2, 48, 256), LOW),
            pltpu.VMEM((8, 512), WIDE),
            pltpu.VMEM((SLOTS, 4, 2, 2, ROWS, LANES), LOW),
            pltpu.VMEM((2, 4, 2, 2, ROWS, LANES), LOW),
            pltpu.VMEM((SLOTS, 4, 2, ROWS, LANES), LOW),
            pltpu.VMEM((SLOTS, 8, ROWS, LANES), LOW),
            pltpu.VMEM((SLOTS, 2, ROWS, LANES), LOW),
            pltpu.SemaphoreType.DMA((CHARS,)),
            pltpu.SemaphoreType.DMA((6, 6)),
            pltpu.SemaphoreType.DMA((THIN + 1,)),
            pltpu.SemaphoreType.DMA((1,)),
            pltpu.SemaphoreType.DMA((count, MOVES)),
            pltpu.SemaphoreType.DMA((count, MOVES)),
            pltpu.SemaphoreType.DMA((2, SUBS + 1)),
            pltpu.SemaphoreType.DMA((count, SUBS)),
            pltpu.SemaphoreType.REGULAR((5,)),
            pltpu.SemaphoreType.DMA((len(EARLY) + 1,)),
            pltpu.VMEM((4, 2, 2) + BLOCKS["CELL"], LOW),
            pltpu.VMEM((TOKENS, TOKENS), jnp.int32),
        ]
        + [pltpu.VMEM(shape, kind) for shape, kind in EARLY.values()],
        compiler_params=pltpu.CompilerParams(collective_id=1, has_side_effects=True, vmem_limit_bytes=63 << 20),
    )(
        *[whole[kind].reshape(views[kind]) for kind in DENSE_KINDS],
        record,
        whole["CELL"],
        codes,
        lengths,
        hidden,
        cotangent,
        valid_keys,
        *[saved[name] for name in SAVED],
        *[saved[name] for name in EARLY],
    )
    return dict(zip(KINDS, results[:8])), results[8]


def unpack_kernel(*refs):
    count = len(KINDS)
    sources, passed = refs[:count], refs[count : count + 2]
    targets = refs[count + 2 : count + 17]
    scratch = refs[count + 17 :]
    held, through = dict(zip(KINDS, scratch[:count])), scratch[count : count + 2]
    made, in_sem, out_sem = scratch[count + 2 : count + 15], scratch[count + 15], scratch[count + 16]
    loads = [
        pltpu.make_async_copy(source, target, in_sem.at[i])
        for i, (source, target) in enumerate(zip((*sources, *passed), (*held.values(), *through)))
    ]
    for copy in loads:
        copy.start()
    loads = dict(zip((*KINDS, 0, 1), loads))
    stores = []

    def store(source, i):
        copy = pltpu.make_async_copy(source, targets[i], out_sem.at[i])
        copy.start()
        stores.append(copy)

    def keep(i, value):
        made[i][...] = value
        store(made[i], 2 + i)

    def rows(kind, first, width):
        if kind in loads:
            loads.pop(kind).wait()
        value = held[kind][:, :, pl.ds(first, width)]
        return value.reshape(-1, width).astype(WIDE)

    for i in range(2):
        loads.pop(i).wait()
        store(through[i], i)
    for k in range(3):
        made[10][k] = rows("MERGE", 1536 * k, 1536)
    store(made[10], 12)
    keep(4, rows("FEED", 0, 3072))
    keep(2, jnp.transpose(rows("IN", 0, 768)))
    for k in range(2):
        made[9][k] = rows("STREAM", 768 * k, 768)
    store(made[9], 11)
    keep(0, rows("ATT", 0, 768))
    keep(1, rows("OUT", 0, 768))
    keep(5, rows("TABLE", 0, 1024)[:, :1000])
    keep(6, rows("CELL", 0, EMB))
    keep(7, rows("CELL", EMB, HID))
    keep(8, jnp.transpose(rows("CELL", EMB + HID, 128))[:2])
    small = jnp.transpose(rows("OUT", 768, 128))
    keep(11, small[10:13])
    keep(12, small[:10])
    low = small[8:24].astype(LOW)
    size = low.shape[1]
    row = lax.broadcasted_iota(jnp.int32, (size, 4 * size), 0)
    lane = lax.broadcasted_iota(jnp.int32, (size, 4 * size), 1)
    flat = jnp.zeros((1, 4 * size), WIDE)
    for j in range(4):
        flat += dot_plain(low, (4 * row + j == lane).astype(LOW))[5 + j : 6 + j]
    keep(3, flat)
    for copy in stores:
        copy.wait()


def unpack(final, output, hidden_grad):
    shapes = [
        (288, 768), (96, 768), (768, 384), (1, 384), (96, 3072), (32, 1000), (288, EMB), (288, HID), (2, 288),
        (2, 96, 768), (3, 96, 1536), (3, 96), (10, 96),
    ]
    anywhere = pl.BlockSpec(memory_space=pl.ANY)
    count = len(KINDS)
    results = pl.pallas_call(
        unpack_kernel,
        out_shape=[jax.ShapeDtypeStruct((TOKENS, 768), LOW)] * 2 + [jax.ShapeDtypeStruct(shape, WIDE) for shape in shapes],
        in_specs=[anywhere] * (count + 2),
        out_specs=[anywhere] * (2 + len(shapes)),
        scratch_shapes=[pltpu.VMEM((2,) + BLOCKS[kind], LOW) for kind in KINDS]
        + [pltpu.VMEM((TOKENS, 768), LOW)] * 2
        + [pltpu.VMEM(shape, WIDE) for shape in shapes]
        + [pltpu.SemaphoreType.DMA((count + 2,)), pltpu.SemaphoreType.DMA((2 + len(shapes),))],
        compiler_params=pltpu.CompilerParams(vmem_limit_bytes=60 << 20),
    )(*[final[kind] for kind in KINDS], output, hidden_grad)
    att, out, feed_in, feed_bias, feed, table, cell_in, cell_back, cell_bias, stream, merge, gains, biases = results[2:]
    return (
        results[0],
        results[1],
        att.T,
        out.T,
        feed_in,
        feed_bias.reshape(-1),
        feed.T,
        table.T,
        cell_in.T,
        cell_back.T,
        cell_bias,
        jnp.swapaxes(stream, 1, 2),
        jnp.swapaxes(merge, 1, 2),
        gains,
        biases,
    )


def shards(hidden, char_codes, word_length, sequence_length, cotangent, *parameters):
    wide = lax.axis_size("wide")
    per_place = wide // 2
    starts = pack(parameters, per_place)
    codes = jnp.transpose(char_codes)
    lengths = word_length[None, :]
    whole, record, saved = gather_and_read(starts, codes, lengths, hidden, sequence_length, per_place)
    final, hidden_grad = reduce_and_return(
        whole, saved, record, codes, lengths, hidden, cotangent, sequence_length, per_place
    )
    return unpack(final, saved["output"], hidden_grad)


def solution(mesh):
    rows = P(("grp", "wide"), None)
    flat = P(("grp", "wide"))
    last = P(None, ("grp", "wide"))
    deep = P(None, None, ("grp", "wide"))
    in_specs = (rows, rows, flat, flat, rows, last, last, last, flat, last, last, last, last, last, deep, deep, last, last)
    out_specs = (rows, rows) + (P(None, "grp"),) * 3 + (P("grp"),) + (P(None, "grp"),) * 5 + (P(None, None, "grp"),) * 2 + (P(None, "grp"),) * 2
    return jax.shard_map(shards, mesh=mesh, in_specs=in_specs, out_specs=out_specs, check_vma=False)
```

```python
from functools import partial

import jax
import jax.numpy as jnp
from jax import lax
from jax.experimental import pallas as pl
from jax.experimental.pallas import tpu as pltpu
from jax.sharding import PartitionSpec as P

HEADS = 12
HID = 384
EMB = 256
CHARS = 20
TOKENS = 128
norm_eps = 1e-05
masked_score = -1e30
MESH = pl.DeviceIdType.MESH
EVERY = slice(None)
LOW = jnp.bfloat16
WIDE = jnp.float32

BLOCKS = {
    "CELL": (144, 768),
    "TABLE": (16, 1024),
    "ATT": (144, 768),
    "OUT": (48, 1024),
    "IN": (192, 768),
    "FEED": (48, 3072),
    "STREAM": (48, 1536),
    "MERGE": (48, 4608),
}
KINDS = tuple(BLOCKS)
STARTS = (
    ("CELL", 0, 256, 1),
    ("CELL", 256, 384, 1),
    ("CELL", 640, 128, 1),
    ("TABLE", 0, 1000, 1),
    ("ATT", 0, 768, 1),
    ("OUT", 0, 768, 1),
    ("OUT", 768, 128, 1),
    ("IN", 0, 768, 1),
    ("FEED", 0, 3072, 1),
    ("STREAM", 0, 768, 2),
    ("MERGE", 0, 1536, 3),
)
PIECES = (
    ("CELL", 0, 384, 128, True),
    ("CELL", 128, 512, 256, True),
    ("TABLE", 0, 512, 512, False),
    ("ATT", 0, 384, 384, False),
    ("OUT", 0, 512, 512, True),
    ("IN", 0, 128, 128, False),
    ("IN", 256, 512, 256, False),
    ("FEED", 0, 768, 768, False),
    ("FEED", 1536, 2304, 768, True),
    ("STREAM", 0, 768, 768, False),
    ("MERGE", 0, 768, 768, False),
    ("MERGE", 1536, 2304, 768, True),
    ("MERGE", 3072, 3840, 768, False),
)
GATHER_MOVES = 11
AHEAD = 3
LAGS = (0, 2, 4, 6)

X_WIDTH = 768
RECORD = X_WIDTH + 4 * HID
GATE_R, GATE_Z, GATE_N, GATE_Q = (X_WIDTH + i * HID for i in range(4))


def dot_plain(left_side, right_side):
    return jnp.dot(left_side, right_side, preferred_element_type=WIDE)


def dot_first(left_side, right_side):
    return lax.dot_general(left_side, right_side, (((0,), (0,)), ((), ())), preferred_element_type=WIDE)


def dot_second(left_side, right_side):
    return lax.dot_general(left_side, right_side, (((1,), (1,)), ((), ())), preferred_element_type=WIDE)


def lanes_of(ref, start, width):
    return ref[:, pl.ds(start, width)]


def sigmoid(inputs):
    return 0.5 * jnp.tanh(0.5 * inputs) + 0.5


class Spot:
    def __init__(self, per_place):
        self.grp, self.wide = lax.axis_index("grp"), lax.axis_index("wide")
        self.z, self.x = self.grp // 2, self.grp % 2
        self.y, self.core = self.wide // per_place, self.wide % 2
        self.to_x = (self.grp + 1 - 2 * self.x, self.wide)
        self.to_y = (self.grp, self.wide + per_place - 2 * per_place * self.y)
        self.sibling = (self.grp, self.wide + 1 - 2 * self.core)

    def hop(self, k):
        return (2 * ((self.z + k) % 4) + self.x, self.wide)

    def greet(self):
        barrier = pltpu.get_barrier_semaphore()
        for other in [self.to_x, self.to_y, self.sibling] + [self.hop(k) for k in (1, 2, 3)]:
            pl.semaphore_signal(barrier, 1, device_id=other, device_id_type=MESH)
        pl.semaphore_wait(barrier, 6)

    def near(self, core):
        if core == 0:
            return self.x, self.y, self.to_x, self.to_y
        return self.y, self.x, self.to_y, self.to_x


def remote(source, target, sent, received, device):
    return pltpu.make_async_remote_copy(
        src_ref=source, dst_ref=target, send_sem=sent, recv_sem=received, device_id=device, device_id_type=MESH
    )


class Gather:
    def __init__(self, spot, whole, sems):
        self.spot, self.whole = spot, whole
        self.sent, self.got = sems

    def region(self, core, p, z, f, l):
        kind, first, second, width, _ = PIECES[p]
        lanes = pl.ds((first, second)[core], width)
        return self.whole[kind].at[z, f, l, :, lanes] if core == 0 else self.whole[kind].at[z, l, f, :, lanes]

    def move(self, part, p, j, device, at_sent=None):
        return remote(part, part, self.sent.at[p, j if at_sent is None else at_sent], self.got.at[p, j], device)

    def hop_part(self, core, p, z):
        f, l, _, _ = self.spot.near(core)
        return self.region(core, p, z, f if PIECES[p][4] else EVERY, l)

    def near_part(self, core, p, mine):
        f, l, _, _ = self.spot.near(core)
        return self.region(core, p, EVERY if PIECES[p][4] else self.spot.z, f if mine else 1 - f, l)

    def far_part(self, core, p, mine):
        _, l, _, _ = self.spot.near(core)
        return self.region(core, p, EVERY, EVERY, l if mine else 1 - l)

    def hop(self, core, p, k):
        return self.move(self.hop_part(core, p, self.spot.z), p, k - 1, self.spot.hop(k))

    def hop_in(self, core, p, k):
        return self.move(self.hop_part(core, p, (self.spot.z + 4 - k) % 4), p, k - 1, self.spot.hop(k))

    def relay(self, core, p, z):
        if z == 2:
            return self.move(self.hop_part(core, p, 0), p, 2, self.spot.hop(1), 10)
        return self.move(self.hop_part(core, p, 3), p, 0, self.spot.hop(3), 10)

    def near(self, core, p, mine):
        return self.move(self.near_part(core, p, mine), p, 3, self.spot.near(core)[2])

    def far(self, core, p, mine):
        return self.move(self.far_part(core, p, mine), p, 4, self.spot.near(core)[3])

    def aside(self, core, p, j):
        if j < 3:
            part = self.hop_part(core, p, (self.spot.z + 3 - j) % 4)
        else:
            part = self.near_part(core, p, False) if j == 3 else self.far_part(core, p, False)
        return self.move(part, p, 5 + j, self.spot.sibling)

    def own_hops(self, core, p, act):
        for k, end in ((2, None), (1, 3), (3, 0)):
            if end is None:
                act(self.hop(core, p, k))
            else:

                @pl.when(self.spot.z != end)
                def _():
                    act(self.hop(core, p, k))

    def relays(self, core, p, act):
        for z in (1, 2):

            @pl.when(self.spot.z == z)
            def _():
                act(self.relay(core, p, z))

    def start_hops(self, core, p):
        self.own_hops(core, p, lambda copy: copy.start())

    def take_hops(self, core, p):
        self.hop_in(core, p, 2).wait_recv()
        self.relays(core, p, lambda copy: copy.start())
        for k in (1, 3):
            self.hop_in(core, p, k).wait_recv()

    def start(self, core, p):
        if PIECES[p][4]:
            self.start_hops(core, p)
        else:
            self.near(core, p, True).start()

    def second(self, core, p):
        if PIECES[p][4]:
            self.take_hops(core, p)
            self.near(core, p, True).start()
            for j in (0, 2, 1):
                self.aside(core, p, j).start()
        else:
            self.near(core, p, False).wait_recv()
            self.start_hops(core, p)
            self.aside(core, p, 3).start()

    def third(self, core, p):
        if PIECES[p][4]:
            self.near(core, p, False).wait_recv()
            self.far(core, p, True).start()
            self.aside(core, p, 3).start()
        else:
            self.take_hops(core, p)
            self.far(core, p, True).start()
            for j in (0, 2, 1):
                self.aside(core, p, j).start()

    def fourth(self, core, p):
        self.far(core, p, False).wait_recv()
        self.aside(core, p, 4).start()

    def fifth(self, core, p):
        for j in range(5):
            self.aside(1 - core, p, j).wait_recv()

    def drain(self, core, p):
        self.own_hops(core, p, lambda copy: copy.wait_send())
        self.relays(core, p, lambda copy: copy.wait_send())
        self.near(core, p, True).wait_send()
        self.far(core, p, True).wait_send()
        for j in range(5):
            self.aside(core, p, j).wait_send()

    def turns(self):
        count = len(PIECES)
        turns = []
        for s in range(count + LAGS[-1]):
            ahead = range(AHEAD + 1) if s == 0 else [s + AHEAD]
            turn = [("start", p) for p in ahead if p < count]
            for lag, stage in zip(LAGS, ("second", "third", "fourth", "fifth")):
                if 0 <= s - lag < count:
                    turn.append((stage, s - lag))
            turns.append(turn)
        return turns

    def run(self, steps):
        for core in (0, 1):

            @pl.when(self.spot.core == core)
            def _():
                for stage, p in steps:
                    getattr(self, stage)(core, p)


RING = 4


def gru_forward_step(t, cell, spelled, record, state, total, shifts, lengths):
    slot = t % RING
    for way in (0, 1):
        base = way * RECORD
        place = t if way == 0 else CHARS - 1 - t
        live = lengths[:, :1] > place
        lanes = pl.ds(way * HID, HID)
        h = state[:, lanes]
        record[slot, :, pl.ds(base, EMB)] = spelled[place]
        record[slot, :, pl.ds(base + EMB, HID)] = h.astype(LOW)
        x = record[slot, :, pl.ds(base, X_WIDTH)]
        weights = cell[pl.ds(2 * way, 2)].reshape(3 * HID, X_WIDTH)
        both = dot_second(x, weights[: 2 * HID])
        drive_n = dot_second(x[:, :EMB], weights[2 * HID :, :EMB]) + shifts[way, 0:1]
        recur_n = dot_second(x[:, EMB : EMB + HID], weights[2 * HID :, EMB : EMB + HID]) + shifts[way, 1:2]
        r = sigmoid(both[:, :HID])
        u = sigmoid(both[:, HID:])
        n = jnp.tanh(drive_n + r * recur_n)
        fresh = jnp.where(live, n + u * (h - n), h)
        state[:, lanes] = fresh
        total[:, lanes] += jnp.where(live, fresh, 0.0)
        record[slot, :, pl.ds(base + GATE_R, HID)] = r.astype(LOW)
        record[slot, :, pl.ds(base + GATE_Z, HID)] = u.astype(LOW)
        record[slot, :, pl.ds(base + GATE_N, HID)] = n.astype(LOW)
        record[slot, :, pl.ds(base + GATE_Q, HID)] = recur_n.astype(LOW)


def spread_matrix():
    shape = (512, 512)
    row, lane = lax.broadcasted_iota(jnp.int32, shape, 0), lax.broadcasted_iota(jnp.int32, shape, 1)
    return (4 * (row % 128) + row // 128 == lane).astype(LOW)


def read_small(out, small, feed_row, shuffle):
    columns = out[:, :, :, :, pl.ds(768, 128)].reshape(768, 128).astype(WIDE)
    rows = jnp.transpose(columns)
    small[...] = rows[:32]
    shuffle[...] = jnp.zeros_like(shuffle)
    for c in range(6):
        for j in range(4):
            shuffle[c : c + 1, 128 * j : 128 * j + 128] = rows[13 + j : 14 + j, 128 * c : 128 * c + 128]
    flat = dot_plain(shuffle[...].astype(LOW), spread_matrix())
    for c in range(6):
        feed_row[:, 512 * c : 512 * c + 512] = flat[c : c + 1]


def norm_forward(inputs, i, small, gain, shift, norms, spreads):
    centred = inputs - jnp.mean(inputs, axis=-1, keepdims=True)
    inverse = lax.rsqrt(jnp.mean(centred * centred, axis=-1, keepdims=True) + norm_eps)
    unit = centred * inverse
    norms[i] = unit
    spreads[i] = jnp.broadcast_to(inverse, spreads.shape[1:])
    return unit * small[gain : gain + 1] + small[shift : shift + 1]


def head_mask(which):
    lane = lax.broadcasted_iota(jnp.int32, (TOKENS, 128), 1)
    return (lane < 64) if which == 0 else (lane >= 64)


def one_head(pair, which):
    return jnp.where(head_mask(which), pair, jnp.zeros_like(pair))


def soft_weights(queries, keys, which, valid):
    scores = dot_second(one_head(queries, which), keys) * 0.125 + valid
    weight = jnp.exp(scores - jnp.max(scores, axis=-1, keepdims=True))
    return weight / jnp.sum(weight, axis=-1, keepdims=True)


def key_mask(count):
    lane = lax.broadcasted_iota(jnp.int32, (TOKENS, TOKENS), 1)
    return jnp.where(lane < count, 0.0, masked_score).astype(WIDE)


def attention_forward(projected, context, valid):
    def pair(i, carry):
        def part(at):
            return projected[:, pl.ds(pl.multiple_of(at * 768 + 128 * i, 128), 128)]

        queries, keys, values = part(0), part(1), part(2)
        total = jnp.zeros((TOKENS, 128), WIDE)
        for which in (0, 1):
            soft = soft_weights(queries, keys, which, valid).astype(LOW)
            total += dot_plain(soft, one_head(values, which))
        context[:, pl.ds(pl.multiple_of(128 * i, 128), 128)] = total.astype(LOW)
        return carry

    lax.fori_loop(0, 6, pair, 0)


def shifted(rows, down):
    turned = pltpu.roll(rows, 1 if down else TOKENS - 1, 0)
    row = lax.broadcasted_iota(jnp.int32, rows.shape, 0)
    return jnp.where(row == (0 if down else TOKENS - 1), 0.0, turned)


def window(joined, k):
    if k == 1:
        return joined[...]
    return shifted(joined[...].astype(WIDE), k == 0).astype(LOW)


def spread_lengths(row, column):
    square = jnp.broadcast_to(row[...].astype(WIDE), (TOKENS, TOKENS))
    column[...] = jnp.transpose(square).astype(jnp.int32)


def forward_kernel(per_place, *refs):
    count = len(KINDS)
    starts = refs[: len(STARTS)]
    codes, length_row, hidden, valid_keys = refs[len(STARTS) : len(STARTS) + 4]
    outs = refs[len(STARTS) + 4 :]
    kept = dict(zip(KINDS, outs[:count]))
    record_out, output, joined, pooled_low, norms, spreads, small = outs[count : count + 7]
    early_out = outs[count + 7 : count + 11]
    scratch = outs[count + 11 :]
    whole = dict(zip(KINDS, scratch[:count]))
    (record, spelled, state, pooled, shifts, feed_row, shuffle, first, second, merged, sent, got, own_sent, own_got, kept_sem, record_sem, early_sem) = scratch[count : count + 17]
    lengths = scratch[3 * count + 17]
    projected, context, active, slope = early = scratch[3 * count + 18 :]
    spread_lengths(length_row, lengths)
    mine, theirs = (dict(zip(KINDS, scratch[at : at + count])) for at in (count + 17, 2 * count + 17))
    spot = Spot(per_place)
    halves = per_place == 2

    def lay(kind):
        if kind in ("TABLE", "OUT"):
            mine[kind][...] = jnp.zeros_like(mine[kind])
        for ref, (owner, first, width, parts) in zip(starts, STARTS):
            if owner != kind:
                continue
            for part in range(parts):
                rows = ref[...] if parts == 1 else ref[part]
                lanes = pl.ds(first + part * width, width)
                if not halves:
                    mine[kind][:, lanes] = rows
                    continue
                rows = rows.astype(WIDE)
                blank = jnp.zeros_like(rows)
                low = jnp.where(spot.core == 0, rows, blank)
                high = jnp.where(spot.core == 0, blank, rows)
                mine[kind][:, lanes] = jnp.concatenate([low, high], axis=0).astype(LOW)

    def swap(kind):
        at = KINDS.index(kind)
        return remote(mine[kind], theirs[kind], own_sent.at[at], own_got.at[at], spot.sibling)

    def ready(kind):
        if halves:
            swap(kind).wait_recv()
            whole[kind][spot.z, spot.x, spot.y] = mine[kind][...] + theirs[kind][...]
        else:
            whole[kind][spot.z, spot.x, spot.y] = mine[kind][...]

    for kind in KINDS[:3]:
        lay(kind)
    spot.greet()
    for kind in KINDS[:3]:
        if halves:
            swap(kind).start()
    for kind in KINDS[3:]:
        lay(kind)
        if halves:
            swap(kind).start()
    gather = Gather(spot, whole, (sent, got))
    turns = gather.turns()

    def keep(kind, part=None):
        at = KINDS.index(kind)
        if part is None:
            return pltpu.make_async_copy(whole[kind], kept[kind], kept_sem.at[at])
        lanes = pl.ds(1536 * part, 1536)
        return pltpu.make_async_copy(whole[kind].at[..., lanes], kept[kind].at[..., lanes], kept_sem.at[at + part])

    def weights(kind):
        value = whole[kind][...]
        return value.reshape(-1, value.shape[-1])

    last_of = {kind: max(p for p, piece in enumerate(PIECES) if piece[0] == kind) for kind in KINDS}
    steps = [step for turn in turns for step in turn]

    def after(kind):
        return steps.index(("fifth", last_of[kind])) + 1

    lead = max(after("CELL"), after("TABLE"))
    waiting = list(KINDS)
    for stage, p in steps[:lead]:
        if stage == "start" and PIECES[p][0] in waiting:
            ready(PIECES[p][0])
            waiting.remove(PIECES[p][0])
        gather.run([(stage, p)])
    for kind in waiting:
        ready(kind)
    for kind in ("CELL", "TABLE"):
        keep(kind).start()
    cell, table = whole["CELL"], weights("TABLE")

    def embed(c, carry):
        which = (lax.broadcasted_iota(jnp.int32, (1024, TOKENS), 0) == codes[pl.ds(c, 1)]).astype(LOW)
        spelled[c] = jnp.transpose(dot_plain(table, which)).astype(LOW)
        return carry

    lax.fori_loop(0, CHARS, embed, 0)
    pick = (
        lax.broadcasted_iota(jnp.int32, (8, 128), 0) == lax.broadcasted_iota(jnp.int32, (8, 128), 1)
    ).astype(LOW)
    ones = (lax.broadcasted_iota(jnp.int32, (TOKENS, 128), 1) < 2).astype(LOW)
    for way in (0, 1):
        late = cell[pl.ds(2 * way, 2)].reshape(3 * HID, X_WIDTH)[2 * HID :, EMB + HID :]
        shifts[way] = dot_second(pick, late)
        for slot in range(RING):
            record[slot, :, pl.ds(way * RECORD + EMB + HID, 128)] = ones
    state[...] = jnp.zeros_like(state)
    pooled[...] = jnp.zeros_like(pooled)

    def attend():
        for kind in ("ATT", "OUT"):
            keep(kind).start()
        read_small(whole["OUT"], small, feed_row, shuffle)
        attention_in = weights("ATT")
        for i, bias in enumerate((0, None, 1)):
            block = dot_second(hidden[...], attention_in[768 * i : 768 * i + 768])
            if bias is not None:
                block = block + small[bias : bias + 1]
            projected[:, 768 * i : 768 * i + 768] = block.astype(LOW)
        attention_forward(projected, context, key_mask(valid_keys[0]))
        store(0).start()
        store(1).start()

    def add_attended():
        attended = dot_second(context[...], weights("OUT")[:, :768]) + small[2:3]
        first[...] = norm_forward(hidden[...].astype(WIDE) + attended, 0, small, 10, 3, norms, spreads)

    def feed(c):
        if c == 0:
            keep("IN").start()
        rows = whole["IN"][c].reshape(768, 768)
        inner = dot_second(first[...].astype(LOW), rows) + feed_row[:, 768 * c : 768 * c + 768]
        share_below = 0.5 * (1.0 + lax.erf(inner * 0.7071067811865476))
        active[:, 768 * c : 768 * c + 768] = (inner * share_below).astype(LOW)
        slope[:, 768 * c : 768 * c + 768] = (
            share_below + inner * (0.3989422804014327 * jnp.exp(-0.5 * inner * inner))
        ).astype(LOW)

    def feed_back():
        store(2).start()
        store(3).start()
        keep("FEED").start()
        two = first[...] + dot_second(active[...], weights("FEED")) + small[4:5]
        second[...] = norm_forward(two, 1, small, 11, 5, norms, spreads)

    def token_side():
        stream = whole["STREAM"][:, :, :, :, pl.ds(0, 768)].reshape(768, 768)
        joined[:, :768] = (dot_second(second[...].astype(LOW), stream) + small[6:7]).astype(LOW)

    def store(i):
        return pltpu.make_async_copy(early[i], early_out[i], early_sem.at[i])

    def record_copy(t):
        return pltpu.make_async_copy(record.at[t % RING], record_out.at[t], record_sem.at[t % RING])

    jobs = [(after("OUT"), attend), (0, add_attended)]
    jobs += [(after("IN"), partial(feed, c)) for c in range(4)]
    jobs += [(after("FEED"), feed_back), (after("STREAM"), token_side)]
    shares = [lead + -(-(GRU_END - lead) * (k + 1) // CHARS) for k in range(CHARS)]
    during = {k: [] for k in range(CHARS)}
    late_jobs = []
    at = 0
    for need, job in jobs:
        ready = [k for k in range(CHARS) if shares[k] >= need]
        at = max([at] + ready[:1]) if ready else CHARS
        if at < CHARS:
            during[at].append(job)
            at += 1
        else:
            late_jobs.append((need, job))

    def advance(t, carry):
        @pl.when(t >= RING)
        def _():
            record_copy(t - RING).wait()

        gru_forward_step(t, cell, spelled, record, state, pooled, shifts, lengths)
        record_copy(t).start()
        for k in range(CHARS):
            part = steps[shares[k - 1] if k else lead : shares[k]]
            if part or during[k]:

                @pl.when(t == k)
                def _():
                    gather.run(part)
                    for job in during[k]:
                        job()

        return carry

    lax.fori_loop(0, CHARS, advance, 0)
    pooled_low[...] = (pooled[...] / lengths[:, :1].astype(WIDE)).astype(LOW)
    done = shares[-1]
    for need, job in late_jobs:
        gather.run(steps[done:need])
        done = max(done, need)
        job()
    gather.run(steps[done : after("STREAM")])
    done = max(done, after("STREAM"))
    keep("STREAM").start()
    stream = whole["STREAM"][:, :, :, :, pl.ds(768, 768)].reshape(768, 768)
    joined[:, 768:] = (dot_second(pooled_low[...], stream) + small[7:8]).astype(LOW)
    taps_at = [p for p, piece in enumerate(PIECES) if piece[0] == "MERGE"]
    for k in range(3):
        until = steps.index(("fifth", taps_at[k])) + 1
        gather.run(steps[done:until])
        done = max(done, until)
        keep("MERGE", k).start()
        taps = whole["MERGE"][:, :, :, :, pl.ds(1536 * k, 1536)].reshape(768, 1536)
        part = dot_second(window(joined, k), taps)
        merged[...] = part if k == 0 else merged[...] + part
    third = second[...] + merged[...] + small[8:9]
    output[...] = norm_forward(third, 2, small, 12, 9, norms, spreads).astype(LOW)

    def landed(t, carry):
        record_copy(t).wait()
        return carry

    lax.fori_loop(CHARS - RING, CHARS, landed, 0)
    gather.run([("drain", p) for p in range(len(PIECES))])
    for i in range(len(EARLY)):
        store(i).wait()
    for kind in KINDS:
        for part in range(3) if kind == "MERGE" else (None,):
            keep(kind, part).wait()
        if halves:
            swap(kind).wait_send()


GRU_END = 62
EARLY = {
    "projected": ((TOKENS, 2304), LOW),
    "context": ((TOKENS, 768), LOW),
    "active": ((TOKENS, 3072), LOW),
    "slope": ((TOKENS, 3072), LOW),
}


def gather_and_read(starts, codes, lengths, hidden, valid_keys, per_place):
    count = len(KINDS)
    in_vmem = pl.BlockSpec(memory_space=pltpu.VMEM)
    anywhere = pl.BlockSpec(memory_space=pl.ANY)
    whole_shapes = [(4, 2, 2) + BLOCKS[kind] for kind in KINDS]
    saved = {
        "output": ((TOKENS, 768), LOW),
        "joined": ((TOKENS, 1536), LOW),
        "pooled": ((TOKENS, 768), LOW),
        "norms": ((3, TOKENS, 768), WIDE),
        "spreads": ((3, TOKENS, 128), WIDE),
        "small": ((32, 768), WIDE),
        **EARLY,
    }
    results = pl.pallas_call(
        partial(forward_kernel, per_place),
        out_shape=[jax.ShapeDtypeStruct(shape, LOW) for shape in whole_shapes]
        + [jax.ShapeDtypeStruct((CHARS, TOKENS, 2 * RECORD), LOW)]
        + [jax.ShapeDtypeStruct(shape, kind) for shape, kind in saved.values()],
        in_specs=[in_vmem] * (len(STARTS) + 3) + [pl.BlockSpec(memory_space=pltpu.SMEM)],
        out_specs=[anywhere] * (count + 1) + [in_vmem] * (len(saved) - len(EARLY)) + [anywhere] * len(EARLY),
        scratch_shapes=[pltpu.VMEM(shape, LOW) for shape in whole_shapes]
        + [
            pltpu.VMEM((RING, TOKENS, 2 * RECORD), LOW),
            pltpu.VMEM((CHARS, TOKENS, EMB), LOW),
            pltpu.VMEM((TOKENS, 2 * HID), WIDE),
            pltpu.VMEM((TOKENS, 2 * HID), WIDE),
            pltpu.VMEM((2, 8, HID), WIDE),
            pltpu.VMEM((1, 3072), WIDE),
            pltpu.VMEM((8, 512), WIDE),
            pltpu.VMEM((TOKENS, 768), WIDE),
            pltpu.VMEM((TOKENS, 768), WIDE),
            pltpu.VMEM((TOKENS, 768), WIDE),
            pltpu.SemaphoreType.DMA((len(PIECES), GATHER_MOVES)),
            pltpu.SemaphoreType.DMA((len(PIECES), GATHER_MOVES)),
            pltpu.SemaphoreType.DMA((count,)),
            pltpu.SemaphoreType.DMA((count,)),
            pltpu.SemaphoreType.DMA((count + 2,)),
            pltpu.SemaphoreType.DMA((RING,)),
            pltpu.SemaphoreType.DMA((len(EARLY),)),
        ]
        + [pltpu.VMEM(BLOCKS[kind], LOW) for kind in KINDS + KINDS]
        + [pltpu.VMEM((TOKENS, TOKENS), jnp.int32)]
        + [pltpu.VMEM(shape, kind) for shape, kind in EARLY.values()],
        compiler_params=pltpu.CompilerParams(collective_id=0, has_side_effects=True, vmem_limit_bytes=60 << 20),
    )(*starts, codes, lengths, hidden, valid_keys)
    return dict(zip(KINDS, results[:count])), results[count], dict(zip(saved, results[count + 1 :]))


def pack(shards, per_place):
    (attention_in, attention_out, feed_in, feed_bias, feed_out, char_table, cell_input, cell_recurrent, cell_bias,
     stream_weight, merging_kernel, norm_gains, biases) = shards

    def lanes(parts, width):
        together = jnp.concatenate(parts, axis=1)
        return jnp.pad(together, ((0, 0), (0, width - together.shape[1])))

    rows = attention_out.shape[1]
    starts = [
        cell_input.T,
        cell_recurrent.T,
        lanes([cell_bias.T], 128),
        char_table.T,
        attention_in.T,
        attention_out.T,
        lanes([biases.T, norm_gains.T, feed_bias.reshape(rows, 4)], 128),
        feed_in.T,
        feed_out.T,
        jnp.swapaxes(stream_weight, 1, 2),
        jnp.swapaxes(merging_kernel, 1, 2),
    ]
    if per_place == 2:
        return starts
    size = lax.axis_size("wide")
    groups = [list(range(i, i + per_place)) for i in range(0, size, per_place)]
    return [
        lax.all_gather(part, "wide", axis=part.ndim - 2, tiled=True, axis_index_groups=groups) for part in starts
    ]


def gru_backward_step(t, cell, record, state_grad, pool_grad, lengths):
    for way in (0, 1):
        base = way * RECORD
        place = t if way == 0 else CHARS - 1 - t
        live = lengths[:, :1] > place
        lanes = pl.ds(way * HID, HID)

        def saved(at):
            return record[t, :, pl.ds(base + at, HID)].astype(WIDE)

        r, u, n, recur_n, h = saved(GATE_R), saved(GATE_Z), saved(GATE_N), saved(GATE_Q), saved(EMB)
        grad = state_grad[:, lanes]
        fresh = jnp.where(live, grad + pool_grad[:, lanes], 0.0)
        kept = jnp.where(live, 0.0, grad)
        grad_n = fresh * (1.0 - u) * (1.0 - n * n)
        grad_z = fresh * (h - n) * u * (1.0 - u)
        grad_r = grad_n * recur_n * r * (1.0 - r)
        low_r, low_z, low_n, low_q = (v.astype(LOW) for v in (grad_r, grad_z, grad_n, grad_n * r))
        record[t, :, pl.ds(base + GATE_R, HID)] = low_r
        record[t, :, pl.ds(base + GATE_Z, HID)] = low_z
        record[t, :, pl.ds(base + GATE_N, HID)] = low_n
        record[t, :, pl.ds(base + GATE_Q, HID)] = low_q
        weights = cell[pl.ds(2 * way, 2)].reshape(3 * HID, X_WIDTH)[:, EMB : EMB + HID]
        gates = jnp.concatenate([low_r, low_z, low_q], axis=1)
        state_grad[:, lanes] = kept + fresh * u + dot_plain(gates, weights)


def cell_gradient(way, record, result):
    base = way * RECORD
    rows = CHARS * TOKENS

    def every(at, width):
        return record[:, :, pl.ds(base + at, width)].reshape(rows, width)

    x = every(0, X_WIDTH)
    parts = [dot_first(every(at, HID), x).astype(LOW) for at in (GATE_R, GATE_Z)]
    ends = EMB + HID
    drive, recur = every(GATE_N, HID), every(GATE_Q, HID)
    late = dot_first(recur, x[:, EMB:])
    lane = lax.broadcasted_iota(jnp.int32, (HID, 128), 1)
    shift = jnp.where(lane == 0, dot_first(drive, x[:, ends:]), late[:, HID:])
    parts.append(jnp.concatenate([dot_first(drive, x[:, :EMB]), late[:, :HID], shift], axis=1).astype(LOW))
    result[:, :, :, 0:144] = jnp.concatenate(parts, axis=0).reshape(2, 2, 2, 144, X_WIDTH)


def table_gradient(i, cell, record, codes, result):
    c = 2 * i

    def drive(way, t):
        gates = record[pl.ds(t, 2), :, pl.ds(way * RECORD + GATE_R, 3 * HID)].reshape(2 * TOKENS, 3 * HID)
        return dot_plain(gates, cell[pl.ds(2 * way, 2)].reshape(3 * HID, X_WIDTH)[:, :EMB])

    behind = drive(1, CHARS - 2 - c)
    both = drive(0, c) + jnp.concatenate([behind[TOKENS:], behind[:TOKENS]], axis=0)
    character = lax.broadcasted_iota(jnp.int32, (1024, TOKENS), 0)
    which = [(character == codes[pl.ds(c + k, 1)]).astype(LOW) for k in (0, 1)]
    result[...] += dot_plain(jnp.concatenate(which, axis=1), both.astype(LOW))


ROWS, LANES = 48, 768
PARTS = (
    [("MERGE", 0, 48, 0, 768, 768, 0, 0, True)],
    [("MERGE", 0, 48, 1536, 2304, 768, 0, 0, True)],
    [("MERGE", 0, 48, 3072, 3840, 768, 0, 0, True)],
    [("STREAM", 0, 48, 0, 768, 768, 0, 0, True)],
    [("FEED", 0, 48, 0, 768, 768, 0, 0, True)],
    [("FEED", 0, 48, 1536, 2304, 768, 0, 0, True)],
    [("IN", 0, 48, 0, 384, 384, 0, 0, True), ("IN", 48, 48, 0, 384, 384, 0, 384, True)],
    [("IN", 96, 48, 0, 384, 384, 0, 0, True), ("IN", 144, 48, 0, 384, 384, 0, 384, True)],
    [("ATT", 0, 48, 0, 384, 384, 0, 0, True), ("ATT", 48, 48, 0, 384, 384, 0, 384, True)],
    [("ATT", 96, 48, 0, 384, 384, 0, 0, True), ("OUT", 0, 48, 0, 512, 384, 0, 384, True)],
    [("CELL", 0, 48, 0, 384, 384, 0, 0, True)],
    [("CELL", 48, 48, 0, 384, 384, 0, 0, True)],
    [("CELL", 96, 48, 0, 384, 384, 0, 0, True)],
    [
        ("OUT", 0, 48, 384, 896, 128, 0, 0, True),
        ("TABLE", 0, 16, 0, 512, 256, 0, 128, True),
        ("TABLE", 0, 16, 256, 768, 256, 16, 128, True),
        ("TABLE", 0, 16, 256, 768, 256, 32, 128, False),
    ],
)
WIDTHS = (768,) * 10 + (384,) * 4
SLOTS = 7
SUBS = 4
DENSE_PARTS = 10
AT_FIRST, AT_HOP, AT_NEXT, AT_LAST, AT_RESULT = SUBS, SUBS, SUBS + 4, SUBS + 5, SUBS + 6
MOVES = 2 * SUBS + 6


class Reduce:
    def __init__(self, spot, grads, landing, buffers, result, sems):
        self.spot, self.grads, self.landing, self.result = spot, grads, landing, result
        self.sums, self.other, self.one_in, self.next_in, self.final = buffers
        self.sent, self.got, self.load_sem, self.keep_sem, self.free = sems

    def lanes(self, p):
        return pl.ds(0, WIDTHS[p])

    def move(self, source, target, p, j, device):
        return remote(source, target, self.sent.at[p, j], self.got.at[p, j], device)

    def outside(self, ref, sub, core):
        _, row, rows, first, second, width, _, _, _ = sub
        return ref.at[..., pl.ds(row, rows), pl.ds((first, second)[core], width)]

    def inside(self, ref, sub):
        _, _, rows, _, _, width, row, lane, _ = sub
        return ref.at[..., pl.ds(row, rows), pl.ds(lane, width)]

    def given(self, core, p):
        return [
            self.move(
                self.outside(self.grads[sub[0]], sub, 1 - core), self.inside(self.landing.at[p], sub), p, i, self.spot.sibling
            )
            for i, sub in enumerate(PARTS[p])
        ]

    def loads(self, core, p):
        w = self.lanes(p)
        own = [
            pltpu.make_async_copy(
                self.outside(self.grads[sub[0]], sub, core), self.inside(self.sums.at[p % SLOTS], sub), self.load_sem.at[p % 2, i]
            )
            for i, sub in enumerate(PARTS[p])
        ]
        return own + [pltpu.make_async_copy(self.landing.at[p, ..., w], self.other.at[p % 2, ..., w], self.load_sem.at[p % 2, SUBS])]

    def first(self, core, p):
        s, slot, w = self.spot, p % SLOTS, self.lanes(p)
        if core == 0:
            return self.move(self.sums.at[slot, :, 1 - s.x, :, :, w], self.one_in.at[slot, ..., w], p, AT_FIRST, s.to_x)
        return self.move(self.sums.at[slot, :, :, 1 - s.y, :, w], self.one_in.at[slot, ..., w], p, AT_FIRST, s.to_y)

    def hop(self, core, p, k):
        s, slot, w = self.spot, p % SLOTS, self.lanes(p)
        z = (s.z + k) % 4
        if core == 0:
            return self.move(self.sums.at[slot, z, s.x, :, :, w], self.next_in.at[slot, pl.ds(2 * k - 2, 2), :, w], p, AT_HOP + k, s.hop(k))
        return self.move(self.sums.at[slot, z, s.x, s.y, :, w], self.next_in.at[slot, 3 + k, :, w], p, AT_HOP + k, s.hop(k))

    def next(self, core, p):
        s, slot, w = self.spot, p % SLOTS, self.lanes(p)
        if core == 0:
            return self.move(self.sums.at[slot, s.z, s.x, :, :, w], self.next_in.at[slot, pl.ds(6, 2), :, w], p, AT_NEXT, s.to_y)
        return self.move(self.sums.at[slot, :, 1 - s.x, s.y, :, w], self.next_in.at[slot, pl.ds(0, 4), :, w], p, AT_NEXT, s.to_x)

    def last(self, p, mine):
        s, slot, w = self.spot, p % SLOTS, self.lanes(p)
        part = self.final.at[slot, s.y if mine else 1 - s.y, :, w]
        return self.move(part, part, p, AT_LAST, s.to_y)

    def results(self, core, p):
        return [
            self.move(self.inside(self.final.at[p % SLOTS], sub), self.outside(self.result[sub[0]], sub, core), p, AT_RESULT + i, self.spot.sibling)
            for i, sub in enumerate(PARTS[p])
            if sub[-1]
        ]

    def kept(self, core, p):
        return [
            pltpu.make_async_copy(
                self.inside(self.final.at[p % SLOTS], sub), self.outside(self.result[sub[0]], sub, core), self.keep_sem.at[p, i]
            )
            for i, sub in enumerate(PARTS[p])
            if sub[-1]
        ]

    def give(self, core, p):
        for copy in self.given(core, p):
            copy.start()

    def fetch(self, core, p):
        for copy in self.given(core, p):
            copy.wait_recv()
        for copy in self.loads(core, p):
            copy.start()

    def stage_one(self, core, p):
        for copy in self.loads(core, p):
            copy.wait()
        slot, w = p % SLOTS, self.lanes(p)

        def add(i, carry):
            at = (i // 4, i // 2 % 2, i % 2)
            self.sums[slot, at[0], at[1], at[2], :, w] += self.other[p % 2, at[0], at[1], at[2], :, w]
            return carry

        lax.fori_loop(0, 16, add, 0)
        if p >= SLOTS:
            for i in range(5):
                pl.semaphore_wait(self.free.at[i], 1)
        self.first(core, p).start()

    def stage_two(self, core, p):
        s, slot, w = self.spot, p % SLOTS, self.lanes(p)
        self.first(core, p).wait_recv()

        def add(i, carry):
            if core == 0:
                self.sums[slot, i // 2, s.x, i % 2, :, w] += self.one_in[slot, i // 2, i % 2, :, w]
            else:
                self.sums[slot, i // 2, i % 2, s.y, :, w] += self.one_in[slot, i // 2, i % 2, :, w]
            return carry

        lax.fori_loop(0, 8, add, 0)
        if core == 0:
            for k in (1, 3, 2):
                self.hop(core, p, k).start()
        else:
            self.next(core, p).start()

    def stage_three(self, core, p):
        s, slot, w = self.spot, p % SLOTS, self.lanes(p)
        if core == 0:
            for k in (1, 3, 2):
                self.hop(core, p, k).wait_recv()

            def add(i, carry):
                total = self.sums[slot, s.z, s.x, i, :, w].astype(WIDE)
                for k in range(3):
                    total += self.next_in[slot, 2 * k + i, :, w].astype(WIDE)
                self.sums[slot, s.z, s.x, i, :, w] = total.astype(LOW)
                return carry

            lax.fori_loop(0, 2, add, 0)
            self.next(core, p).start()
        else:
            self.next(core, p).wait_recv()

            def add(i, carry):
                self.sums[slot, i, s.x, s.y, :, w] += self.next_in[slot, i, :, w]
                return carry

            lax.fori_loop(0, 4, add, 0)
            for k in (1, 3, 2):
                self.hop(core, p, k).start()

    def stage_four(self, core, p):
        s, slot, w = self.spot, p % SLOTS, self.lanes(p)
        if core == 0:
            self.next(core, p).wait_recv()

            def add(i, carry):
                self.final[slot, i, :, w] = self.sums[slot, s.z, s.x, i, :, w] + self.next_in[slot, 6 + i, :, w]
                return carry

            lax.fori_loop(0, 2, add, 0)
        else:
            for k in (1, 3, 2):
                self.hop(core, p, k).wait_recv()
            total = self.sums[slot, s.z, s.x, s.y, :, w].astype(WIDE)
            for k in range(3):
                total += self.next_in[slot, 4 + k, :, w].astype(WIDE)
            self.final[slot, s.y, :, w] = total.astype(LOW)
            self.last(p, True).start()

    def stage_five(self, core, p):
        if core == 1:
            self.last(p, False).wait_recv()
        for copy in self.results(core, p) + self.kept(core, p):
            copy.start()

    def release(self, core, p):
        self.first(core, p).wait_send()
        for k in (1, 2, 3):
            self.hop(core, p, k).wait_send()
        self.next(core, p).wait_send()
        if core == 1:
            self.last(p, True).wait_send()
        for copy in self.results(core, p):
            copy.wait_send()
        for copy in self.kept(core, p):
            copy.wait()
        if p + SLOTS < len(PARTS):
            s = self.spot
            for i, device in enumerate((s.to_x, s.to_y)):
                pl.semaphore_signal(self.free.at[i], 1, device_id=device, device_id_type=MESH)
            for k in (1, 2, 3):
                pl.semaphore_signal(self.free.at[1 + 4 - k], 1, device_id=s.hop(k), device_id_type=MESH)

    def finish(self, core, p):
        for copy in self.given(core, p):
            copy.wait_send()
        for copy in self.results(1 - core, p):
            copy.wait_recv()

    def program(self):
        count = len(PARTS)
        turns = [[("fetch", 0)]]
        for s in range(count + 7):
            turn = []
            for stage, p in (
                ("stage_one", s),
                ("release", s - 6),
                ("fetch", s + 1),
                ("stage_two", s - 2),
                ("stage_three", s - 3),
                ("stage_four", s - 4),
                ("stage_five", s - 5),
            ):
                if 0 <= p < count:
                    turn.append((stage, p))
            turns.append(turn)
        return turns

    def run(self, steps):
        for core in (0, 1):

            @pl.when(self.spot.core == core)
            def _():
                for stage, p in steps:
                    getattr(self, stage)(core, p)


def norm_backward(grad, i, gain, norms, spreads, small, gradients, gain_row, shift_row):
    unit, inverse = norms[i], spreads[i][:, :1]
    scaled = grad * small[gain : gain + 1]
    gradients[gain_row : gain_row + 1] = jnp.sum(grad * unit, axis=0, keepdims=True)
    gradients[shift_row : shift_row + 1] = jnp.sum(grad, axis=0, keepdims=True)
    centre = jnp.mean(scaled, axis=-1, keepdims=True)
    slope = jnp.mean(scaled * unit, axis=-1, keepdims=True)
    return inverse * (scaled - centre - unit * slope)


def attention_backward(projected, back, context_grad, valid, gradients):
    def pair(i, carry):
        def lanes(at):
            return pl.ds(pl.multiple_of(at * 768 + 128 * i, 128), 128)

        queries, keys, values = (projected[:, lanes(at)] for at in range(3))
        above = context_grad[:, lanes(0)]
        totals = [jnp.zeros((TOKENS, 128), WIDE) for _ in range(3)]
        for which in (0, 1):
            soft = soft_weights(queries, keys, which, valid)
            part = one_head(above, which)
            soft_grad = dot_second(part, values)
            score = soft * (soft_grad - jnp.sum(soft * soft_grad, axis=-1, keepdims=True))
            score = score.astype(LOW)
            totals[0] += dot_plain(score, one_head(keys, which))
            totals[1] += dot_first(score, one_head(queries, which))
            totals[2] += dot_first(soft.astype(LOW), part)
        totals[0] *= 0.125
        totals[1] *= 0.125
        for at in range(3):
            back[:, lanes(at)] = totals[at].astype(LOW)
        gradients[0:1, lanes(0)] = jnp.sum(totals[0], axis=0, keepdims=True)
        gradients[1:2, lanes(0)] = jnp.sum(totals[2], axis=0, keepdims=True)
        return carry

    lax.fori_loop(0, 6, pair, 0)


class Outbox:
    def __init__(self, thin, thick, sems):
        self.thin, self.thick, self.sems = thin, thick, sems
        self.count = 0
        self.flying = {}

    def settle(self, key):
        self.flying.pop(key).wait()

    def settle_all(self):
        for key in list(self.flying):
            self.settle(key)

    def send(self, key, source, target):
        copy = pltpu.make_async_copy(source, target, self.sems.at[key])
        copy.start()
        self.flying[key] = copy

    def room(self):
        key = self.count % THIN
        self.count += 1
        if key in self.flying:
            self.settle(key)
        return key

    def square(self, left, right, target):
        key = self.room()
        for half in (0, 1):
            rows = dot_first(left[:, 384 * half : 384 * half + 384], right).astype(LOW)
            self.thin[key, pl.ds(2 * half, 2)] = rows.reshape(2, 2, 2, 48, 768)
        self.send(key, self.thin.at[key], target)

    def block(self, left, right, target, shape):
        if THIN in self.flying:
            self.settle(THIN)
        rows = shape[0] * shape[1] * shape[2] * shape[3]
        parts = [
            dot_first(left[:, at : at + 384], right).astype(LOW) for at in range(0, rows, 384)
        ]
        self.thick[0 : shape[0], :, :, 0 : shape[3]] = jnp.concatenate(parts, axis=0).reshape(shape)
        self.send(THIN, self.thick.at[0 : shape[0], :, :, 0 : shape[3]], target)


THIN = 2
DENSE_KINDS = tuple(kind for kind in KINDS if kind not in ("CELL", "TABLE"))
SAVED = ("joined", "pooled", "norms", "spreads", "small")


def backward_kernel(per_place, *refs):
    weights = dict(zip(DENSE_KINDS, refs[:6]))
    record_in, cell_in, codes, length_row, hidden, cotangent, valid_keys = refs[6:13]
    saved = dict(zip(SAVED, refs[13:18]))
    early_in = refs[18:22]
    outs = refs[22:]
    result = dict(zip(KINDS, outs[:8]))
    hidden_grad, landing = outs[8:10]
    grads = dict(zip(KINDS, outs[10:18]))
    scratch = outs[18:]
    record, state_grad, pool_grad, total, gradients, grad, inner, back, thin, thick = scratch[:10]
    table_part, columns, shuffle = scratch[10:13]
    buffers = scratch[13:18]
    record_sem, weight_sem, outbox_sem, column_sem = scratch[18:22]
    sems = scratch[22:27]
    late_sem, cell, lengths = scratch[27:30]
    saved.update(zip(EARLY, scratch[30:34]))
    spread_lengths(length_row, lengths)
    spot = Spot(per_place)
    norms, spreads, small = saved["norms"], saved["spreads"], saved["small"]

    def weight_copies(kind):
        source = weights[kind]
        if kind == "MERGE":
            pairs = [(source, record.at[pl.ds(14, 6)])]
        elif kind == "FEED":
            pairs = [(source, record.at[pl.ds(8, 6), :, pl.ds(0, 3072)])]
        elif kind == "STREAM":
            pairs = [(source, record.at[pl.ds(8, 6), :, pl.ds(3072, 1536)])]
        elif kind == "OUT":
            pairs = [(source.at[j, :, pl.ds(0, 768)], record.at[0, :, pl.ds(768 * j, 768)]) for j in range(6)]
        else:
            first, count = (4, 4) if kind == "IN" else (1, 3)
            pairs = [(source.at[:, j], record.at[pl.ds(first, count), :, pl.ds(768 * j, 768)]) for j in range(6)]
        at = DENSE_KINDS.index(kind)
        return [pltpu.make_async_copy(a, b, weight_sem.at[at, j]) for j, (a, b) in enumerate(pairs)]

    late = {name: (source, saved[name]) for name, source in zip(EARLY, early_in)}
    late["cell"] = (cell_in, cell)
    late = {name: pltpu.make_async_copy(*pair, late_sem.at[i]) for i, (name, pair) in enumerate(late.items())}

    def need(kind):
        for copy in weight_copies(kind):
            copy.wait()

    def rows_of(slot):
        return jnp.concatenate([record[slot, :, pl.ds(768 * j, 768)] for j in range(6)], axis=0)

    def record_copy(t):
        return pltpu.make_async_copy(record_in.at[t], record.at[t], record_sem.at[t])

    def fill(first, count):
        for t in range(first, first + count):
            record_copy(t).start()

    for kind in ("MERGE", "STREAM", "FEED", "IN", "OUT", "ATT"):
        for copy in weight_copies(kind):
            copy.start()
    for name in ("active", "slope", "context", "projected", "cell"):
        late[name].start()
    spot.greet()
    reduce = Reduce(spot, grads, landing, buffers, result, sems)
    outbox = Outbox(thin, thick, outbox_sem)
    steps = [step for turn in reduce.program() for step in turn]
    given = set()

    def give(*parts):
        outbox.settle_all()
        reduce.run([("give", p) for p in parts])
        given.update(parts)

    def take(count):
        taken = []
        while steps and len(taken) < count and not (steps[0][0] == "fetch" and steps[0][1] not in given):
            taken.append(steps.pop(0))
        return taken

    def go_on(count):
        reduce.run(take(count))

    gradients[...] = jnp.zeros_like(gradients)
    merged = norm_backward(cotangent[...].astype(WIDE), 2, 12, norms, spreads, small, gradients, 12, 9)
    gradients[8:9] = jnp.sum(merged, axis=0, keepdims=True)
    grad[...] = merged
    merged_low = merged.astype(LOW)
    joined = saved["joined"]
    for k in range(3):
        taps = window(joined, k)
        for half in (0, 1):
            lanes = pl.ds(1536 * k + 768 * half, 768)
            outbox.square(merged_low, taps[:, 768 * half : 768 * half + 768], grads["MERGE"].at[..., lanes])
        give(k)
        if k > 0:
            go_on(PACE[0])
    need("MERGE")
    parts = [
        dot_plain(merged_low, record[pl.ds(14, 6), :, pl.ds(1536 * k, 1536)].reshape(768, 1536)) for k in range(3)
    ]
    joined_grad = parts[1] + shifted(parts[0], False) + shifted(parts[2], True)
    fill(14, 6)
    go_on(PACE[1])
    gradients[6:7] = jnp.sum(joined_grad[:, :768], axis=0, keepdims=True)
    gradients[7:8] = jnp.sum(joined_grad[:, 768:], axis=0, keepdims=True)
    token_low, char_low = joined_grad[:, :768].astype(LOW), joined_grad[:, 768:].astype(LOW)
    second_low = (norms[1] * small[11:12] + small[5:6]).astype(LOW)
    outbox.square(token_low, second_low, grads["STREAM"].at[..., pl.ds(0, 768)])
    outbox.square(char_low, saved["pooled"][...], grads["STREAM"].at[..., pl.ds(768, 768)])
    give(3)
    need("STREAM")
    stream = record[pl.ds(8, 6), :, pl.ds(3072, 1536)].reshape(768, 1536)
    pool_grad[...] = dot_plain(char_low, stream[:, 768:]) / lengths[:, :1].astype(WIDE)
    second_grad = grad[...] + dot_plain(token_low, stream[:, :768])
    two = norm_backward(second_grad, 1, 11, norms, spreads, small, gradients, 11, 5)
    gradients[4:5] = jnp.sum(two, axis=0, keepdims=True)
    grad[...] = two
    two_low = two.astype(LOW)
    late["active"].wait()
    for c in range(4):
        outbox.square(two_low, saved["active"][:, 768 * c : 768 * c + 768], grads["FEED"].at[..., pl.ds(768 * c, 768)])
        if c % 2 == 1:
            give(4 + c // 2)
            go_on(PACE[2])
    need("FEED")
    late["slope"].wait()
    first_low = (norms[0] * small[10:11] + small[3:4]).astype(LOW)
    shuffle[...] = jnp.zeros_like(shuffle)
    for c in range(4):
        lanes = pl.ds(768 * c, 768)
        part = dot_plain(two_low, record[pl.ds(8, 6), :, lanes].reshape(768, 768))
        part = part * saved["slope"][:, lanes].astype(WIDE)
        inner[:, lanes] = part.astype(LOW)
        sums = jnp.sum(part, axis=0, keepdims=True)
        for half in (0, 1):
            at = 768 * c + 384 * half
            done = 0
            while done < 384:
                row, lane = (at + done) // 512, (at + done) % 512
                size = min(512 - lane, 384 - done)
                start = 384 * half + done
                shuffle[row : row + 1, lane : lane + size] = sums[:, start : start + size]
                done += size
        outbox.block(inner[:, lanes], first_low, grads["IN"].at[pl.ds(c, 1)], (1, 2, 2, 192, 768))
        go_on(PACE[3])
    fill(8, 6)
    give(6, 7)
    need("IN")
    first_grad = grad[...]
    for c in range(4):
        first_grad += dot_plain(inner[:, 768 * c : 768 * c + 768], rows_of(4 + c))
    one = norm_backward(first_grad, 0, 10, norms, spreads, small, gradients, 10, 3)
    fill(4, 4)
    go_on(PACE[4])
    gradients[2:3] = jnp.sum(one, axis=0, keepdims=True)
    grad[...] = one
    one_low = one.astype(LOW)
    need("OUT")
    context_grad = dot_plain(one_low, rows_of(0)).astype(LOW)
    inner[:, pl.ds(0, 768)] = context_grad
    late["context"].wait()
    late["projected"].wait()
    attention_backward(saved["projected"], back, inner, key_mask(valid_keys[0]), gradients)
    go_on(PACE[5])
    outbox.square(one_low, saved["context"][...], grads["OUT"].at[..., pl.ds(0, 768)])
    flat = dot_second(shuffle[...].astype(LOW), spread_matrix())
    for c in range(6):
        for j in range(4):
            gradients[13 + j : 14 + j, 128 * c : 128 * c + 128] = flat[c : c + 1, 128 * j : 128 * j + 128]
    columns[:, :, :, :, pl.ds(0, 128)] = jnp.transpose(gradients[...]).astype(LOW).reshape(4, 2, 2, 48, 128)
    columns[:, :, :, :, pl.ds(128, 128)] = jnp.zeros((4, 2, 2, 48, 128), LOW)
    column_copy = pltpu.make_async_copy(columns, grads["OUT"].at[..., pl.ds(768, 256)], column_sem.at[0])
    column_copy.start()
    for i in range(2):
        outbox.block(back[:, pl.ds(1152 * i, 1152)], hidden[...], grads["ATT"].at[pl.ds(2 * i, 2)], (2, 2, 2, 144, 768))
        go_on(PACE[6])
    column_copy.wait()
    give(8, 9)
    need("ATT")
    hidden_back = grad[...]
    for i in range(3):
        hidden_back += dot_plain(back[:, pl.ds(768 * i, 768)], rows_of(1 + i))
    hidden_grad[...] = hidden_back.astype(LOW)
    fill(0, 4)

    late["cell"].wait()
    state_grad[...] = jnp.zeros_like(state_grad)
    total[...] = jnp.zeros_like(total)
    shares = [take(PACE[7]) for _ in range(CHARS)]

    def retreat(i, carry):
        t = CHARS - 1 - i
        record_copy(t).wait()
        gru_backward_step(t, cell, record, state_grad, pool_grad, lengths)
        for k in range(CHARS):
            if shares[k]:

                @pl.when(i == k)
                def _():
                    reduce.run(shares[k])

        return carry

    lax.fori_loop(0, CHARS, retreat, 0)
    for way in (0, 1):
        outbox.settle_all()
        cell_gradient(way, record, thick)
        outbox.send(THIN, thick.at[:, :, :, 0:144], grads["CELL"].at[pl.ds(2 * way, 2)])
        if way == 1:
            give(10, 11, 12)
        go_on(PACE[8])

    def look_up(i, carry):
        table_gradient(i, cell, record, codes, total)
        return carry

    lax.fori_loop(0, CHARS // 4, look_up, 0)
    go_on(PACE[9])
    lax.fori_loop(CHARS // 4, CHARS // 2, look_up, 0)
    table_part[...] = jnp.transpose(total[...]).astype(LOW).reshape((4, 2, 2) + BLOCKS["TABLE"])
    outbox.send(0, table_part, grads["TABLE"])
    give(13)
    reduce.run(steps)
    reduce.run([("finish", p) for p in range(len(PARTS))])


PACE = (1, 1, 1, 1, 2, 2, 2, 1, 7, 7)


def reduce_and_return(whole, saved, record, codes, lengths, hidden, cotangent, valid_keys, per_place):
    in_vmem = pl.BlockSpec(memory_space=pltpu.VMEM)
    anywhere = pl.BlockSpec(memory_space=pl.ANY)
    count = len(PARTS)
    shapes = [jax.ShapeDtypeStruct((2,) + BLOCKS[kind], LOW) for kind in KINDS]
    shapes += [
        jax.ShapeDtypeStruct((TOKENS, 768), LOW),
        jax.ShapeDtypeStruct((count, 4, 2, 2, ROWS, LANES), LOW),
    ]
    shapes += [jax.ShapeDtypeStruct((4, 2, 2) + BLOCKS[kind], LOW) for kind in KINDS]
    views = {
        "ATT": (3, 6, 128, 768),
        "OUT": (6, 128, 1024),
        "IN": (4, 6, 128, 768),
        "FEED": (6, 128, 3072),
        "STREAM": (6, 128, 1536),
        "MERGE": (6, 128, 4608),
    }
    results = pl.pallas_call(
        partial(backward_kernel, per_place),
        out_shape=shapes,
        in_specs=[anywhere] * 8
        + [in_vmem] * 4
        + [pl.BlockSpec(memory_space=pltpu.SMEM)]
        + [in_vmem] * len(SAVED)
        + [anywhere] * len(EARLY),
        out_specs=[anywhere] * 8 + [in_vmem] + [anywhere] * 9,
        scratch_shapes=[
            pltpu.VMEM((CHARS, TOKENS, 2 * RECORD), LOW),
            pltpu.VMEM((TOKENS, 2 * HID), WIDE),
            pltpu.VMEM((TOKENS, 2 * HID), WIDE),
            pltpu.VMEM((1024, EMB), WIDE),
            pltpu.VMEM((128, 768), WIDE),
            pltpu.VMEM((TOKENS, 768), WIDE),
            pltpu.VMEM((TOKENS, 3072), LOW),
            pltpu.VMEM((TOKENS, 2304), LOW),
            pltpu.VMEM((THIN, 4, 2, 2, 48, 768), LOW),
            pltpu.VMEM((2, 2, 2, 192, 768), LOW),
            pltpu.VMEM((4, 2, 2) + BLOCKS["TABLE"], LOW),
            pltpu.VMEM((4, 2, 2, 48, 256), LOW),
            pltpu.VMEM((8, 512), WIDE),
            pltpu.VMEM((SLOTS, 4, 2, 2, ROWS, LANES), LOW),
            pltpu.VMEM((2, 4, 2, 2, ROWS, LANES), LOW),
            pltpu.VMEM((SLOTS, 4, 2, ROWS, LANES), LOW),
            pltpu.VMEM((SLOTS, 8, ROWS, LANES), LOW),
            pltpu.VMEM((SLOTS, 2, ROWS, LANES), LOW),
            pltpu.SemaphoreType.DMA((CHARS,)),
            pltpu.SemaphoreType.DMA((6, 6)),
            pltpu.SemaphoreType.DMA((THIN + 1,)),
            pltpu.SemaphoreType.DMA((1,)),
            pltpu.SemaphoreType.DMA((count, MOVES)),
            pltpu.SemaphoreType.DMA((count, MOVES)),
            pltpu.SemaphoreType.DMA((2, SUBS + 1)),
            pltpu.SemaphoreType.DMA((count, SUBS)),
            pltpu.SemaphoreType.REGULAR((5,)),
            pltpu.SemaphoreType.DMA((len(EARLY) + 1,)),
            pltpu.VMEM((4, 2, 2) + BLOCKS["CELL"], LOW),
            pltpu.VMEM((TOKENS, TOKENS), jnp.int32),
        ]
        + [pltpu.VMEM(shape, kind) for shape, kind in EARLY.values()],
        compiler_params=pltpu.CompilerParams(collective_id=1, has_side_effects=True, vmem_limit_bytes=63 << 20),
    )(
        *[whole[kind].reshape(views[kind]) for kind in DENSE_KINDS],
        record,
        whole["CELL"],
        codes,
        lengths,
        hidden,
        cotangent,
        valid_keys,
        *[saved[name] for name in SAVED],
        *[saved[name] for name in EARLY],
    )
    return dict(zip(KINDS, results[:8])), results[8]


def unpack_kernel(*refs):
    count = len(KINDS)
    sources, passed = refs[:count], refs[count : count + 2]
    targets = refs[count + 2 : count + 17]
    scratch = refs[count + 17 :]
    held, through = dict(zip(KINDS, scratch[:count])), scratch[count : count + 2]
    made, in_sem, out_sem = scratch[count + 2 : count + 15], scratch[count + 15], scratch[count + 16]
    loads = [
        pltpu.make_async_copy(source, target, in_sem.at[i])
        for i, (source, target) in enumerate(zip((*sources, *passed), (*held.values(), *through)))
    ]
    for copy in loads:
        copy.start()
    loads = dict(zip((*KINDS, 0, 1), loads))
    stores = []

    def store(source, i):
        copy = pltpu.make_async_copy(source, targets[i], out_sem.at[i])
        copy.start()
        stores.append(copy)

    def keep(i, value):
        made[i][...] = value
        store(made[i], 2 + i)

    def rows(kind, first, width):
        if kind in loads:
            loads.pop(kind).wait()
        value = held[kind][:, :, pl.ds(first, width)]
        return value.reshape(-1, width).astype(WIDE)

    for i in range(2):
        loads.pop(i).wait()
        store(through[i], i)
    for k in range(3):
        made[10][k] = rows("MERGE", 1536 * k, 1536)
    store(made[10], 12)
    keep(4, rows("FEED", 0, 3072))
    keep(2, jnp.transpose(rows("IN", 0, 768)))
    for k in range(2):
        made[9][k] = rows("STREAM", 768 * k, 768)
    store(made[9], 11)
    keep(0, rows("ATT", 0, 768))
    keep(1, rows("OUT", 0, 768))
    keep(5, rows("TABLE", 0, 1024)[:, :1000])
    keep(6, rows("CELL", 0, EMB))
    keep(7, rows("CELL", EMB, HID))
    keep(8, jnp.transpose(rows("CELL", EMB + HID, 128))[:2])
    small = jnp.transpose(rows("OUT", 768, 128))
    keep(11, small[10:13])
    keep(12, small[:10])
    low = small[8:24].astype(LOW)
    size = low.shape[1]
    row = lax.broadcasted_iota(jnp.int32, (size, 4 * size), 0)
    lane = lax.broadcasted_iota(jnp.int32, (size, 4 * size), 1)
    flat = jnp.zeros((1, 4 * size), WIDE)
    for j in range(4):
        flat += dot_plain(low, (4 * row + j == lane).astype(LOW))[5 + j : 6 + j]
    keep(3, flat)
    for copy in stores:
        copy.wait()


def unpack(final, output, hidden_grad):
    shapes = [
        (288, 768), (96, 768), (768, 384), (1, 384), (96, 3072), (32, 1000), (288, EMB), (288, HID), (2, 288),
        (2, 96, 768), (3, 96, 1536), (3, 96), (10, 96),
    ]
    anywhere = pl.BlockSpec(memory_space=pl.ANY)
    count = len(KINDS)
    results = pl.pallas_call(
        unpack_kernel,
        out_shape=[jax.ShapeDtypeStruct((TOKENS, 768), LOW)] * 2 + [jax.ShapeDtypeStruct(shape, WIDE) for shape in shapes],
        in_specs=[anywhere] * (count + 2),
        out_specs=[anywhere] * (2 + len(shapes)),
        scratch_shapes=[pltpu.VMEM((2,) + BLOCKS[kind], LOW) for kind in KINDS]
        + [pltpu.VMEM((TOKENS, 768), LOW)] * 2
        + [pltpu.VMEM(shape, WIDE) for shape in shapes]
        + [pltpu.SemaphoreType.DMA((count + 2,)), pltpu.SemaphoreType.DMA((2 + len(shapes),))],
        compiler_params=pltpu.CompilerParams(vmem_limit_bytes=60 << 20),
    )(*[final[kind] for kind in KINDS], output, hidden_grad)
    att, out, feed_in, feed_bias, feed, table, cell_in, cell_back, cell_bias, stream, merge, gains, biases = results[2:]
    return (
        results[0],
        results[1],
        att.T,
        out.T,
        feed_in,
        feed_bias.reshape(-1),
        feed.T,
        table.T,
        cell_in.T,
        cell_back.T,
        cell_bias,
        jnp.swapaxes(stream, 1, 2),
        jnp.swapaxes(merge, 1, 2),
        gains,
        biases,
    )


def shards(hidden, char_codes, word_length, sequence_length, cotangent, *parameters):
    wide = lax.axis_size("wide")
    per_place = wide // 2
    starts = pack(parameters, per_place)
    codes = jnp.transpose(char_codes)
    lengths = word_length[None, :]
    whole, record, saved = gather_and_read(starts, codes, lengths, hidden, sequence_length, per_place)
    final, hidden_grad = reduce_and_return(
        whole, saved, record, codes, lengths, hidden, cotangent, sequence_length, per_place
    )
    if per_place > 2:
        groups = [[y * per_place + 2 * i + core for i in range(per_place // 2)] for y in (0, 1) for core in (0, 1)]
        final = {
            kind: lax.psum(part.astype(WIDE), "wide", axis_index_groups=groups).astype(LOW)
            for kind, part in final.items()
        }
    return unpack(final, saved["output"], hidden_grad)


def solution(mesh):
    rows = P(("grp", "wide"), None)
    flat = P(("grp", "wide"))
    last = P(None, ("grp", "wide"))
    deep = P(None, None, ("grp", "wide"))
    in_specs = (rows, rows, flat, flat, rows, last, last, last, flat, last, last, last, last, last, deep, deep, last, last)
    out_specs = (rows, rows) + (P(None, "grp"),) * 3 + (P("grp"),) + (P(None, "grp"),) * 5 + (P(None, None, "grp"),) * 2 + (P(None, "grp"),) * 2
    return jax.shard_map(shards, mesh=mesh, in_specs=in_specs, out_specs=out_specs, check_vma=False)
```
